32 devices in a mesh: dp: 2 (over y), seq: 4 (over z), ctx: 4 (over x, core).
Axes of the slice: x: 2, y: 2, z: 4, core: 2. Of those that a mesh axis runs over, the one named last changes fastest.
Arguments:
- tokens: bfloat16 [8192, 2048], P(('dp', 'seq', 'ctx')), may hold values from -6 to 6
- positions: int32 [8192], P(('dp', 'seq', 'ctx')), may hold values from 0 to 7920, as said below
- cotangent: bfloat16 [8192, 2048], P(('dp', 'seq', 'ctx')), may hold values from -6 to 6
- query_weight: bfloat16 [2048, 2048], P(('dp', 'ctx')), may hold values from -0.125 to 0.125
- key_weight: bfloat16 [2048, 256], P(('dp', 'ctx')), may hold values from -0.125 to 0.125
- value_weight: bfloat16 [2048, 256], P(('dp', 'ctx')), may hold values from -0.125 to 0.125
- output_weight: bfloat16 [2048, 2048], P(('dp', 'ctx')), may hold values from -4 to 4
- gate_weight: bfloat16 [2048, 5632], P(('dp', 'ctx')), may hold values from -0.125 to 0.125
- up_weight: bfloat16 [2048, 5632], P(('dp', 'ctx')), may hold values from -0.125 to 0.125
- down_weight: bfloat16 [5632, 2048], P(('dp', 'ctx')), may hold values from -0.078125 to 0.078125
- first_gain: bfloat16 [2048], P(('dp', 'ctx')), may hold values from 0.25 to 1.75
- second_gain: bfloat16 [2048], P(('dp', 'ctx')), may hold values from 0.25 to 1.75
Outputs:
- layer_output: bfloat16 [8192, 2048], P(('dp', 'seq', 'ctx'))
- input_gradient: float32 [8192, 2048], P(('dp', 'seq', 'ctx'))
- query_gradient: float32 [2048, 2048], P(('dp', 'ctx'))
- key_gradient: float32 [2048, 256], P(('dp', 'ctx'))
- value_gradient: float32 [2048, 256], P(('dp', 'ctx'))
- output_gradient: float32 [2048, 2048], P(('dp', 'ctx'))
- gate_gradient: float32 [2048, 5632], P(('dp', 'ctx'))
- up_gradient: float32 [2048, 5632], P(('dp', 'ctx'))
- down_gradient: float32 [5632, 2048], P(('dp', 'ctx'))
- first_gradient: float32 [2048], P(('dp', 'ctx'))
- second_gradient: float32 [2048], P(('dp', 'ctx'))
The draws below stay inside these ranges and needn't reach their ends.
Inputs may be any that keep to these rules, and one draw needn't show every extreme that they name: Within a sequence, positions rise by one inside each 256-token block; each block starts at or after the end of the block before it, at most 255 positions later, and every sequence starts at position 0.
All inputs are finite; a program needn't handle non-finite values.
Results may differ from the reference program's by a relative error of at most 0.023.
Values may be sent and summed in bfloat16 or wider, within the bound.
No kernel may reach another device: no remote copies, remote signals or barrier semaphores. Data moves between devices by JAX's collectives and lax.ppermute only.
A program may use at most 256 MiB of HBM per device.

```python
import jax
import jax.numpy as jnp
from jax import lax

D = 2048
HEADS = 32
KV_HEADS = 4
HEAD_DIM = 64
FF = 5632
BLOCK = 256
LENGTH = 4096
SEQS = 2
TOKENS = 8192


def draw_positions(key, part):
    block_count = LENGTH // BLOCK
    block_gaps = jax.random.randint(key, (SEQS, block_count), 0, BLOCK)
    chosen = jax.random.randint(jax.random.fold_in(key, 7), (), 0, SEQS)
    row = jnp.arange(SEQS)
    block_gaps = jnp.where(row[:, None] == chosen, BLOCK - 1, block_gaps)
    column = jnp.arange(block_count)
    block_gaps = jnp.where(column[None, :] == 0, 0, block_gaps)
    starts = jnp.cumsum(block_gaps, axis=1) + column[None, :] * BLOCK
    places = starts[:, :, None] + jnp.arange(BLOCK)[None, None, :]
    return places.reshape(TOKENS).astype(jnp.int32)


def steps_of(own_key, shape, pieces, low, high):
    loudness, own = 1.0, jax.random.fold_in(own_key, 6)
    for axis_at, blocks in pieces:
        heights = jnp.exp(jax.random.uniform(jax.random.fold_in(own, axis_at), (blocks,), jnp.float32, low / len(pieces), high / len(pieces)))
        loudness = loudness * jnp.repeat(heights, shape[axis_at] // blocks).reshape([-1 if axis == axis_at else 1 for axis in range(len(shape))])
    return loudness


def scatter_about(rng, shape, width, most, cuts=(), kind=jnp.bfloat16):
    entries = width * jax.random.normal(rng, shape, jnp.float32)
    if cuts:
        entries = entries * steps_of(rng, shape, cuts, -0.22, 0.18)
    return jnp.clip(entries, -most, most).astype(kind)


def setup_inputs(seed: int = 0) -> dict:
    arg_keys = jax.random.split(jax.random.key(seed), 13)
    return {
        "tokens": scatter_about(arg_keys[0], (TOKENS, D), 1.0, 6.0, ((0, 32),)),
        "positions": draw_positions(jax.random.fold_in(arg_keys[12], 71), 0),
        "cotangent": scatter_about(arg_keys[2], (TOKENS, D), 1.0, 6.0, ((0, 32),)),
        "query_weight": scatter_about(arg_keys[3], (D, HEADS * HEAD_DIM), D ** -0.5, 0.125, ((0, 8),)),
        "key_weight": scatter_about(arg_keys[4], (D, KV_HEADS * HEAD_DIM), D ** -0.5, 0.125, ((0, 8),)),
        "value_weight": scatter_about(arg_keys[5], (D, KV_HEADS * HEAD_DIM), D ** -0.5, 0.125, ((0, 8),)),
        "output_weight": scatter_about(arg_keys[6], (HEADS * HEAD_DIM, D), (max(D // 1024, 1)) ** -0.5, 4.0, ((0, 8),)),
        "gate_weight": scatter_about(arg_keys[7], (D, FF), D ** -0.5, 0.125, ((0, 8),)),
        "up_weight": scatter_about(arg_keys[8], (D, FF), D ** -0.5, 0.125, ((0, 8),)),
        "down_weight": scatter_about(arg_keys[9], (FF, D), FF ** -0.5, 0.078125, ((0, 8),)),
        "first_gain": jnp.clip(1.0 + 0.15 * jax.random.normal(arg_keys[10], (D,), jnp.float32), 0.25, 1.75).astype(jnp.bfloat16),
        "second_gain": jnp.clip(1.0 + 0.15 * jax.random.normal(arg_keys[11], (D,), jnp.float32), 0.25, 1.75).astype(jnp.bfloat16),
    }


epsilon = 1e-05
rotary_base = 10000.0
masked_score = -1e+30

@jax.custom_vjp
def low(v):
    return lax.optimization_barrier(v.astype(jnp.bfloat16)).astype(jnp.float32)

@jax.custom_vjp
def low_back(v):
    return v

def low_keep(v):
    return (low(v), None)

def low_pass(kept, grad):
    return (grad,)

def back_keep(v):
    return (v, None)

def back_low(kept, grad):
    return (low(grad),)
low.defvjp(low_keep, low_pass)
low_back.defvjp(back_keep, back_low)

def product(left, right):
    return jnp.dot(left, right, precision=lax.Precision.HIGHEST, preferred_element_type=jnp.float32)

def rotate(features, positions):
    half_width = HEAD_DIM // 2
    exponent = jnp.arange(half_width).astype(jnp.float32) * (2.0 / HEAD_DIM)
    frequency = rotary_base ** (-exponent)
    angles = positions.astype(jnp.float32)[:, None] * frequency[None, :]
    cosine = jnp.cos(angles)[:, None, :]
    sine = jnp.sin(angles)[:, None, :]
    shaped = features.reshape(features.shape[0], -1, HEAD_DIM)
    first_half = shaped[:, :, :half_width]
    second_half = shaped[:, :, half_width:]
    turned = jnp.concatenate([first_half * cosine - second_half * sine, second_half * cosine + first_half * sine], axis=2)
    return turned.reshape(features.shape)

def normalize(features):
    inverse_rms = lax.rsqrt(lax.optimization_barrier(jnp.mean(features * features, axis=-1, keepdims=True)) + epsilon)
    return features * inverse_rms

def attend(queries, keys, values):
    group_size = HEADS // KV_HEADS
    query_heads = queries.reshape(LENGTH, HEADS, HEAD_DIM).transpose(1, 0, 2)
    key_heads = jnp.repeat(keys.reshape(LENGTH, KV_HEADS, HEAD_DIM).transpose(1, 0, 2), group_size, axis=0)
    value_heads = jnp.repeat(values.reshape(LENGTH, KV_HEADS, HEAD_DIM).transpose(1, 0, 2), group_size, axis=0)
    block_index = jnp.arange(LENGTH) // BLOCK
    allowed = block_index[None, :] <= block_index[:, None]

    def one_head(operands):
        query_head, key_head, value_head = operands
        scores = low_back(product(query_head, key_head.T) * HEAD_DIM ** (-0.5))
        scores = jnp.where(allowed, scores, masked_score)
        weights = low(jax.nn.softmax(scores, axis=-1))
        return product(weights, value_head)
    outputs = lax.map(jax.checkpoint(one_head), (query_heads, key_heads, value_heads))
    return outputs.transpose(1, 0, 2).reshape(LENGTH, HEADS * HEAD_DIM)

def forward(params, inputs, positions):
    query_weight, key_weight, value_weight, output_weight, gate_weight, up_weight, down_weight, first_gain, second_gain = params
    first_input = low(normalize(inputs) * first_gain)
    query_linear = low_back(product(first_input, query_weight))
    key_linear = low_back(product(first_input, key_weight))
    queries = low_back(low(rotate(query_linear, positions)))
    keys = low_back(low(rotate(key_linear, positions)))
    values = low_back(low(product(first_input, value_weight)))
    attended = low_back(low(attend(queries, keys, values)))
    middle = inputs + low_back(product(attended, output_weight))
    second_input = low(normalize(middle) * second_gain)
    gate_values = low_back(product(second_input, gate_weight))
    up_values = low_back(product(second_input, up_weight))
    hidden = low(jax.nn.silu(gate_values) * up_values)
    return middle + low_back(product(hidden, down_weight))

def reference(tokens, positions, cotangent, query_weight, key_weight, value_weight, output_weight, gate_weight, up_weight, down_weight, first_gain, second_gain):
    params = tuple((weight.astype(jnp.float32) for weight in (query_weight, key_weight, value_weight, output_weight, gate_weight, up_weight, down_weight, first_gain, second_gain)))
    inputs = tokens.astype(jnp.float32).reshape(SEQS, LENGTH, D)
    places = positions.reshape(SEQS, LENGTH)
    slopes = cotangent.astype(jnp.float32).reshape(SEQS, LENGTH, D)

    def one_sequence(totals, operands):
        sequence_input, sequence_places, sequence_slope = operands

        def layer(weights, features):
            return forward(weights, features, sequence_places)
        result, pullback = jax.vjp(layer, params, sequence_input)
        weight_slopes, input_slope = pullback(sequence_slope)
        totals = jax.tree.map(lambda running, extra: running + extra, totals, weight_slopes)
        return (totals, (result, input_slope))
    zeros = jax.tree.map(jnp.zeros_like, params)
    totals, outputs = lax.scan(one_sequence, zeros, (inputs, places, slopes))
    results, input_slopes = outputs
    return (results.reshape(TOKENS, D).astype(jnp.bfloat16), input_slopes.reshape(TOKENS, D), totals[0], totals[1], totals[2], totals[3], totals[4], totals[5], totals[6], totals[7], totals[8])
```

```python
from functools import partial

import jax
import jax.numpy as jnp
from jax import lax
from jax.experimental import pallas as pl
from jax.experimental.pallas import tpu as pltpu
from jax.sharding import PartitionSpec as P

HEADS = 32
KV_HEADS = 4
HEAD_DIM = 64
BLOCK = 256

epsilon = 1e-05
rotary_base = 10000.0
log2_e = 1.4426950408889634
ln_2 = 0.6931471805599453
bf16, f32 = jnp.bfloat16, jnp.float32
PLANE = ("dp", "ctx")
GROUP = ("seq", "ctx")
NT = (((1,), (1,)), ((), ()))
NN = (((1,), (0,)), ((), ()))
TN = (((0,), (0,)), ((), ()))


def dot(left, right, dims=NN):
    return lax.dot_general(left, right, dims, preferred_element_type=f32)


def normalize(features):
    inverse_rms = lax.rsqrt(jnp.mean(features * features, axis=-1, keepdims=True) + epsilon)
    return (features * inverse_rms, inverse_rms)


def norm_backward(slopes, normed, inverse_rms):
    return inverse_rms * (slopes - normed * jnp.mean(slopes * normed, axis=-1, keepdims=True))


def angles_of(places):
    lane = jnp.arange(2 * HEAD_DIM)
    exponent = (lane % (HEAD_DIM // 2)).astype(f32) * (2.0 / HEAD_DIM)
    frequency = rotary_base ** (-exponent)
    angles = places[:, None] * frequency[None, :]
    sign = jnp.where(lane % HEAD_DIM < HEAD_DIM // 2, -1.0, 1.0)
    return jnp.cos(angles), jnp.sin(angles) * sign


def tie(*values):
    return lax.optimization_barrier(values)


def swap(values, mask, axes=PLANE):
    count = lax.axis_size(axes)
    return lax.ppermute(values, axes, [(i, i ^ mask) for i in range(count)])


def halves(count):
    return (slice(0, count // 2), slice(count // 2, count))


class ChipGather:
    def __init__(self, own):
        self.own = own

    def first(self):
        self.ends = {}
        r = 1
        while r < lax.axis_size(PLANE) // 2:
            self.ends[r] = swap(self.own, r << 1)
            r *= 2

    def second(self):
        top, bottom = halves(self.own.shape[0])
        parts = {r: (values[top], values[bottom]) for r, values in self.ends.items()}
        for r in range(1, lax.axis_size(PLANE) // 2):
            low, high = r & -r, 1 << (r.bit_length() - 1)
            if low != high:
                first = swap(parts[r ^ low][0], low << 1)
                parts[r] = (first, swap(parts[r ^ high][1], high << 1))
        self.rest = {r: both for r, both in parts.items() if r not in self.ends}

    def chunks(self):
        half = self.own.shape[0] // 2
        chunks = [(0, 0, self.own)]
        for r in range(1, lax.axis_size(PLANE) // 2):
            if r in self.ends:
                chunks.append((r, 0, self.ends[r]))
            else:
                chunks += [(r, 0, self.rest[r][0]), (r, half, self.rest[r][1])]
        return chunks

    def result(self):
        return jnp.concatenate([values for _, _, values in self.chunks()], axis=0)


def add(left, right):
    return (left.astype(f32) + right.astype(f32)).astype(bf16)


def to_chips(blocks):
    return [block if r == 0 else swap(block, r << 1) for r, block in enumerate(blocks)]


def add_all(values):
    total = values[0].astype(f32)
    for other in values[1:]:
        total = total + other.astype(f32)
    return total


def gather_plane(own):
    rows = own.shape[0]
    owner = lax.axis_index(PLANE)
    full = jnp.zeros((rows * lax.axis_size(PLANE), own.shape[1]), own.dtype)
    gather = ChipGather(own)
    gather.first()
    gather.second()
    for r, first, chunk in gather.chunks():
        other = swap(chunk, 1)
        full = lax.dynamic_update_slice_in_dim(full, chunk, (owner ^ (2 * r)) * rows + first, 0)
        full = lax.dynamic_update_slice_in_dim(full, other, (owner ^ (2 * r + 1)) * rows + first, 0)
    return full


class LaneSum:
    def __init__(self, values):
        owners = lax.axis_size(PLANE)
        owner = lax.axis_index(PLANE)
        rows = values.shape[0] // owners
        self.kept, self.came = [], []
        for r in range(owners // 2):
            away = lax.dynamic_slice_in_dim(values, (owner ^ (2 * r + 1)) * rows, rows, 0)
            self.kept.append(lax.dynamic_slice_in_dim(values, (owner ^ (2 * r)) * rows, rows, 0))
            self.came.append(swap(away, 1))

    def blocks(self):
        return [add(kept, came) for kept, came in zip(self.kept, self.came)]


class LineSum:
    def __init__(self, share):
        self.share = share
        self.moving = lax.ppermute(self.share, "seq", [(0, 1), (3, 2)])

    def across(self):
        self.share = add(self.share, self.moving)
        self.moving = lax.ppermute(self.share, "seq", [(1, 2), (2, 1)])

    def outwards(self):
        self.share = add(self.share, self.moving)
        self.moving = lax.ppermute(self.share, "seq", [(1, 0), (2, 3)])

    def result(self):
        place = lax.axis_index("seq")
        inner = (place == 1) | (place == 2)
        return jnp.where(inner, self.share, self.moving).astype(f32)


def gather_group(line):
    rows = []
    for piece in line:
        rows += [piece, swap(piece, 2, "ctx")]
    pairs = [jnp.concatenate(rows[2 * i : 2 * i + 2], axis=0) for i in range(4)]
    others = [swap(pair, 1, "ctx") for pair in pairs]
    return jnp.concatenate([half for both in zip(pairs, others) for half in both], axis=0)


class GroupSum:
    def __init__(self, values):
        shaped = values.reshape(4, 2, 2, -1, values.shape[1])
        self.kept, self.came = shaped[:, 0], swap(shaped[:, 1], 1, "ctx")

    def along_x(self):
        pair = add(self.kept, self.came)
        self.kept, self.came = pair[:, 0], swap(pair[:, 1], 2, "ctx")

    def along_seq(self):
        line = add(self.kept, self.came)
        self.kept, self.came = line[0], [swap(line[m], m, "seq") for m in (1, 2, 3)]

    def result(self):
        total = self.kept.astype(f32)
        for values in self.came:
            total = total + values.astype(f32)
        return total


def spread(rows):
    count = lax.axis_size(GROUP)
    shaped = rows.reshape(count, -1, rows.shape[1])
    return lax.all_to_all(shaped, GROUP, 0, 0, tiled=True).reshape(rows.shape)


def place_body(at_ref, values_ref, gate_ref, up_ref):
    count = gate_ref.shape[1]
    gate_ref[...] = values_ref[0, :, :count].astype(f32)
    up_ref[...] = values_ref[0, :, count:].astype(f32)


def place_columns(values, at):
    chips, rows, both = values.shape
    count = both // 2
    if count % 128:
        gate = jnp.zeros((rows, chips * count), f32)
        up = jnp.zeros((rows, chips * count), f32)
        for r in range(chips):
            block, start = values[r].astype(f32), (at ^ r) * count
            gate = lax.dynamic_update_slice_in_dim(gate, block[:, :count], start, 1)
            up = lax.dynamic_update_slice_in_dim(up, block[:, count:], start, 1)
        return gate, up
    shape = jax.ShapeDtypeStruct((rows, chips * count), f32)
    return pl.pallas_call(
        place_body,
        grid_spec=pltpu.PrefetchScalarGridSpec(
            num_scalar_prefetch=1,
            grid=(chips,),
            in_specs=[pl.BlockSpec((1, rows, both), lambda t, at_ref: (at_ref[0] ^ t, 0, 0))],
            out_specs=[pl.BlockSpec((rows, count), lambda t, at_ref: (0, t))] * 2,
        ),
        out_shape=(shape, shape),
        cost_estimate=pl.CostEstimate(
            flops=0, bytes_accessed=10 * chips * rows * both // 2, transcendentals=0
        ),
        compiler_params=pltpu.CompilerParams(vmem_limit_bytes=24 * 1024 * 1024),
        name="place_columns",
    )(at.astype(jnp.int32)[None], values)


def stack_heads(block, heads, rows, first):
    return jnp.concatenate(
        [
            block[b * rows : (b + 1) * rows, (first + h) * HEAD_DIM : (first + h + 1) * HEAD_DIM]
            for b in range(2)
            for h in range(heads)
        ],
        axis=0,
    )


def spread_heads(stacked, heads, rows, b):
    return jnp.concatenate(
        [stacked[(b * heads + h) * rows : (b * heads + h + 1) * rows] for h in range(heads)], axis=1
    )


def forward_body(
    q_ref, kv_ref, o_ref, ot_ref, lse_ref, kvt, qs, m_s, l_s, *, groups, heads, rows, blocks
):
    c = pl.program_id(0)
    keys = kv_ref.shape[0] * rows
    width = 2 * heads * rows
    half = heads * rows

    @pl.when(c == 0)
    def _():
        def one(kt, carry):
            for g in range(groups):
                tile = kv_ref[:, kt, :, g * 128 : (g + 1) * 128].reshape(keys, 128)
                kvt[g, kt] = tile.astype(f32).T.astype(bf16)[HEAD_DIM:]
            return carry

        lax.fori_loop(0, blocks, one, 0)

    for g in range(groups):
        q = stack_heads(q_ref[...], heads, rows, g * heads)
        qs[g] = jnp.concatenate([q, jnp.zeros((width, HEAD_DIM), bf16)], axis=1)

    def tiles(kt, lo, first):
        scores = []
        for g in range(groups):
            kv = kv_ref[:, kt, :, g * 128 : (g + 1) * 128].reshape(keys, 128)
            scores.append(dot(kv, qs[g, lo:], NT))
        for g in range(groups):
            st = scores[g]
            peak = jnp.max(st, axis=0, keepdims=True)
            if not first:
                m_old = m_s[g, :, lo:]
                peak = jnp.maximum(m_old, peak)
            p = jnp.exp2(st - peak)
            total = jnp.sum(p, axis=0, keepdims=True)
            pv = dot(kvt[g, kt], p.astype(bf16))
            if first:
                l_s[g, :, lo:] = total
                ot_ref[0, g, :, lo:] = pv
            else:
                shrink = jnp.exp2(m_old - peak)
                l_s[g, :, lo:] = l_s[g, :, lo:] * shrink + total
                ot_ref[0, g, :, lo:] = ot_ref[0, g, :, lo:] * shrink + pv
            m_s[g, :, lo:] = peak

    def step(kt, carry):
        tiles(kt, 0, False)
        return carry

    tiles(0, 0, True)
    lax.fori_loop(1, 2 * c + 1, step, 0)
    tiles(2 * c + 1, half, False)
    for g in range(groups):
        total = l_s[g]
        o = ot_ref[0, g] / total
        ot_ref[0, g] = o
        lse_ref[0, g : g + 1, :] = m_s[g] + jnp.log2(total)
        stacked = o.T.astype(bf16)
        for b in range(2):
            o_ref[b * rows : (b + 1) * rows, g * heads * HEAD_DIM : (g + 1) * heads * HEAD_DIM] = (
                spread_heads(stacked, heads, rows, b)
            )


def attend_forward(q, kv, first, groups):
    devices, blocks, rows, kv_width = kv.shape
    heads = q.shape[1] * 128 // HEAD_DIM // kv_width
    wide = heads * HEAD_DIM * groups
    width = 2 * heads * rows
    pairs = blocks // 2
    keys = devices * rows
    tiles = groups * blocks * (blocks + 1) // 2
    at = first // groups
    return pl.pallas_call(
        partial(forward_body, groups=groups, heads=heads, rows=rows, blocks=blocks),
        grid=(pairs,),
        out_shape=(
            jax.ShapeDtypeStruct((q.shape[0], wide), bf16),
            jax.ShapeDtypeStruct((pairs, groups, HEAD_DIM, width), f32),
            jax.ShapeDtypeStruct((pairs, groups, width), f32),
        ),
        in_specs=[
            pl.BlockSpec((2 * rows, wide), lambda c: (c, at)),
            pl.BlockSpec((devices, blocks, rows, groups * 128), lambda c: (0, 0, 0, at)),
        ],
        out_specs=(
            pl.BlockSpec((2 * rows, wide), lambda c: (c, 0)),
            pl.BlockSpec((1, groups, HEAD_DIM, width), lambda c: (c, 0, 0, 0)),
            pl.BlockSpec((1, groups, width), lambda c: (c, 0, 0)),
        ),
        scratch_shapes=[
            pltpu.VMEM((groups, blocks, HEAD_DIM, keys), bf16),
            pltpu.VMEM((groups, width, 128), bf16),
            pltpu.VMEM((groups, 1, width), f32),
            pltpu.VMEM((groups, 1, width), f32),
        ],
        compiler_params=pltpu.CompilerParams(vmem_limit_bytes=40 * 1024 * 1024),
        cost_estimate=pl.CostEstimate(
            flops=tiles * keys * width * 128 * 8,
            bytes_accessed=6 * 1024 * 1024,
            transcendentals=tiles * keys * width // 2,
        ),
        name="attend_forward",
    )(q, kv)


def backward_body(
    q_ref,
    do_ref,
    kv_ref,
    ot_ref,
    lse_ref,
    dq_ref,
    dkv_ref,
    kt_s,
    qs,
    dos,
    d_s,
    dqt,
    acc,
    *,
    groups,
    heads,
    rows,
    blocks,
    start,
):
    c = pl.program_id(0) + start
    devices = kv_ref.shape[0]
    keys = devices * rows
    width = 2 * heads * rows
    half = heads * rows

    @pl.when(c == start)
    def _():
        def one(kt, carry):
            for g in range(groups):
                tile = kv_ref[:, kt, :, g * 128 : (g + 1) * 128].reshape(keys, 128)
                kt_s[g, kt] = tile.astype(f32).T.astype(bf16)[:HEAD_DIM]
                acc[g, kt] = jnp.zeros((keys, 128), f32)
            return carry

        lax.fori_loop(0, blocks, one, 0)

    zero = jnp.zeros((width, HEAD_DIM), bf16)
    for g in range(groups):
        q = stack_heads(q_ref[...], heads, rows, g * heads)
        do = stack_heads(do_ref[...], heads, rows, g * heads)
        qs[g] = jnp.concatenate([q, zero], axis=1)
        dos[g] = jnp.concatenate([zero, do], axis=1)
        d_s[g] = jnp.sum(do.astype(f32).T * ot_ref[0, g], axis=0, keepdims=True)
        dqt[g] = jnp.zeros((HEAD_DIM, width), f32)

    def tiles(kt, lo):
        kvs = [
            kv_ref[:, kt, :, g * 128 : (g + 1) * 128].reshape(keys, 128) for g in range(groups)
        ]
        sts = [dot(kvs[g], qs[g, lo:], NT) for g in range(groups)]
        dpts = [dot(kvs[g], dos[g, lo:], NT) for g in range(groups)]
        ps = [jnp.exp2(sts[g] - lse_ref[0, g : g + 1, lo:]) for g in range(groups)]
        dss = [(ps[g] * (dpts[g] - d_s[g, :, lo:])).astype(bf16) for g in range(groups)]
        for g in range(groups):
            dqt[g, :, lo:] += dot(kt_s[g, kt], dss[g])
        for g in range(groups):
            acc[g, kt] += dot(dss[g], qs[g, lo:]) + dot(ps[g].astype(bf16), dos[g, lo:])

    def step(kt, carry):
        tiles(kt, 0)
        return carry

    lax.fori_loop(0, 2 * c + 1, step, 0)
    tiles(2 * c + 1, half)
    for g in range(groups):
        dq = (dqt[g] * (HEAD_DIM**-0.5)).T.astype(bf16)
        for b in range(2):
            dq_ref[b * rows : (b + 1) * rows, g * heads * HEAD_DIM : (g + 1) * heads * HEAD_DIM] = (
                spread_heads(dq, heads, rows, b)
            )

    @pl.when(c == start + pl.num_programs(0) - 1)
    def _():
        column = lax.broadcasted_iota(jnp.int32, (1, 128), 1)
        factor = jnp.where(column < HEAD_DIM, ln_2, 1.0)

        def one(kt, carry):
            for g in range(groups):
                dkv_ref[:, kt, :, g * 128 : (g + 1) * 128] = (
                    (acc[g, kt] * factor).astype(bf16).reshape(devices, rows, 128)
                )
            return carry

        lax.fori_loop(0, blocks, one, 0)


def attend_backward(q, do, kv, ot, lse, start, count):
    groups = KV_HEADS
    devices, blocks, rows, kv_width = kv.shape
    heads = q.shape[1] * 128 // HEAD_DIM // kv_width
    wide = heads * HEAD_DIM * groups
    width = 2 * heads * rows
    keys = devices * rows
    tiles = groups * sum(4 * c + 3 for c in range(start, start + count))
    kv_shape = (devices, blocks, rows, groups * 128)
    return pl.pallas_call(
        partial(backward_body, groups=groups, heads=heads, rows=rows, blocks=blocks, start=start),
        grid=(count,),
        out_shape=(
            jax.ShapeDtypeStruct((2 * rows * count, wide), bf16),
            jax.ShapeDtypeStruct(kv_shape, bf16),
        ),
        in_specs=[
            pl.BlockSpec((2 * rows, wide), lambda c: (c + start, 0)),
            pl.BlockSpec((2 * rows, wide), lambda c: (c + start, 0)),
            pl.BlockSpec(kv_shape, lambda c: (0, 0, 0, 0)),
            pl.BlockSpec((1, groups, HEAD_DIM, width), lambda c: (c + start, 0, 0, 0)),
            pl.BlockSpec((1, groups, width), lambda c: (c + start, 0, 0)),
        ],
        out_specs=(
            pl.BlockSpec((2 * rows, wide), lambda c: (c, 0)),
            pl.BlockSpec(kv_shape, lambda c: (0, 0, 0, 0)),
        ),
        scratch_shapes=[
            pltpu.VMEM((groups, blocks, HEAD_DIM, keys), bf16),
            pltpu.VMEM((groups, width, 128), bf16),
            pltpu.VMEM((groups, width, 128), bf16),
            pltpu.VMEM((groups, 1, width), f32),
            pltpu.VMEM((groups, HEAD_DIM, width), f32),
            pltpu.VMEM((groups, blocks, keys, 128), f32),
        ],
        compiler_params=pltpu.CompilerParams(vmem_limit_bytes=40 * 1024 * 1024),
        cost_estimate=pl.CostEstimate(
            flops=tiles * keys * width * 128 * 10,
            bytes_accessed=8 * 1024 * 1024,
            transcendentals=tiles * keys * width // 2,
        ),
        name="attend_backward",
    )(q, do, kv, ot, lse)


def turn_lanes(values, cosine, sine):
    count, width = values.shape
    lane = lax.broadcasted_iota(jnp.int32, (count, width), 1) % HEAD_DIM
    half_width = HEAD_DIM // 2
    other = jnp.where(
        lane < half_width,
        pltpu.roll(values, width - half_width, 1),
        pltpu.roll(values, half_width, 1),
    )
    times = width // cosine.shape[1]
    return values * jnp.tile(cosine, (1, times)) + other * jnp.tile(sine, (1, times))


def project_body(x_ref, w_ref, cosine_ref, sine_ref, out_ref, *, scale):
    values = dot(x_ref[...], w_ref[...])
    out_ref[...] = (turn_lanes(values, cosine_ref[...], sine_ref[...]) * scale).astype(bf16)


def project(x, weight, cosine, sine, scale, width):
    count, depth = x.shape
    tile = min(width, 512)
    return pl.pallas_call(
        partial(project_body, scale=scale),
        grid=(width // tile,),
        out_shape=jax.ShapeDtypeStruct((count, width), bf16),
        in_specs=[
            pl.BlockSpec((count, depth), lambda i: (0, 0)),
            pl.BlockSpec((depth, tile), lambda i: (0, i)),
            pl.BlockSpec(cosine.shape, lambda i: (0, 0)),
            pl.BlockSpec(sine.shape, lambda i: (0, 0)),
        ],
        out_specs=pl.BlockSpec((count, tile), lambda i: (0, i)),
        compiler_params=pltpu.CompilerParams(vmem_limit_bytes=24 * 1024 * 1024),
        cost_estimate=pl.CostEstimate(
            flops=2 * count * depth * width,
            bytes_accessed=2 * (count * depth + depth * width + count * width),
            transcendentals=0,
        ),
        name="project",
    )(x, weight, cosine, sine)


def turn_body(x_ref, cosine_ref, sine_ref, out_ref):
    values = x_ref[...].astype(f32)
    out_ref[...] = turn_lanes(values, cosine_ref[...], sine_ref[...]).astype(bf16)


def turn_back(x, cosine, sine):
    count, width = x.shape
    tile = min(width, 512)
    return pl.pallas_call(
        turn_body,
        grid=(width // tile,),
        out_shape=jax.ShapeDtypeStruct(x.shape, bf16),
        in_specs=[
            pl.BlockSpec((count, tile), lambda i: (0, i)),
            pl.BlockSpec(cosine.shape, lambda i: (0, 0)),
            pl.BlockSpec(sine.shape, lambda i: (0, 0)),
        ],
        out_specs=pl.BlockSpec((count, tile), lambda i: (0, i)),
        cost_estimate=pl.CostEstimate(
            flops=6 * count * width, bytes_accessed=4 * count * width, transcendentals=0
        ),
        name="turn_back",
    )(x, cosine, -sine)


def on_device(
    tokens,
    positions,
    cotangent,
    query_weight,
    key_weight,
    value_weight,
    output_weight,
    gate_weight,
    up_weight,
    down_weight,
    first_gain,
    second_gain,
):
    token_count, width = tokens.shape
    group = lax.axis_size(GROUP)
    owners = lax.axis_size(PLANE)
    owner = lax.axis_index(PLANE)
    lane = owner % 2
    chip = owner // 2
    chips = owners // 2
    rows = token_count // group
    own_rows = query_weight.shape[0]
    hidden_part = gate_weight.shape[1] // chips
    down_rows = down_weight.shape[0]
    kv_width = key_weight.shape[1]
    line = lax.axis_size("seq")
    line_place = lax.axis_index("seq")
    direct = [r for r in range(1, chips) if r & (r - 1) == 0]
    indirect = [r for r in range(1, chips) if r & (r - 1)]

    digits = jnp.stack([positions // 256, positions % 256], axis=1).astype(bf16)
    moved = spread(jnp.concatenate([tokens, jnp.pad(digits, ((0, 0), (0, 126)))], axis=1))
    by_head = (own_rows, KV_HEADS, 1, HEAD_DIM)
    gains = jnp.pad(jnp.stack([first_gain, second_gain], axis=1), ((0, 0), (0, 126)))
    pair_own = jnp.concatenate([key_weight.reshape(by_head), value_weight.reshape(by_head)], 2)
    pair_own = jnp.concatenate([pair_own.reshape(own_rows, 2 * kv_width), gains], axis=1)
    pair_weight = gather_plane(pair_own)
    query_full = lax.all_gather(query_weight, PLANE, axis=0, tiled=True)
    output_full = lax.all_gather(output_weight, PLANE, axis=0, tiled=True)
    scales = pair_weight[:, 2 * kv_width : 2 * kv_width + 2].astype(f32).T
    first_scale, second_scale = scales[0:1], scales[1:2]

    def columns(r, first, count):
        start = (chip ^ r) * hidden_part
        parts = []
        for weight in (gate_weight, up_weight):
            some = lax.dynamic_slice_in_dim(weight, first, count, 0)
            parts.append(lax.dynamic_slice_in_dim(some, start, hidden_part, 1))
        return jnp.concatenate(parts, axis=1)

    blocks = [columns(r, 0, own_rows) for r in range(chips)]

    places = moved[:, width].astype(f32) * 256.0 + moved[:, width + 1].astype(f32)
    cosine, sine = angles_of(places)
    is_key = jnp.arange(2 * HEAD_DIM) < HEAD_DIM
    pair_cosine, pair_sine = jnp.where(is_key, cosine, 1.0), jnp.where(is_key, sine, 0.0)
    inputs = moved[:, :width].astype(f32)
    first_normed, first_inverse = normalize(inputs)
    first_input = (first_normed * first_scale).astype(bf16)
    paired = project(first_input, pair_weight, pair_cosine, pair_sine, 1.0, 2 * kv_width)

    line_pairs = [paired] + [swap(paired, m, "seq") for m in (1, 2, 3)]
    both_full = jnp.broadcast_to(moved[0, 0] * 0.0, (own_rows * owners, 2 * hidden_part))
    line_pairs[0], both_full = tie(line_pairs[0], both_full)
    all_pairs = gather_group(line_pairs).reshape(group, group, rows, -1)
    query_scale = HEAD_DIM**-0.5 * log2_e
    queries = project(first_input, query_full, cosine, sine, query_scale, width)

    queries, all_pairs, blocks, cotangent, down_weight = tie(
        queries, all_pairs, blocks, cotangent, down_weight
    )
    blocks = to_chips(blocks)
    slopes = spread(cotangent)
    down_other = swap(down_weight, 1)
    own_other = swap(blocks[0], 1)
    attended, raw_outputs, log_sums = attend_forward(queries, all_pairs, 0, KV_HEADS)
    attended, down_other, own_other = tie(attended, down_other, own_other)

    middle = inputs + dot(attended, output_full)
    second_normed, second_inverse = normalize(middle)
    second_input = (second_normed * second_scale).astype(bf16)
    second_input, slopes = tie(second_input, slopes)
    feed_input = ChipGather(second_input)
    feed_input.first()
    both_full = lax.dynamic_update_slice_in_dim(both_full, blocks[0], owner * own_rows, 0)
    both_full = lax.dynamic_update_slice_in_dim(both_full, own_other, (owner ^ 1) * own_rows, 0)
    down_full = jnp.where(
        lane == 0,
        jnp.concatenate([down_weight, down_other], axis=0),
        jnp.concatenate([down_other, down_weight], axis=0),
    )
    feed_input.ends, blocks, both_full, down_full, slopes = tie(
        feed_input.ends, blocks, both_full, down_full, slopes
    )
    feed_input.second()
    feed_slope = ChipGather(slopes)
    feed_slope.first()
    for r in range(1, chips):
        other = swap(blocks[r], 1)
        both_full = lax.dynamic_update_slice_in_dim(
            both_full, blocks[r], (owner ^ (2 * r)) * own_rows, 0
        )
        both_full = lax.dynamic_update_slice_in_dim(
            both_full, other, (owner ^ (2 * r + 1)) * own_rows, 0
        )
    feed_slope.ends, feed_input.rest = tie(feed_slope.ends, feed_input.rest)
    feed_slope.second()
    feed_input = feed_input.result()

    gate_values = dot(feed_input, both_full[:, :hidden_part])
    up_values = dot(feed_input, both_full[:, hidden_part:])
    feed_slope.rest, up_values, gate_values = tie(feed_slope.rest, up_values, gate_values)
    feed_slope = feed_slope.result()
    hidden_slope = dot(feed_slope, down_full, NT)
    gate_sigmoid = jax.nn.sigmoid(gate_values)
    hidden = (gate_values * gate_sigmoid * up_values).astype(bf16)
    gate_slope = (
        hidden_slope * up_values * gate_sigmoid * (1.0 + gate_values * (1.0 - gate_sigmoid))
    ).astype(bf16)
    up_slope = (hidden_slope * gate_values * gate_sigmoid).astype(bf16)
    both_slope = jnp.concatenate([gate_slope, up_slope], axis=1)

    def by_chip(share):
        return [share[r * token_count : (r + 1) * token_count] for r in range(chips)]

    def for_chips(features):
        count = 2 * own_rows
        return [
            lax.dynamic_slice_in_dim(features, (chip ^ r) * count, count, 1) for r in range(chips)
        ]

    def swap_rows(share):
        count = share.shape[0] // 2
        kept = lax.dynamic_slice_in_dim(share, lane * count, count, 0)
        return kept, swap(lax.dynamic_slice_in_dim(share, (1 - lane) * count, count, 0), 1)

    feed_share = dot(both_slope, both_full, NT).astype(bf16)
    feed_share, both_slope, hidden = tie(feed_share, both_slope, hidden)
    second_parts = to_chips(by_chip(feed_share))
    down_rows_two = swap_rows(dot(hidden, feed_slope, TN).astype(bf16))
    both_slope, down_rows_two = tie(both_slope, down_rows_two)
    down_part = lax.psum_scatter(add(*down_rows_two), "seq", scatter_dimension=0, tiled=True)
    both_lanes = LaneSum(dot(feed_input, both_slope, TN).astype(bf16))
    both_stack = jnp.stack(both_lanes.blocks())
    second_parts, both_stack = tie(second_parts, both_stack)
    both_part = lax.psum_scatter(both_stack, "seq", scatter_dimension=1, tiled=True)
    second_slope = add_all(second_parts)
    second_gain_share = jnp.sum(second_slope * second_normed, axis=0)
    middle_slope = slopes.astype(f32) + norm_backward(
        second_slope * second_scale, second_normed, second_inverse
    )
    attention_slope = middle_slope.astype(bf16)
    attended_slope = dot(attention_slope, output_full, NT).astype(bf16)

    attended_slope, attention_slope, first_input, attended = tie(
        attended_slope, attention_slope, first_input, attended
    )
    slope_chunks = to_chips([attention_slope] * chips)
    attended_columns = to_chips(for_chips(attended))
    first_columns = to_chips(for_chips(first_input))
    query_turned, pair_terms = attend_backward(
        queries, attended_slope, all_pairs, raw_outputs, log_sums, 0, group // 2
    )
    query_turned, pair_terms, slope_chunks, attended_columns, first_columns, down_part = tie(
        query_turned, pair_terms, slope_chunks, attended_columns, first_columns, down_part
    )

    pair_slope = GroupSum(pair_terms.reshape(token_count * group, -1))
    down_sum = lax.all_gather(down_part, "seq", axis=0, tiled=True)
    query_slope = turn_back(query_turned, cosine, sine)
    query_side = dot(query_slope, query_full, NT)
    pair_slope.came, query_slope, query_side, both_part, hidden, slope_chunks = tie(
        pair_slope.came, query_slope, query_side, both_part, hidden, slope_chunks
    )
    pair_slope.along_x()
    both_part = to_chips([both_part[r] for r in range(chips)])
    out_share = dot(hidden, down_full).astype(bf16)
    output_share = dot(
        jnp.concatenate(attended_columns), jnp.concatenate(slope_chunks), TN
    ).astype(bf16)
    pair_slope.came, both_part, out_share, output_share, query_slope = tie(
        pair_slope.came, both_part, out_share, output_share, query_slope
    )
    pair_slope.along_seq()
    both_stack = jnp.stack(both_part)
    query_chunks = to_chips([query_slope] * chips)
    output_own = add(*swap_rows(output_share))
    pair_slope.came, output_own, both_stack, down_sum = tie(
        pair_slope.came, output_own, both_stack, down_sum
    )
    both_sums = lax.all_gather(both_stack, "seq", axis=1, tiled=True)
    outputs = LineSum(output_own)
    kv_slope = turn_back(pair_slope.result().astype(bf16), pair_cosine, pair_sine)
    first_slope = query_side + dot(kv_slope, pair_weight[:, : 2 * kv_width], NT)
    input_gradient = middle_slope + norm_backward(
        first_slope * first_scale, first_normed, first_inverse
    )
    gain_shares = jnp.stack([jnp.sum(first_slope * first_normed, axis=0), second_gain_share])
    input_gradient, kv_slope, gain_shares, query_chunks, outputs.moving = tie(
        input_gradient.astype(bf16),
        kv_slope,
        gain_shares.astype(bf16),
        query_chunks,
        outputs.moving,
    )
    kv_chunks = to_chips([kv_slope] * chips)
    gain_parts = to_chips(for_chips(gain_shares))
    outputs.across()
    first_columns = jnp.concatenate(first_columns)
    query_share = dot(first_columns, jnp.concatenate(query_chunks), TN).astype(bf16)
    query_own = add(*swap_rows(query_share))
    query_own, kv_chunks, gain_parts, outputs.moving, input_gradient, out_share = tie(
        query_own, kv_chunks, gain_parts, outputs.moving, input_gradient, out_share
    )
    outputs.outwards()
    squares = LineSum(query_own)
    input_gradient = spread(input_gradient)
    out_parts = to_chips(by_chip(out_share))
    kv_share = dot(first_columns, jnp.concatenate(kv_chunks), TN).astype(bf16)
    gain_two = swap_rows(add_all(gain_parts).T.astype(bf16))
    pairs = jnp.concatenate(
        [add(*swap_rows(kv_share)), jnp.pad(add(*gain_two), ((0, 0), (0, 126)))], axis=1
    )
    squares.moving, pairs, outputs.moving, input_gradient = tie(
        squares.moving, pairs, outputs.moving, input_gradient
    )
    squares.across()
    pairs = LineSum(pairs)
    squares.moving, pairs.moving, out_parts = tie(squares.moving, pairs.moving, out_parts)
    squares.outwards()
    pairs.across()
    layer_output = spread((middle + add_all(out_parts)).astype(bf16))
    squares.moving, pairs.moving = tie(squares.moving, pairs.moving)
    pairs.outwards()
    pairs.moving, both_sums, layer_output = tie(pairs.moving, both_sums, layer_output)

    input_gradient = input_gradient.astype(f32)
    down_gradient = down_sum.astype(f32)
    query_gradient, output_gradient = squares.result(), outputs.result()
    pairs = pairs.result()
    gain_gradients = pairs[:, 2 * kv_width : 2 * kv_width + 2].T
    pairs = pairs[:, : 2 * kv_width].reshape(own_rows, KV_HEADS, 2, HEAD_DIM)
    gate_gradient, up_gradient = place_columns(both_sums, chip)
    return (
        layer_output,
        input_gradient,
        query_gradient,
        pairs[:, :, 0].reshape(own_rows, kv_width),
        pairs[:, :, 1].reshape(own_rows, kv_width),
        output_gradient,
        gate_gradient,
        up_gradient,
        down_gradient,
        gain_gradients[0],
        gain_gradients[1],
    )


def solution(mesh):
    tokens = P(("dp", "seq", "ctx"), None)
    rows = P(PLANE, None)
    return jax.shard_map(
        on_device,
        mesh=mesh,
        in_specs=(tokens, P(("dp", "seq", "ctx")), tokens) + (rows,) * 7 + (P(PLANE),) * 2,
        out_specs=(tokens,) * 2 + (rows,) * 7 + (P(PLANE),) * 2,
        check_vma=False,
    )
```

```python
from functools import partial

import jax
import jax.numpy as jnp
from jax import lax
from jax.experimental import pallas as pl
from jax.experimental.pallas import tpu as pltpu
from jax.sharding import PartitionSpec as P

HEADS = 32
KV_HEADS = 4
HEAD_DIM = 64
BLOCK = 256

epsilon = 1e-05
rotary_base = 10000.0
log2_e = 1.4426950408889634
ln_2 = 0.6931471805599453
bf16, f32 = jnp.bfloat16, jnp.float32
PLANE = ("dp", "ctx")
GROUP = ("seq", "ctx")
NT = (((1,), (1,)), ((), ()))
NN = (((1,), (0,)), ((), ()))
TN = (((0,), (0,)), ((), ()))


def dot(left, right, dims=NN):
    return lax.dot_general(left, right, dims, preferred_element_type=f32)


def normalize(features):
    inverse_rms = lax.rsqrt(jnp.mean(features * features, axis=-1, keepdims=True) + epsilon)
    return (features * inverse_rms, inverse_rms)


def norm_backward(slopes, normed, inverse_rms):
    return inverse_rms * (slopes - normed * jnp.mean(slopes * normed, axis=-1, keepdims=True))


def angles_of(places):
    lane = jnp.arange(2 * HEAD_DIM)
    exponent = (lane % (HEAD_DIM // 2)).astype(f32) * (2.0 / HEAD_DIM)
    frequency = rotary_base ** (-exponent)
    angles = places[:, None] * frequency[None, :]
    sign = jnp.where(lane % HEAD_DIM < HEAD_DIM // 2, -1.0, 1.0)
    return jnp.cos(angles), jnp.sin(angles) * sign


def tie(*values):
    return lax.optimization_barrier(values)


def swap(values, mask, axes=PLANE):
    count = lax.axis_size(axes)
    return lax.ppermute(values, axes, [(i, i ^ mask) for i in range(count)])


def halves(count):
    return (slice(0, count // 2), slice(count // 2, count))


class ChipGather:
    def __init__(self, own):
        self.own = own

    def first(self):
        self.ends = {}
        r = 1
        while r < lax.axis_size(PLANE) // 2:
            self.ends[r] = swap(self.own, r << 1)
            r *= 2

    def second(self):
        top, bottom = halves(self.own.shape[0])
        parts = {r: (values[top], values[bottom]) for r, values in self.ends.items()}
        for r in range(1, lax.axis_size(PLANE) // 2):
            low, high = r & -r, 1 << (r.bit_length() - 1)
            if low != high:
                first = swap(parts[r ^ low][0], low << 1)
                parts[r] = (first, swap(parts[r ^ high][1], high << 1))
        self.rest = {r: both for r, both in parts.items() if r not in self.ends}

    def chunks(self):
        half = self.own.shape[0] // 2
        chunks = [(0, 0, self.own)]
        for r in range(1, lax.axis_size(PLANE) // 2):
            if r in self.ends:
                chunks.append((r, 0, self.ends[r]))
            else:
                chunks += [(r, 0, self.rest[r][0]), (r, half, self.rest[r][1])]
        return chunks

    def result(self):
        return jnp.concatenate([values for _, _, values in self.chunks()], axis=0)


def add(left, right):
    return (left.astype(f32) + right.astype(f32)).astype(bf16)


class ChipSum:
    def __init__(self, blocks):
        self.parts = [[block[half] for half in halves(block.shape[0])] for block in blocks]

    def first(self):
        chips = len(self.parts)
        self.came = {}
        for r in sorted(range(1, chips), key=lambda r: -bin(r).count("1")):
            low, high = r & -r, 1 << (r.bit_length() - 1)
            if low == high:
                continue
            if bin(r).count("1") < bin(chips - 1).count("1"):
                self.settle(r)
            self.came[r ^ low, 0, r] = swap(self.parts[r][0], low << 1)
            self.came[r ^ high, 1, r] = swap(self.parts[r][1], high << 1)

    def settle(self, only=None):
        for key in sorted(self.came):
            if only is None or key[0] == only:
                self.parts[key[0]][key[1]] = add(self.parts[key[0]][key[1]], self.came.pop(key))

    def second(self):
        self.settle()
        self.ends = []
        r = 1
        while r < len(self.parts):
            self.ends.append(swap(jnp.concatenate(self.parts[r], axis=0), r << 1))
            r *= 2

    def result(self):
        return add_all([jnp.concatenate(self.parts[0], axis=0)] + self.ends)


def to_chips(blocks):
    return [block if r == 0 else swap(block, r << 1) for r, block in enumerate(blocks)]


def add_all(values):
    total = values[0].astype(f32)
    for other in values[1:]:
        total = total + other.astype(f32)
    return total


def gather_plane(own):
    rows = own.shape[0]
    owner = lax.axis_index(PLANE)
    full = jnp.zeros((rows * lax.axis_size(PLANE), own.shape[1]), own.dtype)
    gather = ChipGather(own)
    gather.first()
    gather.second()
    for r, first, chunk in gather.chunks():
        other = swap(chunk, 1)
        full = lax.dynamic_update_slice_in_dim(full, chunk, (owner ^ (2 * r)) * rows + first, 0)
        full = lax.dynamic_update_slice_in_dim(full, other, (owner ^ (2 * r + 1)) * rows + first, 0)
    return full


class LaneSum:
    def __init__(self, values):
        owners = lax.axis_size(PLANE)
        owner = lax.axis_index(PLANE)
        rows = values.shape[0] // owners
        self.kept, self.came = [], []
        for r in range(owners // 2):
            away = lax.dynamic_slice_in_dim(values, (owner ^ (2 * r + 1)) * rows, rows, 0)
            self.kept.append(lax.dynamic_slice_in_dim(values, (owner ^ (2 * r)) * rows, rows, 0))
            self.came.append(swap(away, 1))

    def blocks(self):
        return [add(kept, came) for kept, came in zip(self.kept, self.came)]


class LineTree:
    def __init__(self, share):
        self.share = share
        self.moving = lax.ppermute(share, "seq", [(0, 1), (3, 2)])

    def across(self):
        self.share = add(self.share, self.moving)
        self.moving = lax.ppermute(self.share, "seq", [(1, 2), (2, 1)])

    def outwards(self):
        self.share = add(self.share, self.moving)
        self.moving = lax.ppermute(self.share, "seq", [(1, 0), (2, 3)])

    def result(self):
        place = lax.axis_index("seq")
        inner = (place == 1) | (place == 2)
        return jnp.where(inner, self.share, self.moving).astype(f32)


class LineSum:
    def __init__(self, share):
        self.share = share

    def scatter(self):
        place = lax.axis_index("seq")
        count = lax.axis_size("seq")
        rows = self.share.shape[0] // count

        def part(m):
            return lax.dynamic_slice_in_dim(self.share, (place ^ m) * rows, rows, 0)

        self.parts = [part(0)] + [swap(part(m), m, "seq") for m in range(1, count)]

    def gather(self):
        total = add_all(self.parts).astype(bf16)
        self.parts = [total] + [swap(total, m, "seq") for m in range(1, len(self.parts))]

    def result(self):
        place = lax.axis_index("seq")
        rows = self.parts[0].shape[0]
        out = self.share
        for m, values in enumerate(self.parts):
            out = lax.dynamic_update_slice_in_dim(out, values, (place ^ m) * rows, 0)
        return out


def gather_lanes(pairs):
    pairs = [jnp.concatenate(pair, axis=0) for pair in pairs]
    others = [swap(pair, 1, "ctx") for pair in pairs]
    return jnp.concatenate([half for both in zip(pairs, others) for half in both], axis=0)


class GroupSum:
    def __init__(self, values):
        shaped = values.reshape(4, 2, 2, -1, values.shape[1])
        self.kept, self.came = shaped[:, 0], swap(shaped[:, 1], 1, "ctx")

    def along_x(self):
        pair = add(self.kept, self.came)
        self.kept, self.came = pair[:, 0], swap(pair[:, 1], 2, "ctx")

    def along_seq(self):
        line = add(self.kept, self.came)
        self.kept, self.came = line[0], [swap(line[m], m, "seq") for m in (1, 2, 3)]

    def result(self):
        total = self.kept.astype(f32)
        for values in self.came:
            total = total + values.astype(f32)
        return total


def spread(rows):
    count = lax.axis_size(GROUP)
    shaped = rows.reshape(count, -1, rows.shape[1])
    return lax.all_to_all(shaped, GROUP, 0, 0, tiled=True).reshape(rows.shape)


def place_body(at_ref, values_ref, gate_ref, up_ref):
    count = gate_ref.shape[1]
    gate_ref[...] = values_ref[0, :, :count].astype(f32)
    up_ref[...] = values_ref[0, :, count:].astype(f32)


def place_columns(values, at):
    chips, rows, both = values.shape
    count = both // 2
    if count % 128:
        gate = jnp.zeros((rows, chips * count), f32)
        up = jnp.zeros((rows, chips * count), f32)
        for r in range(chips):
            block, start = values[r].astype(f32), (at ^ r) * count
            gate = lax.dynamic_update_slice_in_dim(gate, block[:, :count], start, 1)
            up = lax.dynamic_update_slice_in_dim(up, block[:, count:], start, 1)
        return gate, up
    shape = jax.ShapeDtypeStruct((rows, chips * count), f32)
    return pl.pallas_call(
        place_body,
        grid_spec=pltpu.PrefetchScalarGridSpec(
            num_scalar_prefetch=1,
            grid=(chips,),
            in_specs=[pl.BlockSpec((1, rows, both), lambda t, at_ref: (at_ref[0] ^ t, 0, 0))],
            out_specs=[pl.BlockSpec((rows, count), lambda t, at_ref: (0, t))] * 2,
        ),
        out_shape=(shape, shape),
        cost_estimate=pl.CostEstimate(
            flops=0, bytes_accessed=10 * chips * rows * both // 2, transcendentals=0
        ),
        compiler_params=pltpu.CompilerParams(vmem_limit_bytes=24 * 1024 * 1024),
        name="place_columns",
    )(at.astype(jnp.int32)[None], values)


class LineGather:
    def __init__(self, own):
        self.own, self.right, self.left = own, [], []

    def step(self):
        at = len(self.right)
        count = lax.axis_size("seq")
        right = self.right[-1] if at else self.own
        left = self.left[-1] if at else self.own
        pairs = [(i, i + 1) for i in range(at, count - 1)]
        self.right.append(lax.ppermute(right, "seq", pairs))
        back = [(i, i - 1) for i in range(count - 1 - at, 0, -1)]
        self.left.append(lax.ppermute(left, "seq", back))

    def result(self):
        count = lax.axis_size("seq")
        rows = self.own.shape[0]
        around = jnp.concatenate([*self.right[::-1], self.own, *self.left], axis=0)
        start = (count - 1 - lax.axis_index("seq")) * rows
        return lax.dynamic_slice_in_dim(around, start, count * rows, 0)


def stack_heads(block, heads, rows, first):
    return jnp.concatenate(
        [
            block[b * rows : (b + 1) * rows, (first + h) * HEAD_DIM : (first + h + 1) * HEAD_DIM]
            for b in range(2)
            for h in range(heads)
        ],
        axis=0,
    )


def spread_heads(stacked, heads, rows, b):
    return jnp.concatenate(
        [stacked[(b * heads + h) * rows : (b * heads + h + 1) * rows] for h in range(heads)], axis=1
    )


def forward_body(
    q_ref, kv_ref, o_ref, ot_ref, lse_ref, kvt, qs, m_s, l_s, *, groups, heads, rows, blocks
):
    c = pl.program_id(0)
    keys = kv_ref.shape[0] * rows
    width = 2 * heads * rows
    half = heads * rows

    @pl.when(c == 0)
    def _():
        def one(kt, carry):
            for g in range(groups):
                tile = kv_ref[:, kt, :, g * 128 : (g + 1) * 128].reshape(keys, 128)
                kvt[g, kt] = tile.astype(f32).T.astype(bf16)[HEAD_DIM:]
            return carry

        lax.fori_loop(0, blocks, one, 0)

    for g in range(groups):
        q = stack_heads(q_ref[...], heads, rows, g * heads)
        qs[g] = jnp.concatenate([q, jnp.zeros((width, HEAD_DIM), bf16)], axis=1)

    def tiles(kt, lo, first):
        scores = []
        for g in range(groups):
            kv = kv_ref[:, kt, :, g * 128 : (g + 1) * 128].reshape(keys, 128)
            scores.append(dot(kv, qs[g, lo:], NT))
        for g in range(groups):
            st = scores[g]
            peak = jnp.max(st, axis=0, keepdims=True)
            if not first:
                m_old = m_s[g, :, lo:]
                peak = jnp.maximum(m_old, peak)
            p = jnp.exp2(st - peak)
            total = jnp.sum(p, axis=0, keepdims=True)
            pv = dot(kvt[g, kt], p.astype(bf16))
            if first:
                l_s[g, :, lo:] = total
                ot_ref[0, g, :, lo:] = pv
            else:
                shrink = jnp.exp2(m_old - peak)
                l_s[g, :, lo:] = l_s[g, :, lo:] * shrink + total
                ot_ref[0, g, :, lo:] = ot_ref[0, g, :, lo:] * shrink + pv
            m_s[g, :, lo:] = peak

    def step(kt, carry):
        tiles(kt, 0, False)
        return carry

    tiles(0, 0, True)
    lax.fori_loop(1, 2 * c + 1, step, 0)
    tiles(2 * c + 1, half, False)
    for g in range(groups):
        total = l_s[g]
        o = ot_ref[0, g] / total
        ot_ref[0, g] = o
        lse_ref[0, g : g + 1, :] = m_s[g] + jnp.log2(total)
        stacked = o.T.astype(bf16)
        for b in range(2):
            o_ref[b * rows : (b + 1) * rows, g * heads * HEAD_DIM : (g + 1) * heads * HEAD_DIM] = (
                spread_heads(stacked, heads, rows, b)
            )


def attend_forward(q, kv, first, groups):
    devices, blocks, rows, kv_width = kv.shape
    heads = q.shape[1] * 128 // HEAD_DIM // kv_width
    wide = heads * HEAD_DIM * groups
    width = 2 * heads * rows
    pairs = blocks // 2
    keys = devices * rows
    tiles = groups * blocks * (blocks + 1) // 2
    at = first // groups
    return pl.pallas_call(
        partial(forward_body, groups=groups, heads=heads, rows=rows, blocks=blocks),
        grid=(pairs,),
        out_shape=(
            jax.ShapeDtypeStruct((q.shape[0], wide), bf16),
            jax.ShapeDtypeStruct((pairs, groups, HEAD_DIM, width), f32),
            jax.ShapeDtypeStruct((pairs, groups, width), f32),
        ),
        in_specs=[
            pl.BlockSpec((2 * rows, wide), lambda c: (c, at)),
            pl.BlockSpec((devices, blocks, rows, groups * 128), lambda c: (0, 0, 0, at)),
        ],
        out_specs=(
            pl.BlockSpec((2 * rows, wide), lambda c: (c, 0)),
            pl.BlockSpec((1, groups, HEAD_DIM, width), lambda c: (c, 0, 0, 0)),
            pl.BlockSpec((1, groups, width), lambda c: (c, 0, 0)),
        ),
        scratch_shapes=[
            pltpu.VMEM((groups, blocks, HEAD_DIM, keys), bf16),
            pltpu.VMEM((groups, width, 128), bf16),
            pltpu.VMEM((groups, 1, width), f32),
            pltpu.VMEM((groups, 1, width), f32),
        ],
        compiler_params=pltpu.CompilerParams(vmem_limit_bytes=40 * 1024 * 1024),
        cost_estimate=pl.CostEstimate(
            flops=tiles * keys * width * 128 * 8,
            bytes_accessed=6 * 1024 * 1024,
            transcendentals=tiles * keys * width // 2,
        ),
        name="attend_forward",
    )(q, kv)


def backward_body(
    q_ref,
    do_ref,
    kv_ref,
    ot_ref,
    lse_ref,
    dq_ref,
    dkv_ref,
    kt_s,
    qs,
    dos,
    d_s,
    dqt,
    acc,
    *,
    groups,
    heads,
    rows,
    blocks,
    start,
):
    c = pl.program_id(0) + start
    devices = kv_ref.shape[0]
    keys = devices * rows
    width = 2 * heads * rows
    half = heads * rows

    @pl.when(c == start)
    def _():
        def one(kt, carry):
            for g in range(groups):
                tile = kv_ref[:, kt, :, g * 128 : (g + 1) * 128].reshape(keys, 128)
                kt_s[g, kt] = tile.astype(f32).T.astype(bf16)[:HEAD_DIM]
                acc[g, kt] = jnp.zeros((keys, 128), f32)
            return carry

        lax.fori_loop(0, blocks, one, 0)

    zero = jnp.zeros((width, HEAD_DIM), bf16)
    for g in range(groups):
        q = stack_heads(q_ref[...], heads, rows, g * heads)
        do = stack_heads(do_ref[...], heads, rows, g * heads)
        qs[g] = jnp.concatenate([q, zero], axis=1)
        dos[g] = jnp.concatenate([zero, do], axis=1)
        d_s[g] = jnp.sum(do.astype(f32).T * ot_ref[0, g], axis=0, keepdims=True)
        dqt[g] = jnp.zeros((HEAD_DIM, width), f32)

    def tiles(kt, lo):
        kvs = [
            kv_ref[:, kt, :, g * 128 : (g + 1) * 128].reshape(keys, 128) for g in range(groups)
        ]
        sts = [dot(kvs[g], qs[g, lo:], NT) for g in range(groups)]
        dpts = [dot(kvs[g], dos[g, lo:], NT) for g in range(groups)]
        ps = [jnp.exp2(sts[g] - lse_ref[0, g : g + 1, lo:]) for g in range(groups)]
        dss = [(ps[g] * (dpts[g] - d_s[g, :, lo:])).astype(bf16) for g in range(groups)]
        for g in range(groups):
            dqt[g, :, lo:] += dot(kt_s[g, kt], dss[g])
        for g in range(groups):
            acc[g, kt] += dot(dss[g], qs[g, lo:]) + dot(ps[g].astype(bf16), dos[g, lo:])

    def step(kt, carry):
        tiles(kt, 0)
        return carry

    lax.fori_loop(0, 2 * c + 1, step, 0)
    tiles(2 * c + 1, half)
    for g in range(groups):
        dq = (dqt[g] * (HEAD_DIM**-0.5)).T.astype(bf16)
        for b in range(2):
            dq_ref[b * rows : (b + 1) * rows, g * heads * HEAD_DIM : (g + 1) * heads * HEAD_DIM] = (
                spread_heads(dq, heads, rows, b)
            )

    @pl.when(c == start + pl.num_programs(0) - 1)
    def _():
        column = lax.broadcasted_iota(jnp.int32, (1, 128), 1)
        factor = jnp.where(column < HEAD_DIM, ln_2, 1.0)

        def one(kt, carry):
            for g in range(groups):
                dkv_ref[:, kt, :, g * 128 : (g + 1) * 128] = (
                    (acc[g, kt] * factor).astype(bf16).reshape(devices, rows, 128)
                )
            return carry

        lax.fori_loop(0, blocks, one, 0)


def attend_backward(q, do, kv, ot, lse, start, count):
    groups = KV_HEADS
    devices, blocks, rows, kv_width = kv.shape
    heads = q.shape[1] * 128 // HEAD_DIM // kv_width
    wide = heads * HEAD_DIM * groups
    width = 2 * heads * rows
    keys = devices * rows
    tiles = groups * sum(4 * c + 3 for c in range(start, start + count))
    kv_shape = (devices, blocks, rows, groups * 128)
    return pl.pallas_call(
        partial(backward_body, groups=groups, heads=heads, rows=rows, blocks=blocks, start=start),
        grid=(count,),
        out_shape=(
            jax.ShapeDtypeStruct((2 * rows * count, wide), bf16),
            jax.ShapeDtypeStruct(kv_shape, bf16),
        ),
        in_specs=[
            pl.BlockSpec((2 * rows, wide), lambda c: (c + start, 0)),
            pl.BlockSpec((2 * rows, wide), lambda c: (c + start, 0)),
            pl.BlockSpec(kv_shape, lambda c: (0, 0, 0, 0)),
            pl.BlockSpec((1, groups, HEAD_DIM, width), lambda c: (c + start, 0, 0, 0)),
            pl.BlockSpec((1, groups, width), lambda c: (c + start, 0, 0)),
        ],
        out_specs=(
            pl.BlockSpec((2 * rows, wide), lambda c: (c, 0)),
            pl.BlockSpec(kv_shape, lambda c: (0, 0, 0, 0)),
        ),
        scratch_shapes=[
            pltpu.VMEM((groups, blocks, HEAD_DIM, keys), bf16),
            pltpu.VMEM((groups, width, 128), bf16),
            pltpu.VMEM((groups, width, 128), bf16),
            pltpu.VMEM((groups, 1, width), f32),
            pltpu.VMEM((groups, HEAD_DIM, width), f32),
            pltpu.VMEM((groups, blocks, keys, 128), f32),
        ],
        compiler_params=pltpu.CompilerParams(vmem_limit_bytes=40 * 1024 * 1024),
        cost_estimate=pl.CostEstimate(
            flops=tiles * keys * width * 8,
            bytes_accessed=8 * 1024 * 1024,
            transcendentals=0,
        ),
        name="attend_backward",
    )(q, do, kv, ot, lse)


def turn_lanes(values, cosine, sine):
    count, width = values.shape
    lane = lax.broadcasted_iota(jnp.int32, (count, width), 1) % HEAD_DIM
    half_width = HEAD_DIM // 2
    other = jnp.where(
        lane < half_width,
        pltpu.roll(values, width - half_width, 1),
        pltpu.roll(values, half_width, 1),
    )
    times = width // cosine.shape[1]
    return values * jnp.tile(cosine, (1, times)) + other * jnp.tile(sine, (1, times))


def project_body(x_ref, w_ref, cosine_ref, sine_ref, out_ref, *, scale):
    values = dot(x_ref[...], w_ref[...])
    out_ref[...] = (turn_lanes(values, cosine_ref[...], sine_ref[...]) * scale).astype(bf16)


def project(x, weight, cosine, sine, scale, width):
    count, depth = x.shape
    tile = min(width, 512)
    return pl.pallas_call(
        partial(project_body, scale=scale),
        grid=(width // tile,),
        out_shape=jax.ShapeDtypeStruct((count, width), bf16),
        in_specs=[
            pl.BlockSpec((count, depth), lambda i: (0, 0)),
            pl.BlockSpec((depth, tile), lambda i: (0, i)),
            pl.BlockSpec(cosine.shape, lambda i: (0, 0)),
            pl.BlockSpec(sine.shape, lambda i: (0, 0)),
        ],
        out_specs=pl.BlockSpec((count, tile), lambda i: (0, i)),
        compiler_params=pltpu.CompilerParams(vmem_limit_bytes=24 * 1024 * 1024),
        cost_estimate=pl.CostEstimate(
            flops=2 * count * depth * width,
            bytes_accessed=2 * (count * depth + depth * width + count * width),
            transcendentals=0,
        ),
        name="project",
    )(x, weight, cosine, sine)


def turn_body(x_ref, cosine_ref, sine_ref, out_ref):
    values = x_ref[...].astype(f32)
    out_ref[...] = turn_lanes(values, cosine_ref[...], sine_ref[...]).astype(bf16)


def turn_back(x, cosine, sine):
    count, width = x.shape
    tile = min(width, 512)
    return pl.pallas_call(
        turn_body,
        grid=(width // tile,),
        out_shape=jax.ShapeDtypeStruct(x.shape, bf16),
        in_specs=[
            pl.BlockSpec((count, tile), lambda i: (0, i)),
            pl.BlockSpec(cosine.shape, lambda i: (0, 0)),
            pl.BlockSpec(sine.shape, lambda i: (0, 0)),
        ],
        out_specs=pl.BlockSpec((count, tile), lambda i: (0, i)),
        cost_estimate=pl.CostEstimate(
            flops=6 * count * width, bytes_accessed=4 * count * width, transcendentals=0
        ),
        name="turn_back",
    )(x, cosine, -sine)


def tiles_of(count):
    return [(at, min(256, count - at)) for at in range(0, count, 256)]


def feed_body(x_ref, w_ref, values_ref, hidden_ref):
    count = hidden_ref.shape[1]
    for at, size in tiles_of(count):
        here, there = slice(at, at + size), slice(count + at, count + at + size)
        gate = dot(x_ref[...], w_ref[:, here])
        up = dot(x_ref[...], w_ref[:, there])
        values_ref[:, here] = gate
        values_ref[:, there] = up
        hidden_ref[:, here] = (gate * jax.nn.sigmoid(gate) * up).astype(bf16)


def feed_back_body(c_ref, d_ref, values_ref, slope_ref):
    count = d_ref.shape[0]
    for at, size in tiles_of(count):
        here, there = slice(at, at + size), slice(count + at, count + at + size)
        slope = dot(c_ref[...], d_ref[here, :], NT)
        gate, up = values_ref[:, here], values_ref[:, there]
        sigmoid = jax.nn.sigmoid(gate)
        silu = gate * sigmoid
        slope_ref[:, here] = (slope * up * sigmoid * (1.0 + gate * (1.0 - sigmoid))).astype(bf16)
        slope_ref[:, there] = (slope * silu).astype(bf16)


def feed(x, both, count):
    tokens, width = x.shape
    tile = min(tokens, 256)
    return pl.pallas_call(
        feed_body,
        grid=(tokens // tile,),
        out_shape=(
            jax.ShapeDtypeStruct((tokens, 2 * count), f32),
            jax.ShapeDtypeStruct((tokens, count), bf16),
        ),
        in_specs=[
            pl.BlockSpec((tile, width), lambda i: (i, 0)),
            pl.BlockSpec(both.shape, lambda i: (0, 0), pipeline_mode=pl.Buffered(1)),
        ],
        out_specs=(
            pl.BlockSpec((tile, 2 * count), lambda i: (i, 0)),
            pl.BlockSpec((tile, count), lambda i: (i, 0)),
        ),
        compiler_params=pltpu.CompilerParams(vmem_limit_bytes=40 * 1024 * 1024),
        cost_estimate=pl.CostEstimate(
            flops=4 * tokens * width * count,
            bytes_accessed=2 * (tokens * width + 2 * width * count + 5 * tokens * count),
            transcendentals=tokens * count,
        ),
        name="feed",
    )(x, both)


def feed_back(cotangent, down, values):
    tokens, width = cotangent.shape
    count = down.shape[0]
    tile = min(tokens, 256)
    return pl.pallas_call(
        feed_back_body,
        grid=(tokens // tile,),
        out_shape=jax.ShapeDtypeStruct((tokens, 2 * count), bf16),
        in_specs=[
            pl.BlockSpec((tile, width), lambda i: (i, 0)),
            pl.BlockSpec(down.shape, lambda i: (0, 0), pipeline_mode=pl.Buffered(1)),
            pl.BlockSpec((tile, 2 * count), lambda i: (i, 0)),
        ],
        out_specs=pl.BlockSpec((tile, 2 * count), lambda i: (i, 0)),
        compiler_params=pltpu.CompilerParams(vmem_limit_bytes=32 * 1024 * 1024),
        cost_estimate=pl.CostEstimate(
            flops=2 * tokens * width * count,
            bytes_accessed=2 * (tokens * width + width * count + 6 * tokens * count),
            transcendentals=tokens * count,
        ),
        name="feed_back",
    )(cotangent, down, values)


def on_device(
    tokens,
    positions,
    cotangent,
    query_weight,
    key_weight,
    value_weight,
    output_weight,
    gate_weight,
    up_weight,
    down_weight,
    first_gain,
    second_gain,
):
    token_count, width = tokens.shape
    group = lax.axis_size(GROUP)
    owners = lax.axis_size(PLANE)
    owner = lax.axis_index(PLANE)
    lane = owner % 2
    chip = owner // 2
    chips = owners // 2
    rows = token_count // group
    own_rows = query_weight.shape[0]
    hidden_part = gate_weight.shape[1] // chips
    down_rows = down_weight.shape[0]
    kv_width = key_weight.shape[1]
    line = lax.axis_size("seq")
    line_place = lax.axis_index("seq")
    direct = [r for r in range(1, chips) if r & (r - 1) == 0]
    indirect = [r for r in range(1, chips) if r & (r - 1)]

    digits = jnp.stack([positions // 256, positions % 256], axis=1).astype(bf16)
    moved = spread(jnp.concatenate([tokens, jnp.pad(digits, ((0, 0), (0, 126)))], axis=1))
    by_head = (own_rows, KV_HEADS, 1, HEAD_DIM)
    gains = jnp.pad(jnp.stack([first_gain, second_gain], axis=1), ((0, 0), (0, 126)))
    pair_own = jnp.concatenate([key_weight.reshape(by_head), value_weight.reshape(by_head)], 2)
    pair_own = jnp.concatenate([pair_own.reshape(own_rows, 2 * kv_width), gains], axis=1)
    pair_weight = gather_plane(pair_own)
    query_full = lax.all_gather(query_weight, PLANE, axis=0, tiled=True)
    output_full = lax.all_gather(output_weight, PLANE, axis=0, tiled=True)
    scales = pair_weight[:, 2 * kv_width : 2 * kv_width + 2].astype(f32).T
    first_scale, second_scale = scales[0:1], scales[1:2]

    def columns(r, first, count):
        start = (chip ^ r) * hidden_part
        parts = []
        for weight in (gate_weight, up_weight):
            some = lax.dynamic_slice_in_dim(weight, first, count, 0)
            parts.append(lax.dynamic_slice_in_dim(some, start, hidden_part, 1))
        return jnp.concatenate(parts, axis=1)

    blocks = [columns(r, 0, own_rows) for r in range(chips)]

    places = moved[:, width].astype(f32) * 256.0 + moved[:, width + 1].astype(f32)
    cosine, sine = angles_of(places)
    is_key = jnp.arange(2 * HEAD_DIM) < HEAD_DIM
    pair_cosine, pair_sine = jnp.where(is_key, cosine, 1.0), jnp.where(is_key, sine, 0.0)
    inputs = moved[:, :width].astype(f32)
    first_normed, first_inverse = normalize(inputs)
    first_input = (first_normed * first_scale).astype(bf16)
    paired = project(first_input, pair_weight, pair_cosine, pair_sine, 1.0, 2 * kv_width)

    line_pairs = [paired] + [swap(paired, m, "seq") for m in (1, 2, 3)]
    both_full = jnp.broadcast_to(moved[0, 0] * 0.0, (own_rows * owners, 2 * hidden_part))
    line_pairs[0], both_full = tie(line_pairs[0], both_full)
    pairs = [(piece, swap(piece, 2, "ctx")) for piece in line_pairs]
    all_pairs = gather_lanes(pairs).reshape(group, group, rows, -1)
    query_scale = HEAD_DIM**-0.5 * log2_e
    queries = project(first_input, query_full, cosine, sine, query_scale, width)

    queries, all_pairs, blocks, cotangent, down_weight = tie(
        queries, all_pairs, blocks, cotangent, down_weight
    )
    blocks = to_chips(blocks)
    slopes = spread(cotangent)
    down_other = swap(down_weight, 1)
    own_other = swap(blocks[0], 1)
    attended, raw_outputs, log_sums = attend_forward(queries, all_pairs, 0, KV_HEADS)
    attended, down_other, own_other = tie(attended, down_other, own_other)

    middle = inputs + dot(attended, output_full)
    second_normed, second_inverse = normalize(middle)
    second_input = (second_normed * second_scale).astype(bf16)
    second_input, slopes = tie(second_input, slopes)
    feed_input = ChipGather(second_input)
    feed_input.first()
    both_full = lax.dynamic_update_slice_in_dim(both_full, blocks[0], owner * own_rows, 0)
    both_full = lax.dynamic_update_slice_in_dim(both_full, own_other, (owner ^ 1) * own_rows, 0)
    down_full = jnp.where(
        lane == 0,
        jnp.concatenate([down_weight, down_other], axis=0),
        jnp.concatenate([down_other, down_weight], axis=0),
    )
    feed_input.ends, blocks, both_full, down_full, slopes = tie(
        feed_input.ends, blocks, both_full, down_full, slopes
    )
    feed_input.second()
    feed_slope = ChipGather(slopes)
    feed_slope.first()
    for r in range(1, chips):
        other = swap(blocks[r], 1)
        both_full = lax.dynamic_update_slice_in_dim(
            both_full, blocks[r], (owner ^ (2 * r)) * own_rows, 0
        )
        both_full = lax.dynamic_update_slice_in_dim(
            both_full, other, (owner ^ (2 * r + 1)) * own_rows, 0
        )
    feed_slope.ends, feed_input.rest = tie(feed_slope.ends, feed_input.rest)
    feed_slope.second()
    feed_input = feed_input.result()

    if hidden_part % 128:
        gate_values = dot(feed_input, both_full[:, :hidden_part])
        up_values = dot(feed_input, both_full[:, hidden_part:])
        gate_sigmoid = jax.nn.sigmoid(gate_values)
        hidden = (gate_values * gate_sigmoid * up_values).astype(bf16)
    else:
        feed_values, hidden = feed(feed_input, both_full, hidden_part)
    hidden, feed_slope.rest = tie(hidden, feed_slope.rest)
    feed_slope = feed_slope.result()
    if hidden_part % 128:
        hidden_slope = dot(feed_slope, down_full, NT)
        gate_slope = (
            hidden_slope * up_values * gate_sigmoid * (1.0 + gate_values * (1.0 - gate_sigmoid))
        ).astype(bf16)
        up_slope = (hidden_slope * gate_values * gate_sigmoid).astype(bf16)
        both_slope = jnp.concatenate([gate_slope, up_slope], axis=1)
    else:
        both_slope = feed_back(feed_slope, down_full, feed_values)

    def by_chip(share):
        return [share[r * token_count : (r + 1) * token_count] for r in range(chips)]

    def for_chips(features):
        count = 2 * own_rows
        return [
            lax.dynamic_slice_in_dim(features, (chip ^ r) * count, count, 1) for r in range(chips)
        ]

    def swap_rows(share):
        count = share.shape[0] // 2
        kept = lax.dynamic_slice_in_dim(share, lane * count, count, 0)
        return kept, swap(lax.dynamic_slice_in_dim(share, (1 - lane) * count, count, 0), 1)

    feed_share = dot(both_slope, both_full, NT).astype(bf16)
    feed_share, both_slope, hidden = tie(feed_share, both_slope, hidden)
    second_slope = ChipSum(by_chip(feed_share))
    second_slope.first()
    down_share = dot(hidden, feed_slope, TN).astype(bf16)
    second_slope.came, down_share, both_slope = tie(second_slope.came, down_share, both_slope)
    second_slope.second()
    down_two = swap_rows(down_share)
    down_two, both_slope = tie(down_two, both_slope)
    down_part = lax.psum_scatter(add(*down_two), "seq", scatter_dimension=0, tiled=True)
    both_lanes = LaneSum(dot(feed_input, both_slope, TN).astype(bf16))
    both_stack = jnp.stack(both_lanes.blocks())
    second_slope.ends, both_stack = tie(second_slope.ends, both_stack)
    both_part = lax.psum_scatter(both_stack, "seq", scatter_dimension=1, tiled=True)
    second_slope = second_slope.result()
    second_gain_share = jnp.sum(second_slope * second_normed, axis=0)
    middle_slope = slopes.astype(f32) + norm_backward(
        second_slope * second_scale, second_normed, second_inverse
    )
    attention_slope = middle_slope.astype(bf16)
    attended_slope = dot(attention_slope, output_full, NT).astype(bf16)
    payload = [
        jnp.concatenate([attention_slope, *both], axis=1)
        for both in zip(for_chips(attended), for_chips(first_input))
    ]

    attended_slope, payload = tie(attended_slope, payload)
    payload = to_chips(payload)
    query_turned, pair_terms = attend_backward(
        queries, attended_slope, all_pairs, raw_outputs, log_sums, 0, group // 2
    )
    query_turned, pair_terms, payload, down_part = tie(
        query_turned, pair_terms, payload, down_part
    )

    pair_slope = GroupSum(pair_terms.reshape(token_count * group, -1))
    down_sum = lax.all_gather(down_part, "seq", axis=0, tiled=True)
    query_slope = turn_back(query_turned, cosine, sine)
    pair_slope.came, query_slope, payload = tie(pair_slope.came, query_slope, payload)
    pair_slope.along_x()
    payload = jnp.concatenate(payload)
    output_share = dot(payload[:, width : width + 2 * own_rows], payload[:, :width], TN)
    first_columns = payload[:, width + 2 * own_rows :]
    query_side = dot(query_slope, query_full, NT)
    pair_slope.came, output_share, query_side, query_slope, both_part, hidden = tie(
        pair_slope.came, output_share.astype(bf16), query_side, query_slope, both_part, hidden
    )
    pair_slope.along_seq()
    both_part = to_chips([both_part[r] for r in range(chips)])
    query_chunks = to_chips([query_slope] * chips)
    output_own = add(*swap_rows(output_share))
    out_share = dot(hidden, down_full).astype(bf16)
    pair_slope.came, both_part, output_own, out_share = tie(
        pair_slope.came, both_part, output_own, out_share
    )
    both_sums = lax.all_gather(jnp.stack(both_part), "seq", axis=1, tiled=True)
    kv_slope = turn_back(pair_slope.result().astype(bf16), pair_cosine, pair_sine)
    first_slope = query_side + dot(kv_slope, pair_weight[:, : 2 * kv_width], NT)
    input_gradient = middle_slope + norm_backward(
        first_slope * first_scale, first_normed, first_inverse
    )
    gain_shares = jnp.stack([jnp.sum(first_slope * first_normed, axis=0), second_gain_share])
    input_gradient, kv_slope, gain_shares, query_chunks = tie(
        input_gradient.astype(bf16), kv_slope, gain_shares.astype(bf16), query_chunks
    )
    kv_chunks = to_chips([kv_slope] * chips)
    gain_parts = to_chips(for_chips(gain_shares))
    query_share = dot(first_columns, jnp.concatenate(query_chunks), TN).astype(bf16)
    query_own = add(*swap_rows(query_share))
    query_own, kv_chunks, gain_parts, out_share, down_sum = tie(
        query_own, kv_chunks, gain_parts, out_share, down_sum
    )
    out_parts = to_chips(by_chip(out_share))
    kv_share = dot(first_columns, jnp.concatenate(kv_chunks), TN).astype(bf16)
    gain_two = swap_rows(add_all(gain_parts).T.astype(bf16))
    last = jnp.concatenate(
        [
            query_own,
            output_own,
            add(*swap_rows(kv_share)),
            jnp.pad(add(*gain_two), ((0, 0), (0, 126))),
        ],
        axis=1,
    )
    last, input_gradient, both_sums, down_sum = tie(last, input_gradient, both_sums, down_sum)
    lasts = [LineTree(last[half]) for half in halves(own_rows)[:1]]
    input_gradient = spread(input_gradient)
    gate_gradient, up_gradient = place_columns(both_sums, chip)
    lasts[0].moving, gate_gradient, last = tie(lasts[0].moving, gate_gradient, last)
    lasts[0].across()
    lasts.append(LineTree(last[halves(own_rows)[1]]))
    layer_output = (middle + add_all(out_parts)).astype(bf16)
    lasts[0].moving, lasts[1].moving, layer_output = tie(
        lasts[0].moving, lasts[1].moving, layer_output
    )
    lasts[0].outwards()
    lasts[1].across()
    layer_output = spread(layer_output)
    lasts[1].moving, input_gradient = tie(lasts[1].moving, input_gradient)
    lasts[1].outwards()
    down_gradient = down_sum.astype(f32)
    input_gradient = input_gradient.astype(f32)
    lasts[0].moving, lasts[1].moving, layer_output, down_gradient, input_gradient = tie(
        lasts[0].moving, lasts[1].moving, layer_output, down_gradient, input_gradient
    )

    last = jnp.concatenate([part.result() for part in lasts])
    query_gradient = last[:, :width]
    output_gradient = last[:, width : 2 * width]
    pairs = last[:, 2 * width :]
    gain_gradients = pairs[:, 2 * kv_width : 2 * kv_width + 2].T
    pairs = pairs[:, : 2 * kv_width].reshape(own_rows, KV_HEADS, 2, HEAD_DIM)
    return (
        layer_output,
        input_gradient,
        query_gradient,
        pairs[:, :, 0].reshape(own_rows, kv_width),
        pairs[:, :, 1].reshape(own_rows, kv_width),
        output_gradient,
        gate_gradient,
        up_gradient,
        down_gradient,
        gain_gradients[0],
        gain_gradients[1],
    )


def solution(mesh):
    tokens = P(("dp", "seq", "ctx"), None)
    rows = P(PLANE, None)
    return jax.shard_map(
        on_device,
        mesh=mesh,
        in_specs=(tokens, P(("dp", "seq", "ctx")), tokens) + (rows,) * 7 + (P(PLANE),) * 2,
        out_specs=(tokens,) * 2 + (rows,) * 7 + (P(PLANE),) * 2,
        check_vma=False,
    )
```

```python
from functools import partial

import jax
import jax.numpy as jnp
from jax import lax
from jax.experimental import pallas as pl
from jax.experimental.pallas import tpu as pltpu
from jax.sharding import PartitionSpec as P

HEADS = 32
KV_HEADS = 4
HEAD_DIM = 64
BLOCK = 256

epsilon = 1e-05
rotary_base = 10000.0
log2_e = 1.4426950408889634
ln_2 = 0.6931471805599453
bf16, f32 = jnp.bfloat16, jnp.float32
PLANE = ("dp", "ctx")
GROUP = ("seq", "ctx")
NT = (((1,), (1,)), ((), ()))
NN = (((1,), (0,)), ((), ()))
TN = (((0,), (0,)), ((), ()))


def dot(left, right, dims=NN):
    return lax.dot_general(left, right, dims, preferred_element_type=f32)


def normalize(features):
    inverse_rms = lax.rsqrt(jnp.mean(features * features, axis=-1, keepdims=True) + epsilon)
    return (features * inverse_rms, inverse_rms)


def norm_backward(slopes, normed, inverse_rms):
    return inverse_rms * (slopes - normed * jnp.mean(slopes * normed, axis=-1, keepdims=True))


def angles_of(places):
    lane = jnp.arange(2 * HEAD_DIM)
    exponent = (lane % (HEAD_DIM // 2)).astype(f32) * (2.0 / HEAD_DIM)
    frequency = rotary_base ** (-exponent)
    angles = places[:, None] * frequency[None, :]
    sign = jnp.where(lane % HEAD_DIM < HEAD_DIM // 2, -1.0, 1.0)
    return jnp.cos(angles), jnp.sin(angles) * sign


def tie(*values):
    return lax.optimization_barrier(values)


def swap(values, mask, axes=PLANE):
    count = lax.axis_size(axes)
    return lax.ppermute(values, axes, [(i, i ^ mask) for i in range(count)])


def halves(count):
    return (slice(0, count // 2), slice(count // 2, count))


class ChipGather:
    def __init__(self, own):
        self.own = own

    def first(self):
        self.ends = {}
        r = 1
        while r < lax.axis_size(PLANE) // 2:
            self.ends[r] = swap(self.own, r << 1)
            r *= 2

    def second(self):
        top, bottom = halves(self.own.shape[0])
        parts = {r: (values[top], values[bottom]) for r, values in self.ends.items()}
        for r in range(1, lax.axis_size(PLANE) // 2):
            low, high = r & -r, 1 << (r.bit_length() - 1)
            if low != high:
                first = swap(parts[r ^ low][0], low << 1)
                parts[r] = (first, swap(parts[r ^ high][1], high << 1))
        self.rest = {r: both for r, both in parts.items() if r not in self.ends}

    def chunks(self):
        half = self.own.shape[0] // 2
        chunks = [(0, 0, self.own)]
        for r in range(1, lax.axis_size(PLANE) // 2):
            if r in self.ends:
                chunks.append((r, 0, self.ends[r]))
            else:
                chunks += [(r, 0, self.rest[r][0]), (r, half, self.rest[r][1])]
        return chunks

    def result(self):
        return jnp.concatenate([values for _, _, values in self.chunks()], axis=0)


def add(left, right):
    return (left.astype(f32) + right.astype(f32)).astype(bf16)


class ChipSum:
    def __init__(self, blocks):
        self.parts = [[block[half] for half in halves(block.shape[0])] for block in blocks]

    def first(self):
        chips = len(self.parts)
        self.came = {}
        for r in sorted(range(1, chips), key=lambda r: -bin(r).count("1")):
            low, high = r & -r, 1 << (r.bit_length() - 1)
            if low == high:
                continue
            if bin(r).count("1") < bin(chips - 1).count("1"):
                self.settle(r)
            self.came[r ^ low, 0, r] = swap(self.parts[r][0], low << 1)
            self.came[r ^ high, 1, r] = swap(self.parts[r][1], high << 1)

    def settle(self, only=None):
        for key in sorted(self.came):
            if only is None or key[0] == only:
                self.parts[key[0]][key[1]] = add(self.parts[key[0]][key[1]], self.came.pop(key))

    def second(self):
        self.settle()
        self.ends = []
        r = 1
        while r < len(self.parts):
            self.ends.append(swap(jnp.concatenate(self.parts[r], axis=0), r << 1))
            r *= 2

    def result(self):
        return add_all([jnp.concatenate(self.parts[0], axis=0)] + self.ends)


def to_chips(blocks):
    return [block if r == 0 else swap(block, r << 1) for r, block in enumerate(blocks)]


def add_all(values):
    total = values[0].astype(f32)
    for other in values[1:]:
        total = total + other.astype(f32)
    return total


def gather_plane(own):
    rows = own.shape[0]
    owner = lax.axis_index(PLANE)
    full = jnp.zeros((rows * lax.axis_size(PLANE), own.shape[1]), own.dtype)
    gather = ChipGather(own)
    gather.first()
    gather.second()
    for r, first, chunk in gather.chunks():
        other = swap(chunk, 1)
        full = lax.dynamic_update_slice_in_dim(full, chunk, (owner ^ (2 * r)) * rows + first, 0)
        full = lax.dynamic_update_slice_in_dim(full, other, (owner ^ (2 * r + 1)) * rows + first, 0)
    return full


class LaneSum:
    def __init__(self, values):
        owners = lax.axis_size(PLANE)
        owner = lax.axis_index(PLANE)
        rows = values.shape[0] // owners
        self.kept, self.came = [], []
        for r in range(owners // 2):
            away = lax.dynamic_slice_in_dim(values, (owner ^ (2 * r + 1)) * rows, rows, 0)
            self.kept.append(lax.dynamic_slice_in_dim(values, (owner ^ (2 * r)) * rows, rows, 0))
            self.came.append(swap(away, 1))

    def blocks(self):
        return [add(kept, came) for kept, came in zip(self.kept, self.came)]


class LineTree:
    def __init__(self, share):
        self.share = share
        self.moving = lax.ppermute(share, "seq", [(0, 1), (3, 2)])

    def across(self):
        self.share = add(self.share, self.moving)
        self.moving = lax.ppermute(self.share, "seq", [(1, 2), (2, 1)])

    def outwards(self):
        self.share = add(self.share, self.moving)
        self.moving = lax.ppermute(self.share, "seq", [(1, 0), (2, 3)])

    def result(self):
        place = lax.axis_index("seq")
        inner = (place == 1) | (place == 2)
        return jnp.where(inner, self.share, self.moving).astype(f32)


class LineSum:
    def __init__(self, share):
        self.share = share

    def scatter(self):
        place = lax.axis_index("seq")
        count = lax.axis_size("seq")
        rows = self.share.shape[0] // count

        def part(m):
            return lax.dynamic_slice_in_dim(self.share, (place ^ m) * rows, rows, 0)

        self.parts = [part(0)] + [swap(part(m), m, "seq") for m in range(1, count)]

    def gather(self):
        total = add_all(self.parts).astype(bf16)
        self.parts = [total] + [swap(total, m, "seq") for m in range(1, len(self.parts))]

    def result(self):
        place = lax.axis_index("seq")
        rows = self.parts[0].shape[0]
        out = self.share
        for m, values in enumerate(self.parts):
            out = lax.dynamic_update_slice_in_dim(out, values, (place ^ m) * rows, 0)
        return out


def gather_lanes(pairs):
    pairs = [jnp.concatenate(pair, axis=0) for pair in pairs]
    others = [swap(pair, 1, "ctx") for pair in pairs]
    return jnp.concatenate([half for both in zip(pairs, others) for half in both], axis=0)


class GroupSum:
    def __init__(self, values):
        shaped = values.reshape(4, 2, 2, -1, values.shape[1])
        self.kept, self.came = shaped[:, 0], swap(shaped[:, 1], 1, "ctx")

    def along_x(self):
        pair = add(self.kept, self.came)
        self.kept, self.came = pair[:, 0], swap(pair[:, 1], 2, "ctx")

    def along_seq(self):
        line = add(self.kept, self.came)
        self.kept, self.came = line[0], [swap(line[m], m, "seq") for m in (1, 2, 3)]

    def result(self):
        total = self.kept.astype(f32)
        for values in self.came:
            total = total + values.astype(f32)
        return total


def spread(rows):
    count = lax.axis_size(GROUP)
    shaped = rows.reshape(count, -1, rows.shape[1])
    return lax.all_to_all(shaped, GROUP, 0, 0, tiled=True).reshape(rows.shape)


def place_body(at_ref, values_ref, gate_ref, up_ref):
    count = gate_ref.shape[1]
    gate_ref[...] = values_ref[0, :, :count].astype(f32)
    up_ref[...] = values_ref[0, :, count:].astype(f32)


def place_columns(values, at):
    chips, rows, both = values.shape
    count = both // 2
    if count % 128:
        gate = jnp.zeros((rows, chips * count), f32)
        up = jnp.zeros((rows, chips * count), f32)
        for r in range(chips):
            block, start = values[r].astype(f32), (at ^ r) * count
            gate = lax.dynamic_update_slice_in_dim(gate, block[:, :count], start, 1)
            up = lax.dynamic_update_slice_in_dim(up, block[:, count:], start, 1)
        return gate, up
    shape = jax.ShapeDtypeStruct((rows, chips * count), f32)
    return pl.pallas_call(
        place_body,
        grid_spec=pltpu.PrefetchScalarGridSpec(
            num_scalar_prefetch=1,
            grid=(chips,),
            in_specs=[pl.BlockSpec((1, rows, both), lambda t, at_ref: (at_ref[0] ^ t, 0, 0))],
            out_specs=[pl.BlockSpec((rows, count), lambda t, at_ref: (0, t))] * 2,
        ),
        out_shape=(shape, shape),
        cost_estimate=pl.CostEstimate(
            flops=0, bytes_accessed=10 * chips * rows * both // 2, transcendentals=0
        ),
        compiler_params=pltpu.CompilerParams(vmem_limit_bytes=24 * 1024 * 1024),
        name="place_columns",
    )(at.astype(jnp.int32)[None], values)


class LineGather:
    def __init__(self, own):
        self.own, self.right, self.left = own, [], []

    def step(self):
        at = len(self.right)
        count = lax.axis_size("seq")
        right = self.right[-1] if at else self.own
        left = self.left[-1] if at else self.own
        pairs = [(i, i + 1) for i in range(at, count - 1)]
        self.right.append(lax.ppermute(right, "seq", pairs))
        back = [(i, i - 1) for i in range(count - 1 - at, 0, -1)]
        self.left.append(lax.ppermute(left, "seq", back))

    def result(self):
        count = lax.axis_size("seq")
        rows = self.own.shape[0]
        around = jnp.concatenate([*self.right[::-1], self.own, *self.left], axis=0)
        start = (count - 1 - lax.axis_index("seq")) * rows
        return lax.dynamic_slice_in_dim(around, start, count * rows, 0)


def stack_heads(block, heads, rows, first):
    return jnp.concatenate(
        [
            block[b * rows : (b + 1) * rows, (first + h) * HEAD_DIM : (first + h + 1) * HEAD_DIM]
            for b in range(2)
            for h in range(heads)
        ],
        axis=0,
    )


def spread_heads(stacked, heads, rows, b):
    return jnp.concatenate(
        [stacked[(b * heads + h) * rows : (b * heads + h + 1) * rows] for h in range(heads)], axis=1
    )


def forward_body(
    q_ref, kv_ref, o_ref, ot_ref, lse_ref, kvt, qs, m_s, l_s, *, groups, heads, rows, blocks
):
    c = pl.program_id(0)
    keys = kv_ref.shape[0] * rows
    width = 2 * heads * rows
    half = heads * rows

    @pl.when(c == 0)
    def _():
        def one(kt, carry):
            for g in range(groups):
                tile = kv_ref[:, kt, :, g * 128 : (g + 1) * 128].reshape(keys, 128)
                kvt[g, kt] = tile.astype(f32).T.astype(bf16)[HEAD_DIM:]
            return carry

        lax.fori_loop(0, blocks, one, 0)

    for g in range(groups):
        q = stack_heads(q_ref[...], heads, rows, g * heads)
        qs[g] = jnp.concatenate([q, jnp.zeros((width, HEAD_DIM), bf16)], axis=1)

    def tiles(kts, lo, first):
        scores = []
        for g in range(groups):
            for kt in kts:
                kv = kv_ref[:, kt, :, g * 128 : (g + 1) * 128].reshape(keys, 128)
                scores.append(dot(kv, qs[g, lo:], NT))
        for g in range(groups):
            sts = scores[g * len(kts) : (g + 1) * len(kts)]
            peak = jnp.max(sts[0], axis=0, keepdims=True)
            for st in sts[1:]:
                peak = jnp.maximum(peak, jnp.max(st, axis=0, keepdims=True))
            if not first:
                m_old = m_s[g, :, lo:]
                peak = jnp.maximum(m_old, peak)
            total, pv = 0.0, 0.0
            for kt, st in zip(kts, sts):
                p = jnp.exp2(st - peak)
                total = total + jnp.sum(p, axis=0, keepdims=True)
                pv = pv + dot(kvt[g, kt], p.astype(bf16))
            if first:
                l_s[g, :, lo:] = total
                ot_ref[0, g, :, lo:] = pv
            else:
                shrink = jnp.exp2(m_old - peak)
                l_s[g, :, lo:] = l_s[g, :, lo:] * shrink + total
                ot_ref[0, g, :, lo:] = ot_ref[0, g, :, lo:] * shrink + pv
            m_s[g, :, lo:] = peak

    def step(i, carry):
        tiles((2 * i + 1, 2 * i + 2), 0, False)
        return carry

    tiles((0,), 0, True)
    lax.fori_loop(0, c, step, 0)
    tiles((2 * c + 1,), half, False)
    for g in range(groups):
        total = l_s[g]
        o = ot_ref[0, g] / total
        ot_ref[0, g] = o
        lse_ref[0, g : g + 1, :] = m_s[g] + jnp.log2(total)
        stacked = o.T.astype(bf16)
        for b in range(2):
            o_ref[b * rows : (b + 1) * rows, g * heads * HEAD_DIM : (g + 1) * heads * HEAD_DIM] = (
                spread_heads(stacked, heads, rows, b)
            )


def attend_forward(q, kv, first, groups):
    devices, blocks, rows, kv_width = kv.shape
    heads = q.shape[1] * 128 // HEAD_DIM // kv_width
    wide = heads * HEAD_DIM * groups
    width = 2 * heads * rows
    pairs = blocks // 2
    keys = devices * rows
    tiles = groups * blocks * (blocks + 1) // 2
    at = first // groups
    return pl.pallas_call(
        partial(forward_body, groups=groups, heads=heads, rows=rows, blocks=blocks),
        grid=(pairs,),
        out_shape=(
            jax.ShapeDtypeStruct((q.shape[0], wide), bf16),
            jax.ShapeDtypeStruct((pairs, groups, HEAD_DIM, width), f32),
            jax.ShapeDtypeStruct((pairs, groups, width), f32),
        ),
        in_specs=[
            pl.BlockSpec((2 * rows, wide), lambda c: (c, at)),
            pl.BlockSpec((devices, blocks, rows, groups * 128), lambda c: (0, 0, 0, at)),
        ],
        out_specs=(
            pl.BlockSpec((2 * rows, wide), lambda c: (c, 0)),
            pl.BlockSpec((1, groups, HEAD_DIM, width), lambda c: (c, 0, 0, 0)),
            pl.BlockSpec((1, groups, width), lambda c: (c, 0, 0)),
        ),
        scratch_shapes=[
            pltpu.VMEM((groups, blocks, HEAD_DIM, keys), bf16),
            pltpu.VMEM((groups, width, 128), bf16),
            pltpu.VMEM((groups, 1, width), f32),
            pltpu.VMEM((groups, 1, width), f32),
        ],
        compiler_params=pltpu.CompilerParams(vmem_limit_bytes=40 * 1024 * 1024),
        cost_estimate=pl.CostEstimate(
            flops=tiles * keys * width * 128 * 8,
            bytes_accessed=6 * 1024 * 1024,
            transcendentals=tiles * keys * width // 2,
        ),
        name="attend_forward",
    )(q, kv)


def backward_body(
    q_ref,
    do_ref,
    kv_ref,
    ot_ref,
    lse_ref,
    dq_ref,
    dkv_ref,
    kt_s,
    qs,
    dos,
    d_s,
    dqt,
    acc,
    *,
    groups,
    heads,
    rows,
    blocks,
    start,
):
    c = pl.program_id(0) + start
    devices = kv_ref.shape[0]
    keys = devices * rows
    width = 2 * heads * rows
    half = heads * rows

    @pl.when(c == start)
    def _():
        def one(kt, carry):
            for g in range(groups):
                tile = kv_ref[:, kt, :, g * 128 : (g + 1) * 128].reshape(keys, 128)
                kt_s[g, kt] = tile.astype(f32).T.astype(bf16)[:HEAD_DIM]
                acc[g, kt] = jnp.zeros((keys, 128), f32)
            return carry

        lax.fori_loop(0, blocks, one, 0)

    zero = jnp.zeros((width, HEAD_DIM), bf16)
    for g in range(groups):
        q = stack_heads(q_ref[...], heads, rows, g * heads)
        do = stack_heads(do_ref[...], heads, rows, g * heads)
        qs[g] = jnp.concatenate([q, zero], axis=1)
        dos[g] = jnp.concatenate([zero, do], axis=1)
        d_s[g] = jnp.sum(do.astype(f32).T * ot_ref[0, g], axis=0, keepdims=True)
        dqt[g] = jnp.zeros((HEAD_DIM, width), f32)

    def tiles(kt, lo):
        kvs = [
            kv_ref[:, kt, :, g * 128 : (g + 1) * 128].reshape(keys, 128) for g in range(groups)
        ]
        sts = [dot(kvs[g], qs[g, lo:], NT) for g in range(groups)]
        dpts = [dot(kvs[g], dos[g, lo:], NT) for g in range(groups)]
        ps = [jnp.exp2(sts[g] - lse_ref[0, g : g + 1, lo:]) for g in range(groups)]
        dss = [(ps[g] * (dpts[g] - d_s[g, :, lo:])).astype(bf16) for g in range(groups)]
        for g in range(groups):
            dqt[g, :, lo:] += dot(kt_s[g, kt], dss[g])
        for g in range(groups):
            acc[g, kt] += dot(dss[g], qs[g, lo:]) + dot(ps[g].astype(bf16), dos[g, lo:])

    def step(kt, carry):
        tiles(kt, 0)
        return carry

    lax.fori_loop(0, 2 * c + 1, step, 0)
    tiles(2 * c + 1, half)
    for g in range(groups):
        dq = (dqt[g] * (HEAD_DIM**-0.5)).T.astype(bf16)
        for b in range(2):
            dq_ref[b * rows : (b + 1) * rows, g * heads * HEAD_DIM : (g + 1) * heads * HEAD_DIM] = (
                spread_heads(dq, heads, rows, b)
            )

    @pl.when(c == start + pl.num_programs(0) - 1)
    def _():
        column = lax.broadcasted_iota(jnp.int32, (1, 128), 1)
        factor = jnp.where(column < HEAD_DIM, ln_2, 1.0)

        def one(kt, carry):
            for g in range(groups):
                dkv_ref[:, kt, :, g * 128 : (g + 1) * 128] = (
                    (acc[g, kt] * factor).astype(bf16).reshape(devices, rows, 128)
                )
            return carry

        lax.fori_loop(0, blocks, one, 0)


def attend_backward(q, do, kv, ot, lse, start, count):
    groups = KV_HEADS
    devices, blocks, rows, kv_width = kv.shape
    heads = q.shape[1] * 128 // HEAD_DIM // kv_width
    wide = heads * HEAD_DIM * groups
    width = 2 * heads * rows
    keys = devices * rows
    tiles = groups * sum(4 * c + 3 for c in range(start, start + count))
    kv_shape = (devices, blocks, rows, groups * 128)
    return pl.pallas_call(
        partial(backward_body, groups=groups, heads=heads, rows=rows, blocks=blocks, start=start),
        grid=(count,),
        out_shape=(
            jax.ShapeDtypeStruct((2 * rows * count, wide), bf16),
            jax.ShapeDtypeStruct(kv_shape, bf16),
        ),
        in_specs=[
            pl.BlockSpec((2 * rows, wide), lambda c: (c + start, 0)),
            pl.BlockSpec((2 * rows, wide), lambda c: (c + start, 0)),
            pl.BlockSpec(kv_shape, lambda c: (0, 0, 0, 0)),
            pl.BlockSpec((1, groups, HEAD_DIM, width), lambda c: (c + start, 0, 0, 0)),
            pl.BlockSpec((1, groups, width), lambda c: (c + start, 0, 0)),
        ],
        out_specs=(
            pl.BlockSpec((2 * rows, wide), lambda c: (c, 0)),
            pl.BlockSpec(kv_shape, lambda c: (0, 0, 0, 0)),
        ),
        scratch_shapes=[
            pltpu.VMEM((groups, blocks, HEAD_DIM, keys), bf16),
            pltpu.VMEM((groups, width, 128), bf16),
            pltpu.VMEM((groups, width, 128), bf16),
            pltpu.VMEM((groups, 1, width), f32),
            pltpu.VMEM((groups, HEAD_DIM, width), f32),
            pltpu.VMEM((groups, blocks, keys, 128), f32),
        ],
        compiler_params=pltpu.CompilerParams(vmem_limit_bytes=40 * 1024 * 1024),
        cost_estimate=pl.CostEstimate(
            flops=tiles * keys * width * 8,
            bytes_accessed=8 * 1024 * 1024,
            transcendentals=0,
        ),
        name="attend_backward",
    )(q, do, kv, ot, lse)


def turn_lanes(values, cosine, sine):
    count, width = values.shape
    lane = lax.broadcasted_iota(jnp.int32, (count, width), 1) % HEAD_DIM
    half_width = HEAD_DIM // 2
    other = jnp.where(
        lane < half_width,
        pltpu.roll(values, width - half_width, 1),
        pltpu.roll(values, half_width, 1),
    )
    times = width // cosine.shape[1]
    return values * jnp.tile(cosine, (1, times)) + other * jnp.tile(sine, (1, times))


def project_body(x_ref, w_ref, cosine_ref, sine_ref, out_ref, *, scale):
    values = dot(x_ref[...], w_ref[...])
    out_ref[...] = (turn_lanes(values, cosine_ref[...], sine_ref[...]) * scale).astype(bf16)


def project(x, weight, cosine, sine, scale, width):
    count, depth = x.shape
    tile = min(width, 512)
    return pl.pallas_call(
        partial(project_body, scale=scale),
        grid=(width // tile,),
        out_shape=jax.ShapeDtypeStruct((count, width), bf16),
        in_specs=[
            pl.BlockSpec((count, depth), lambda i: (0, 0)),
            pl.BlockSpec((depth, tile), lambda i: (0, i)),
            pl.BlockSpec(cosine.shape, lambda i: (0, 0)),
            pl.BlockSpec(sine.shape, lambda i: (0, 0)),
        ],
        out_specs=pl.BlockSpec((count, tile), lambda i: (0, i)),
        compiler_params=pltpu.CompilerParams(vmem_limit_bytes=24 * 1024 * 1024),
        cost_estimate=pl.CostEstimate(
            flops=2 * count * depth * width,
            bytes_accessed=2 * (count * depth + depth * width + count * width),
            transcendentals=0,
        ),
        name="project",
    )(x, weight, cosine, sine)


def turn_body(x_ref, cosine_ref, sine_ref, out_ref):
    values = x_ref[...].astype(f32)
    out_ref[...] = turn_lanes(values, cosine_ref[...], sine_ref[...]).astype(bf16)


def turn_back(x, cosine, sine):
    count, width = x.shape
    tile = min(width, 512)
    return pl.pallas_call(
        turn_body,
        grid=(width // tile,),
        out_shape=jax.ShapeDtypeStruct(x.shape, bf16),
        in_specs=[
            pl.BlockSpec((count, tile), lambda i: (0, i)),
            pl.BlockSpec(cosine.shape, lambda i: (0, 0)),
            pl.BlockSpec(sine.shape, lambda i: (0, 0)),
        ],
        out_specs=pl.BlockSpec((count, tile), lambda i: (0, i)),
        cost_estimate=pl.CostEstimate(
            flops=6 * count * width, bytes_accessed=4 * count * width, transcendentals=0
        ),
        name="turn_back",
    )(x, cosine, -sine)


def tiles_of(count):
    return [(at, min(256, count - at)) for at in range(0, count, 256)]


def feed_body(x_ref, w_ref, values_ref, hidden_ref):
    count = hidden_ref.shape[1]
    for at, size in tiles_of(count):
        here, there = slice(at, at + size), slice(count + at, count + at + size)
        gate = dot(x_ref[...], w_ref[:, here])
        up = dot(x_ref[...], w_ref[:, there])
        values_ref[:, here] = gate
        values_ref[:, there] = up
        hidden_ref[:, here] = (gate * jax.nn.sigmoid(gate) * up).astype(bf16)


def feed_back_body(c_ref, d_ref, values_ref, slope_ref):
    count = d_ref.shape[0]
    for at, size in tiles_of(count):
        here, there = slice(at, at + size), slice(count + at, count + at + size)
        slope = dot(c_ref[...], d_ref[here, :], NT)
        gate, up = values_ref[:, here], values_ref[:, there]
        sigmoid = jax.nn.sigmoid(gate)
        silu = gate * sigmoid
        slope_ref[:, here] = (slope * up * sigmoid * (1.0 + gate * (1.0 - sigmoid))).astype(bf16)
        slope_ref[:, there] = (slope * silu).astype(bf16)


def feed(x, both, count):
    tokens, width = x.shape
    tile = min(tokens, 256)
    return pl.pallas_call(
        feed_body,
        grid=(tokens // tile,),
        out_shape=(
            jax.ShapeDtypeStruct((tokens, 2 * count), f32),
            jax.ShapeDtypeStruct((tokens, count), bf16),
        ),
        in_specs=[
            pl.BlockSpec((tile, width), lambda i: (i, 0)),
            pl.BlockSpec(both.shape, lambda i: (0, 0), pipeline_mode=pl.Buffered(1)),
        ],
        out_specs=(
            pl.BlockSpec((tile, 2 * count), lambda i: (i, 0)),
            pl.BlockSpec((tile, count), lambda i: (i, 0)),
        ),
        compiler_params=pltpu.CompilerParams(vmem_limit_bytes=40 * 1024 * 1024),
        cost_estimate=pl.CostEstimate(
            flops=4 * tokens * width * count,
            bytes_accessed=2 * (tokens * width + 2 * width * count + 5 * tokens * count),
            transcendentals=tokens * count,
        ),
        name="feed",
    )(x, both)


def feed_back(cotangent, down, values):
    tokens, width = cotangent.shape
    count = down.shape[0]
    tile = min(tokens, 256)
    return pl.pallas_call(
        feed_back_body,
        grid=(tokens // tile,),
        out_shape=jax.ShapeDtypeStruct((tokens, 2 * count), bf16),
        in_specs=[
            pl.BlockSpec((tile, width), lambda i: (i, 0)),
            pl.BlockSpec(down.shape, lambda i: (0, 0), pipeline_mode=pl.Buffered(1)),
            pl.BlockSpec((tile, 2 * count), lambda i: (i, 0)),
        ],
        out_specs=pl.BlockSpec((tile, 2 * count), lambda i: (i, 0)),
        compiler_params=pltpu.CompilerParams(vmem_limit_bytes=32 * 1024 * 1024),
        cost_estimate=pl.CostEstimate(
            flops=2 * tokens * width * count,
            bytes_accessed=2 * (tokens * width + width * count + 6 * tokens * count),
            transcendentals=tokens * count,
        ),
        name="feed_back",
    )(cotangent, down, values)


def on_device(
    tokens,
    positions,
    cotangent,
    query_weight,
    key_weight,
    value_weight,
    output_weight,
    gate_weight,
    up_weight,
    down_weight,
    first_gain,
    second_gain,
):
    token_count, width = tokens.shape
    group = lax.axis_size(GROUP)
    owners = lax.axis_size(PLANE)
    owner = lax.axis_index(PLANE)
    lane = owner % 2
    chip = owner // 2
    chips = owners // 2
    rows = token_count // group
    own_rows = query_weight.shape[0]
    hidden_part = gate_weight.shape[1] // chips
    down_rows = down_weight.shape[0]
    kv_width = key_weight.shape[1]
    line = lax.axis_size("seq")
    line_place = lax.axis_index("seq")
    direct = [r for r in range(1, chips) if r & (r - 1) == 0]
    indirect = [r for r in range(1, chips) if r & (r - 1)]

    digits = jnp.stack([positions // 256, positions % 256], axis=1).astype(bf16)
    moved = spread(jnp.concatenate([tokens, jnp.pad(digits, ((0, 0), (0, 126)))], axis=1))
    by_head = (own_rows, KV_HEADS, 1, HEAD_DIM)
    gains = jnp.pad(jnp.stack([first_gain, second_gain], axis=1), ((0, 0), (0, 126)))
    pair_own = jnp.concatenate([key_weight.reshape(by_head), value_weight.reshape(by_head)], 2)
    pair_own = jnp.concatenate([pair_own.reshape(own_rows, 2 * kv_width), gains], axis=1)
    pair_weight = gather_plane(pair_own)
    query_full = lax.all_gather(query_weight, PLANE, axis=0, tiled=True)
    output_full = lax.all_gather(output_weight, PLANE, axis=0, tiled=True)
    scales = pair_weight[:, 2 * kv_width : 2 * kv_width + 2].astype(f32).T
    first_scale, second_scale = scales[0:1], scales[1:2]

    def columns(r, first, count):
        start = (chip ^ r) * hidden_part
        parts = []
        for weight in (gate_weight, up_weight):
            some = lax.dynamic_slice_in_dim(weight, first, count, 0)
            parts.append(lax.dynamic_slice_in_dim(some, start, hidden_part, 1))
        return jnp.concatenate(parts, axis=1)

    blocks = [columns(r, 0, own_rows) for r in range(chips)]

    places = moved[:, width].astype(f32) * 256.0 + moved[:, width + 1].astype(f32)
    cosine, sine = angles_of(places)
    is_key = jnp.arange(2 * HEAD_DIM) < HEAD_DIM
    pair_cosine, pair_sine = jnp.where(is_key, cosine, 1.0), jnp.where(is_key, sine, 0.0)
    inputs = moved[:, :width].astype(f32)
    first_normed, first_inverse = normalize(inputs)
    first_input = (first_normed * first_scale).astype(bf16)
    paired = project(first_input, pair_weight, pair_cosine, pair_sine, 1.0, 2 * kv_width)

    line_pairs = [paired] + [swap(paired, m, "seq") for m in (1, 2, 3)]
    both_full = jnp.broadcast_to(moved[0, 0] * 0.0, (own_rows * owners, 2 * hidden_part))
    line_pairs[0], both_full = tie(line_pairs[0], both_full)
    pairs = [(piece, swap(piece, 2, "ctx")) for piece in line_pairs]
    all_pairs = gather_lanes(pairs).reshape(group, group, rows, -1)
    query_scale = HEAD_DIM**-0.5 * log2_e
    queries = project(first_input, query_full, cosine, sine, query_scale, width)

    queries, all_pairs, blocks, cotangent, down_weight = tie(
        queries, all_pairs, blocks, cotangent, down_weight
    )
    blocks = to_chips(blocks)
    slopes = spread(cotangent)
    down_other = swap(down_weight, 1)
    own_other = swap(blocks[0], 1)
    attended, raw_outputs, log_sums = attend_forward(queries, all_pairs, 0, KV_HEADS)
    attended, down_other, own_other = tie(attended, down_other, own_other)

    middle = inputs + dot(attended, output_full)
    second_normed, second_inverse = normalize(middle)
    second_input = (second_normed * second_scale).astype(bf16)
    second_input, slopes = tie(second_input, slopes)
    feed_input = ChipGather(second_input)
    feed_input.first()
    both_full = lax.dynamic_update_slice_in_dim(both_full, blocks[0], owner * own_rows, 0)
    both_full = lax.dynamic_update_slice_in_dim(both_full, own_other, (owner ^ 1) * own_rows, 0)
    down_full = jnp.where(
        lane == 0,
        jnp.concatenate([down_weight, down_other], axis=0),
        jnp.concatenate([down_other, down_weight], axis=0),
    )
    feed_input.ends, blocks, both_full, down_full, slopes = tie(
        feed_input.ends, blocks, both_full, down_full, slopes
    )
    feed_input.second()
    feed_slope = ChipGather(slopes)
    feed_slope.first()
    for r in range(1, chips):
        other = swap(blocks[r], 1)
        both_full = lax.dynamic_update_slice_in_dim(
            both_full, blocks[r], (owner ^ (2 * r)) * own_rows, 0
        )
        both_full = lax.dynamic_update_slice_in_dim(
            both_full, other, (owner ^ (2 * r + 1)) * own_rows, 0
        )
    feed_slope.ends, feed_input.rest, both_full = tie(
        feed_slope.ends, feed_input.rest, both_full
    )
    feed_slope.second()
    feed_input = feed_input.result()

    if hidden_part % 128:
        gate_values = dot(feed_input, both_full[:, :hidden_part])
        up_values = dot(feed_input, both_full[:, hidden_part:])
        gate_sigmoid = jax.nn.sigmoid(gate_values)
        hidden = (gate_values * gate_sigmoid * up_values).astype(bf16)
    else:
        feed_values, hidden = feed(feed_input, both_full, hidden_part)
    hidden, feed_slope.rest = tie(hidden, feed_slope.rest)
    feed_slope = feed_slope.result()
    if hidden_part % 128:
        hidden_slope = dot(feed_slope, down_full, NT)
        gate_slope = (
            hidden_slope * up_values * gate_sigmoid * (1.0 + gate_values * (1.0 - gate_sigmoid))
        ).astype(bf16)
        up_slope = (hidden_slope * gate_values * gate_sigmoid).astype(bf16)
        both_slope = jnp.concatenate([gate_slope, up_slope], axis=1)
    else:
        both_slope = feed_back(feed_slope, down_full, feed_values)

    def by_chip(share):
        return [share[r * token_count : (r + 1) * token_count] for r in range(chips)]

    def for_chips(features):
        count = 2 * own_rows
        return [
            lax.dynamic_slice_in_dim(features, (chip ^ r) * count, count, 1) for r in range(chips)
        ]

    def swap_rows(share):
        count = share.shape[0] // 2
        kept = lax.dynamic_slice_in_dim(share, lane * count, count, 0)
        return kept, swap(lax.dynamic_slice_in_dim(share, (1 - lane) * count, count, 0), 1)

    feed_share = dot(both_slope, both_full, NT).astype(bf16)
    feed_share, both_slope, hidden = tie(feed_share, both_slope, hidden)
    second_slope = ChipSum(by_chip(feed_share))
    second_slope.first()
    down_share = dot(hidden, feed_slope, TN).astype(bf16)
    second_slope.came, down_share, both_slope = tie(second_slope.came, down_share, both_slope)
    second_slope.second()
    down_two = swap_rows(down_share)
    down_two, both_slope = tie(down_two, both_slope)
    down_part = lax.psum_scatter(add(*down_two), "seq", scatter_dimension=0, tiled=True)
    both_lanes = LaneSum(dot(feed_input, both_slope, TN).astype(bf16))
    both_stack = jnp.stack(both_lanes.blocks())
    second_slope.ends, both_stack = tie(second_slope.ends, both_stack)
    both_part = lax.psum_scatter(both_stack, "seq", scatter_dimension=1, tiled=True)
    second_slope = second_slope.result()
    second_gain_share = jnp.sum(second_slope * second_normed, axis=0)
    middle_slope = slopes.astype(f32) + norm_backward(
        second_slope * second_scale, second_normed, second_inverse
    )
    attention_slope = middle_slope.astype(bf16)
    attended_slope = dot(attention_slope, output_full, NT).astype(bf16)
    payload = [
        jnp.concatenate([attention_slope, *both], axis=1)
        for both in zip(for_chips(attended), for_chips(first_input))
    ]

    attended_slope, payload = tie(attended_slope, payload)
    payload = to_chips(payload)
    query_turned, pair_terms = attend_backward(
        queries, attended_slope, all_pairs, raw_outputs, log_sums, 0, group // 2
    )
    query_turned, pair_terms, payload, down_part = tie(
        query_turned, pair_terms, payload, down_part
    )

    pair_slope = GroupSum(pair_terms.reshape(token_count * group, -1))
    down_sum = lax.all_gather(down_part, "seq", axis=0, tiled=True)
    query_slope = turn_back(query_turned, cosine, sine)
    pair_slope.came, query_slope, payload = tie(pair_slope.came, query_slope, payload)
    pair_slope.along_x()
    payload = jnp.concatenate(payload)
    output_share = dot(payload[:, width : width + 2 * own_rows], payload[:, :width], TN)
    first_columns = payload[:, width + 2 * own_rows :]
    query_side = dot(query_slope, query_full, NT)
    pair_slope.came, output_share, query_side, query_slope, both_part, hidden = tie(
        pair_slope.came, output_share.astype(bf16), query_side, query_slope, both_part, hidden
    )
    pair_slope.along_seq()
    both_part = to_chips([both_part[r] for r in range(chips)])
    query_chunks = to_chips([query_slope] * chips)
    output_own = add(*swap_rows(output_share))
    out_share = dot(hidden, down_full).astype(bf16)
    pair_slope.came, both_part, output_own, out_share = tie(
        pair_slope.came, both_part, output_own, out_share
    )
    both_sums = lax.all_gather(jnp.stack(both_part), "seq", axis=1, tiled=True)
    kv_slope = turn_back(pair_slope.result().astype(bf16), pair_cosine, pair_sine)
    first_slope = query_side + dot(kv_slope, pair_weight[:, : 2 * kv_width], NT)
    input_gradient = middle_slope + norm_backward(
        first_slope * first_scale, first_normed, first_inverse
    )
    gain_shares = jnp.stack([jnp.sum(first_slope * first_normed, axis=0), second_gain_share])
    input_gradient, kv_slope, gain_shares, query_chunks = tie(
        input_gradient.astype(bf16), kv_slope, gain_shares.astype(bf16), query_chunks
    )
    kv_chunks = to_chips([kv_slope] * chips)
    gain_parts = to_chips(for_chips(gain_shares))
    query_share = dot(first_columns, jnp.concatenate(query_chunks), TN).astype(bf16)
    query_own = add(*swap_rows(query_share))
    query_own, kv_chunks, gain_parts, out_share, down_sum = tie(
        query_own, kv_chunks, gain_parts, out_share, down_sum
    )
    out_parts = to_chips(by_chip(out_share))
    kv_share = dot(first_columns, jnp.concatenate(kv_chunks), TN).astype(bf16)
    gain_two = swap_rows(add_all(gain_parts).T.astype(bf16))
    last = jnp.concatenate(
        [
            query_own,
            output_own,
            add(*swap_rows(kv_share)),
            jnp.pad(add(*gain_two), ((0, 0), (0, 126))),
        ],
        axis=1,
    )
    last, input_gradient, both_sums, down_sum = tie(last, input_gradient, both_sums, down_sum)
    lasts = [LineTree(last[half]) for half in halves(own_rows)[:1]]
    input_gradient = spread(input_gradient)
    gate_gradient, up_gradient = place_columns(both_sums, chip)
    lasts[0].moving, gate_gradient, last = tie(lasts[0].moving, gate_gradient, last)
    lasts[0].across()
    lasts.append(LineTree(last[halves(own_rows)[1]]))
    layer_output = (middle + add_all(out_parts)).astype(bf16)
    lasts[0].moving, lasts[1].moving, layer_output = tie(
        lasts[0].moving, lasts[1].moving, layer_output
    )
    lasts[0].outwards()
    lasts[1].across()
    layer_output = spread(layer_output)
    lasts[1].moving, input_gradient = tie(lasts[1].moving, input_gradient)
    lasts[1].outwards()
    down_gradient = down_sum.astype(f32)
    input_gradient = input_gradient.astype(f32)
    lasts[0].moving, lasts[1].moving, layer_output, down_gradient, input_gradient = tie(
        lasts[0].moving, lasts[1].moving, layer_output, down_gradient, input_gradient
    )

    last = jnp.concatenate([part.result() for part in lasts])
    query_gradient = last[:, :width]
    output_gradient = last[:, width : 2 * width]
    pairs = last[:, 2 * width :]
    gain_gradients = pairs[:, 2 * kv_width : 2 * kv_width + 2].T
    pairs = pairs[:, : 2 * kv_width].reshape(own_rows, KV_HEADS, 2, HEAD_DIM)
    return (
        layer_output,
        input_gradient,
        query_gradient,
        pairs[:, :, 0].reshape(own_rows, kv_width),
        pairs[:, :, 1].reshape(own_rows, kv_width),
        output_gradient,
        gate_gradient,
        up_gradient,
        down_gradient,
        gain_gradients[0],
        gain_gradients[1],
    )


def solution(mesh):
    tokens = P(("dp", "seq", "ctx"), None)
    rows = P(PLANE, None)
    return jax.shard_map(
        on_device,
        mesh=mesh,
        in_specs=(tokens, P(("dp", "seq", "ctx")), tokens) + (rows,) * 7 + (P(PLANE),) * 2,
        out_specs=(tokens,) * 2 + (rows,) * 7 + (P(PLANE),) * 2,
        check_vma=False,
    )
```

```python
from functools import partial

import jax
import jax.numpy as jnp
from jax import lax
from jax.experimental import pallas as pl
from jax.experimental.pallas import tpu as pltpu
from jax.sharding import PartitionSpec as P

HEADS = 32
KV_HEADS = 4
HEAD_DIM = 64
BLOCK = 256

epsilon = 1e-05
rotary_base = 10000.0
log2_e = 1.4426950408889634
ln_2 = 0.6931471805599453
bf16, f32 = jnp.bfloat16, jnp.float32
PLANE = ("dp", "ctx")
GROUP = ("seq", "ctx")
NT = (((1,), (1,)), ((), ()))
NN = (((1,), (0,)), ((), ()))
TN = (((0,), (0,)), ((), ()))


def dot(left, right, dims=NN):
    return lax.dot_general(left, right, dims, preferred_element_type=f32)


def normalize(features):
    inverse_rms = lax.rsqrt(jnp.mean(features * features, axis=-1, keepdims=True) + epsilon)
    return (features * inverse_rms, inverse_rms)


def norm_backward(slopes, normed, inverse_rms):
    return inverse_rms * (slopes - normed * jnp.mean(slopes * normed, axis=-1, keepdims=True))


def angles_of(places):
    lane = jnp.arange(2 * HEAD_DIM)
    exponent = (lane % (HEAD_DIM // 2)).astype(f32) * (2.0 / HEAD_DIM)
    frequency = rotary_base ** (-exponent)
    angles = places[:, None] * frequency[None, :]
    sign = jnp.where(lane % HEAD_DIM < HEAD_DIM // 2, -1.0, 1.0)
    return jnp.cos(angles), jnp.sin(angles) * sign


def tie(*values):
    return lax.optimization_barrier(values)


def swap(values, mask, axes=PLANE):
    count = lax.axis_size(axes)
    return lax.ppermute(values, axes, [(i, i ^ mask) for i in range(count)])


def halves(count):
    return (slice(0, count // 2), slice(count // 2, count))


class ChipGather:
    def __init__(self, own):
        self.own = own

    def first(self):
        self.ends = {}
        r = 1
        while r < lax.axis_size(PLANE) // 2:
            self.ends[r] = swap(self.own, r << 1)
            r *= 2

    def second(self):
        top, bottom = halves(self.own.shape[0])
        parts = {r: (values[top], values[bottom]) for r, values in self.ends.items()}
        for r in range(1, lax.axis_size(PLANE) // 2):
            low, high = r & -r, 1 << (r.bit_length() - 1)
            if low != high:
                first = swap(parts[r ^ low][0], low << 1)
                parts[r] = (first, swap(parts[r ^ high][1], high << 1))
        self.rest = {r: both for r, both in parts.items() if r not in self.ends}

    def chunks(self):
        half = self.own.shape[0] // 2
        chunks = [(0, 0, self.own)]
        for r in range(1, lax.axis_size(PLANE) // 2):
            if r in self.ends:
                chunks.append((r, 0, self.ends[r]))
            else:
                chunks += [(r, 0, self.rest[r][0]), (r, half, self.rest[r][1])]
        return chunks

    def result(self):
        return jnp.concatenate([values for _, _, values in self.chunks()], axis=0)


def add(left, right):
    return (left.astype(f32) + right.astype(f32)).astype(bf16)


class ChipSum:
    def __init__(self, blocks):
        self.parts = [[block[half] for half in halves(block.shape[0])] for block in blocks]

    def first(self):
        chips = len(self.parts)
        self.came = {}
        for r in sorted(range(1, chips), key=lambda r: -bin(r).count("1")):
            low, high = r & -r, 1 << (r.bit_length() - 1)
            if low == high:
                continue
            if bin(r).count("1") < bin(chips - 1).count("1"):
                self.settle(r)
            self.came[r ^ low, 0, r] = swap(self.parts[r][0], low << 1)
            self.came[r ^ high, 1, r] = swap(self.parts[r][1], high << 1)

    def settle(self, only=None):
        for key in sorted(self.came):
            if only is None or key[0] == only:
                self.parts[key[0]][key[1]] = add(self.parts[key[0]][key[1]], self.came.pop(key))

    def second(self):
        self.settle()
        self.ends = []
        r = 1
        while r < len(self.parts):
            self.ends.append(swap(jnp.concatenate(self.parts[r], axis=0), r << 1))
            r *= 2

    def result(self):
        return add_all([jnp.concatenate(self.parts[0], axis=0)] + self.ends)


def to_chips(blocks):
    return [block if r == 0 else swap(block, r << 1) for r, block in enumerate(blocks)]


def add_all(values):
    total = values[0].astype(f32)
    for other in values[1:]:
        total = total + other.astype(f32)
    return total


def gather_plane(own):
    rows = own.shape[0]
    owner = lax.axis_index(PLANE)
    full = jnp.zeros((rows * lax.axis_size(PLANE), own.shape[1]), own.dtype)
    gather = ChipGather(own)
    gather.first()
    gather.second()
    for r, first, chunk in gather.chunks():
        other = swap(chunk, 1)
        full = lax.dynamic_update_slice_in_dim(full, chunk, (owner ^ (2 * r)) * rows + first, 0)
        full = lax.dynamic_update_slice_in_dim(full, other, (owner ^ (2 * r + 1)) * rows + first, 0)
    return full


class LaneSum:
    def __init__(self, values):
        owners = lax.axis_size(PLANE)
        owner = lax.axis_index(PLANE)
        rows = values.shape[0] // owners
        self.kept, self.came = [], []
        for r in range(owners // 2):
            away = lax.dynamic_slice_in_dim(values, (owner ^ (2 * r + 1)) * rows, rows, 0)
            self.kept.append(lax.dynamic_slice_in_dim(values, (owner ^ (2 * r)) * rows, rows, 0))
            self.came.append(swap(away, 1))

    def blocks(self):
        return [add(kept, came) for kept, came in zip(self.kept, self.came)]


class LineTree:
    def __init__(self, share):
        self.share = share
        self.moving = lax.ppermute(share, "seq", [(0, 1), (3, 2)])

    def across(self):
        self.share = add(self.share, self.moving)
        self.moving = lax.ppermute(self.share, "seq", [(1, 2), (2, 1)])

    def outwards(self):
        self.share = add(self.share, self.moving)
        self.moving = lax.ppermute(self.share, "seq", [(1, 0), (2, 3)])

    def result(self):
        place = lax.axis_index("seq")
        inner = (place == 1) | (place == 2)
        return jnp.where(inner, self.share, self.moving).astype(f32)


class LineSum:
    def __init__(self, share):
        self.share = share

    def scatter(self):
        place = lax.axis_index("seq")
        count = lax.axis_size("seq")
        rows = self.share.shape[0] // count

        def part(m):
            return lax.dynamic_slice_in_dim(self.share, (place ^ m) * rows, rows, 0)

        self.parts = [part(0)] + [swap(part(m), m, "seq") for m in range(1, count)]

    def gather(self):
        total = add_all(self.parts).astype(bf16)
        self.parts = [total] + [swap(total, m, "seq") for m in range(1, len(self.parts))]

    def result(self):
        place = lax.axis_index("seq")
        rows = self.parts[0].shape[0]
        out = self.share
        for m, values in enumerate(self.parts):
            out = lax.dynamic_update_slice_in_dim(out, values, (place ^ m) * rows, 0)
        return out


def gather_lanes(pairs):
    pairs = [jnp.concatenate(pair, axis=0) for pair in pairs]
    others = [swap(pair, 1, "ctx") for pair in pairs]
    return jnp.concatenate([half for both in zip(pairs, others) for half in both], axis=0)


class GroupSum:
    def __init__(self, values):
        shaped = values.reshape(4, 2, 2, -1, values.shape[1])
        self.kept, self.came = shaped[:, 0], swap(shaped[:, 1], 1, "ctx")

    def along_x(self):
        pair = add(self.kept, self.came)
        self.kept, self.came = pair[:, 0], swap(pair[:, 1], 2, "ctx")

    def along_seq(self):
        line = add(self.kept, self.came)
        self.kept, self.came = line[0], [swap(line[m], m, "seq") for m in (1, 2, 3)]

    def result(self):
        total = self.kept.astype(f32)
        for values in self.came:
            total = total + values.astype(f32)
        return total


def spread(rows):
    count = lax.axis_size(GROUP)
    shaped = rows.reshape(count, -1, rows.shape[1])
    return lax.all_to_all(shaped, GROUP, 0, 0, tiled=True).reshape(rows.shape)


def place_body(at_ref, values_ref, gate_ref, up_ref):
    count = gate_ref.shape[1]
    gate_ref[...] = values_ref[0, :, :count].astype(f32)
    up_ref[...] = values_ref[0, :, count:].astype(f32)


def place_columns(values, at):
    chips, rows, both = values.shape
    count = both // 2
    if count % 128:
        gate = jnp.zeros((rows, chips * count), f32)
        up = jnp.zeros((rows, chips * count), f32)
        for r in range(chips):
            block, start = values[r].astype(f32), (at ^ r) * count
            gate = lax.dynamic_update_slice_in_dim(gate, block[:, :count], start, 1)
            up = lax.dynamic_update_slice_in_dim(up, block[:, count:], start, 1)
        return gate, up
    shape = jax.ShapeDtypeStruct((rows, chips * count), f32)
    return pl.pallas_call(
        place_body,
        grid_spec=pltpu.PrefetchScalarGridSpec(
            num_scalar_prefetch=1,
            grid=(chips,),
            in_specs=[pl.BlockSpec((1, rows, both), lambda t, at_ref: (at_ref[0] ^ t, 0, 0))],
            out_specs=[pl.BlockSpec((rows, count), lambda t, at_ref: (0, t))] * 2,
        ),
        out_shape=(shape, shape),
        cost_estimate=pl.CostEstimate(
            flops=0, bytes_accessed=10 * chips * rows * both // 2, transcendentals=0
        ),
        compiler_params=pltpu.CompilerParams(vmem_limit_bytes=24 * 1024 * 1024),
        name="place_columns",
    )(at.astype(jnp.int32)[None], values)


class LineGather:
    def __init__(self, own):
        self.own, self.right, self.left = own, [], []

    def step(self):
        at = len(self.right)
        count = lax.axis_size("seq")
        right = self.right[-1] if at else self.own
        left = self.left[-1] if at else self.own
        pairs = [(i, i + 1) for i in range(at, count - 1)]
        self.right.append(lax.ppermute(right, "seq", pairs))
        back = [(i, i - 1) for i in range(count - 1 - at, 0, -1)]
        self.left.append(lax.ppermute(left, "seq", back))

    def result(self):
        count = lax.axis_size("seq")
        rows = self.own.shape[0]
        around = jnp.concatenate([*self.right[::-1], self.own, *self.left], axis=0)
        start = (count - 1 - lax.axis_index("seq")) * rows
        return lax.dynamic_slice_in_dim(around, start, count * rows, 0)


def stack_heads(block, heads, rows, first):
    return jnp.concatenate(
        [
            block[b * rows : (b + 1) * rows, (first + h) * HEAD_DIM : (first + h + 1) * HEAD_DIM]
            for b in range(2)
            for h in range(heads)
        ],
        axis=0,
    )


def spread_heads(stacked, heads, rows, b):
    return jnp.concatenate(
        [stacked[(b * heads + h) * rows : (b * heads + h + 1) * rows] for h in range(heads)], axis=1
    )


def forward_body(
    q_ref, kv_ref, o_ref, ot_ref, lse_ref, kvt, qs, m_s, l_s, *, groups, heads, rows, blocks
):
    c = pl.program_id(0)
    keys = kv_ref.shape[0] * rows
    width = 2 * heads * rows
    half = heads * rows

    @pl.when(c == 0)
    def _():
        def one(kt, carry):
            for g in range(groups):
                tile = kv_ref[:, kt, :, g * 128 : (g + 1) * 128].reshape(keys, 128)
                kvt[g, kt] = tile.astype(f32).T.astype(bf16)[HEAD_DIM:]
            return carry

        lax.fori_loop(0, blocks, one, 0)

    for g in range(groups):
        q = stack_heads(q_ref[...], heads, rows, g * heads)
        qs[g] = jnp.concatenate([q, jnp.zeros((width, HEAD_DIM), bf16)], axis=1)

    def tiles(kts, lo, first):
        scores = []
        for g in range(groups):
            for kt in kts:
                kv = kv_ref[:, kt, :, g * 128 : (g + 1) * 128].reshape(keys, 128)
                scores.append(dot(kv, qs[g, lo:], NT))
        for g in range(groups):
            sts = scores[g * len(kts) : (g + 1) * len(kts)]
            peak = jnp.max(sts[0], axis=0, keepdims=True)
            for st in sts[1:]:
                peak = jnp.maximum(peak, jnp.max(st, axis=0, keepdims=True))
            if not first:
                m_old = m_s[g, :, lo:]
                peak = jnp.maximum(m_old, peak)
            total, pv = 0.0, 0.0
            for kt, st in zip(kts, sts):
                p = jnp.exp2(st - peak)
                total = total + jnp.sum(p, axis=0, keepdims=True)
                pv = pv + dot(kvt[g, kt], p.astype(bf16))
            if first:
                l_s[g, :, lo:] = total
                ot_ref[0, g, :, lo:] = pv
            else:
                shrink = jnp.exp2(m_old - peak)
                l_s[g, :, lo:] = l_s[g, :, lo:] * shrink + total
                ot_ref[0, g, :, lo:] = ot_ref[0, g, :, lo:] * shrink + pv
            m_s[g, :, lo:] = peak

    def step(i, carry):
        tiles((2 * i + 1, 2 * i + 2), 0, False)
        return carry

    tiles((0,), 0, True)
    lax.fori_loop(0, c, step, 0)
    tiles((2 * c + 1,), half, False)
    for g in range(groups):
        total = l_s[g]
        o = ot_ref[0, g] / total
        ot_ref[0, g] = o
        lse_ref[0, g : g + 1, :] = m_s[g] + jnp.log2(total)
        stacked = o.T.astype(bf16)
        for b in range(2):
            o_ref[b * rows : (b + 1) * rows, g * heads * HEAD_DIM : (g + 1) * heads * HEAD_DIM] = (
                spread_heads(stacked, heads, rows, b)
            )


def attend_forward(q, kv, first, groups):
    devices, blocks, rows, kv_width = kv.shape
    heads = q.shape[1] * 128 // HEAD_DIM // kv_width
    wide = heads * HEAD_DIM * groups
    width = 2 * heads * rows
    pairs = blocks // 2
    keys = devices * rows
    tiles = groups * blocks * (blocks + 1) // 2
    at = first // groups
    return pl.pallas_call(
        partial(forward_body, groups=groups, heads=heads, rows=rows, blocks=blocks),
        grid=(pairs,),
        out_shape=(
            jax.ShapeDtypeStruct((q.shape[0], wide), bf16),
            jax.ShapeDtypeStruct((pairs, groups, HEAD_DIM, width), f32),
            jax.ShapeDtypeStruct((pairs, groups, width), f32),
        ),
        in_specs=[
            pl.BlockSpec((2 * rows, wide), lambda c: (c, at)),
            pl.BlockSpec((devices, blocks, rows, groups * 128), lambda c: (0, 0, 0, at)),
        ],
        out_specs=(
            pl.BlockSpec((2 * rows, wide), lambda c: (c, 0)),
            pl.BlockSpec((1, groups, HEAD_DIM, width), lambda c: (c, 0, 0, 0)),
            pl.BlockSpec((1, groups, width), lambda c: (c, 0, 0)),
        ),
        scratch_shapes=[
            pltpu.VMEM((groups, blocks, HEAD_DIM, keys), bf16),
            pltpu.VMEM((groups, width, 128), bf16),
            pltpu.VMEM((groups, 1, width), f32),
            pltpu.VMEM((groups, 1, width), f32),
        ],
        compiler_params=pltpu.CompilerParams(vmem_limit_bytes=40 * 1024 * 1024),
        cost_estimate=pl.CostEstimate(
            flops=tiles * keys * width * 128 * 8,
            bytes_accessed=6 * 1024 * 1024,
            transcendentals=tiles * keys * width // 2,
        ),
        name="attend_forward",
    )(q, kv)


def backward_body(
    q_ref,
    do_ref,
    kv_ref,
    ot_ref,
    lse_ref,
    dq_ref,
    dkv_ref,
    kt_s,
    qs,
    dos,
    d_s,
    dqt,
    acc,
    *,
    groups,
    heads,
    rows,
    blocks,
    start,
):
    c = pl.program_id(0) + start
    devices = kv_ref.shape[0]
    keys = devices * rows
    width = 2 * heads * rows
    half = heads * rows

    @pl.when(c == start)
    def _():
        def one(kt, carry):
            for g in range(groups):
                tile = kv_ref[:, kt, :, g * 128 : (g + 1) * 128].reshape(keys, 128)
                kt_s[g, kt] = tile.astype(f32).T.astype(bf16)[:HEAD_DIM]
                acc[g, kt] = jnp.zeros((keys, 128), f32)
            return carry

        lax.fori_loop(0, blocks, one, 0)

    zero = jnp.zeros((width, HEAD_DIM), bf16)
    for g in range(groups):
        q = stack_heads(q_ref[...], heads, rows, g * heads)
        do = stack_heads(do_ref[...], heads, rows, g * heads)
        qs[g] = jnp.concatenate([q, zero], axis=1)
        dos[g] = jnp.concatenate([zero, do], axis=1)
        d_s[g] = jnp.sum(do.astype(f32).T * ot_ref[0, g], axis=0, keepdims=True)
        dqt[g] = jnp.zeros((HEAD_DIM, width), f32)

    def tiles(kt, lo):
        kvs = [
            kv_ref[:, kt, :, g * 128 : (g + 1) * 128].reshape(keys, 128) for g in range(groups)
        ]
        sts = [dot(kvs[g], qs[g, lo:], NT) for g in range(groups)]
        dpts = [dot(kvs[g], dos[g, lo:], NT) for g in range(groups)]
        ps = [jnp.exp2(sts[g] - lse_ref[0, g : g + 1, lo:]) for g in range(groups)]
        dss = [(ps[g] * (dpts[g] - d_s[g, :, lo:])).astype(bf16) for g in range(groups)]
        for g in range(groups):
            dqt[g, :, lo:] += dot(kt_s[g, kt], dss[g])
        for g in range(groups):
            acc[g, kt] += dot(dss[g], qs[g, lo:]) + dot(ps[g].astype(bf16), dos[g, lo:])

    def step(kt, carry):
        tiles(kt, 0)
        return carry

    lax.fori_loop(0, 2 * c + 1, step, 0)
    tiles(2 * c + 1, half)
    for g in range(groups):
        dq = (dqt[g] * (HEAD_DIM**-0.5)).T.astype(bf16)
        for b in range(2):
            dq_ref[b * rows : (b + 1) * rows, g * heads * HEAD_DIM : (g + 1) * heads * HEAD_DIM] = (
                spread_heads(dq, heads, rows, b)
            )

    @pl.when(c == start + pl.num_programs(0) - 1)
    def _():
        column = lax.broadcasted_iota(jnp.int32, (1, 128), 1)
        factor = jnp.where(column < HEAD_DIM, ln_2, 1.0)

        def one(kt, carry):
            for g in range(groups):
                dkv_ref[:, kt, :, g * 128 : (g + 1) * 128] = (
                    (acc[g, kt] * factor).astype(bf16).reshape(devices, rows, 128)
                )
            return carry

        lax.fori_loop(0, blocks, one, 0)


def attend_backward(q, do, kv, ot, lse, start, count):
    groups = KV_HEADS
    devices, blocks, rows, kv_width = kv.shape
    heads = q.shape[1] * 128 // HEAD_DIM // kv_width
    wide = heads * HEAD_DIM * groups
    width = 2 * heads * rows
    keys = devices * rows
    tiles = groups * sum(4 * c + 3 for c in range(start, start + count))
    kv_shape = (devices, blocks, rows, groups * 128)
    return pl.pallas_call(
        partial(backward_body, groups=groups, heads=heads, rows=rows, blocks=blocks, start=start),
        grid=(count,),
        out_shape=(
            jax.ShapeDtypeStruct((2 * rows * count, wide), bf16),
            jax.ShapeDtypeStruct(kv_shape, bf16),
        ),
        in_specs=[
            pl.BlockSpec((2 * rows, wide), lambda c: (c + start, 0)),
            pl.BlockSpec((2 * rows, wide), lambda c: (c + start, 0)),
            pl.BlockSpec(kv_shape, lambda c: (0, 0, 0, 0)),
            pl.BlockSpec((1, groups, HEAD_DIM, width), lambda c: (c + start, 0, 0, 0)),
            pl.BlockSpec((1, groups, width), lambda c: (c + start, 0, 0)),
        ],
        out_specs=(
            pl.BlockSpec((2 * rows, wide), lambda c: (c, 0)),
            pl.BlockSpec(kv_shape, lambda c: (0, 0, 0, 0)),
        ),
        scratch_shapes=[
            pltpu.VMEM((groups, blocks, HEAD_DIM, keys), bf16),
            pltpu.VMEM((groups, width, 128), bf16),
            pltpu.VMEM((groups, width, 128), bf16),
            pltpu.VMEM((groups, 1, width), f32),
            pltpu.VMEM((groups, HEAD_DIM, width), f32),
            pltpu.VMEM((groups, blocks, keys, 128), f32),
        ],
        compiler_params=pltpu.CompilerParams(vmem_limit_bytes=40 * 1024 * 1024),
        cost_estimate=pl.CostEstimate(
            flops=tiles * keys * width * 8,
            bytes_accessed=8 * 1024 * 1024,
            transcendentals=0,
        ),
        name="attend_backward",
    )(q, do, kv, ot, lse)


def turn_lanes(values, cosine, sine):
    count, width = values.shape
    lane = lax.broadcasted_iota(jnp.int32, (count, width), 1) % HEAD_DIM
    half_width = HEAD_DIM // 2
    other = jnp.where(
        lane < half_width,
        pltpu.roll(values, width - half_width, 1),
        pltpu.roll(values, half_width, 1),
    )
    times = width // cosine.shape[1]
    return values * jnp.tile(cosine, (1, times)) + other * jnp.tile(sine, (1, times))


def project_body(x_ref, w_ref, cosine_ref, sine_ref, out_ref, *, scale):
    values = dot(x_ref[...], w_ref[...])
    out_ref[...] = (turn_lanes(values, cosine_ref[...], sine_ref[...]) * scale).astype(bf16)


def project(x, weight, cosine, sine, scale, width):
    count, depth = x.shape
    tile = min(width, 512)
    return pl.pallas_call(
        partial(project_body, scale=scale),
        grid=(width // tile,),
        out_shape=jax.ShapeDtypeStruct((count, width), bf16),
        in_specs=[
            pl.BlockSpec((count, depth), lambda i: (0, 0)),
            pl.BlockSpec((depth, tile), lambda i: (0, i)),
            pl.BlockSpec(cosine.shape, lambda i: (0, 0)),
            pl.BlockSpec(sine.shape, lambda i: (0, 0)),
        ],
        out_specs=pl.BlockSpec((count, tile), lambda i: (0, i)),
        compiler_params=pltpu.CompilerParams(vmem_limit_bytes=24 * 1024 * 1024),
        cost_estimate=pl.CostEstimate(
            flops=2 * count * depth * width,
            bytes_accessed=2 * (count * depth + depth * width + count * width),
            transcendentals=0,
        ),
        name="project",
    )(x, weight, cosine, sine)


def turn_body(x_ref, cosine_ref, sine_ref, out_ref):
    values = x_ref[...].astype(f32)
    out_ref[...] = turn_lanes(values, cosine_ref[...], sine_ref[...]).astype(bf16)


def turn_back(x, cosine, sine):
    count, width = x.shape
    tile = min(width, 512)
    return pl.pallas_call(
        turn_body,
        grid=(width // tile,),
        out_shape=jax.ShapeDtypeStruct(x.shape, bf16),
        in_specs=[
            pl.BlockSpec((count, tile), lambda i: (0, i)),
            pl.BlockSpec(cosine.shape, lambda i: (0, 0)),
            pl.BlockSpec(sine.shape, lambda i: (0, 0)),
        ],
        out_specs=pl.BlockSpec((count, tile), lambda i: (0, i)),
        cost_estimate=pl.CostEstimate(
            flops=6 * count * width, bytes_accessed=4 * count * width, transcendentals=0
        ),
        name="turn_back",
    )(x, cosine, -sine)


def tiles_of(count):
    return [(at, min(256, count - at)) for at in range(0, count, 256)]


def feed_body(x_ref, w_ref, values_ref, hidden_ref):
    count = hidden_ref.shape[1]
    for at, size in tiles_of(count):
        here, there = slice(at, at + size), slice(count + at, count + at + size)
        gate = dot(x_ref[...], w_ref[:, here])
        up = dot(x_ref[...], w_ref[:, there])
        values_ref[:, here] = gate
        values_ref[:, there] = up
        hidden_ref[:, here] = (gate * jax.nn.sigmoid(gate) * up).astype(bf16)


def feed_back_body(c_ref, d_ref, values_ref, slope_ref):
    count = d_ref.shape[0]
    for at, size in tiles_of(count):
        here, there = slice(at, at + size), slice(count + at, count + at + size)
        slope = dot(c_ref[...], d_ref[here, :], NT)
        gate, up = values_ref[:, here], values_ref[:, there]
        sigmoid = jax.nn.sigmoid(gate)
        silu = gate * sigmoid
        slope_ref[:, here] = (slope * up * sigmoid * (1.0 + gate * (1.0 - sigmoid))).astype(bf16)
        slope_ref[:, there] = (slope * silu).astype(bf16)


def feed(x, both, count):
    tokens, width = x.shape
    tile = min(tokens, 256)
    return pl.pallas_call(
        feed_body,
        grid=(tokens // tile,),
        out_shape=(
            jax.ShapeDtypeStruct((tokens, 2 * count), f32),
            jax.ShapeDtypeStruct((tokens, count), bf16),
        ),
        in_specs=[
            pl.BlockSpec((tile, width), lambda i: (i, 0)),
            pl.BlockSpec(both.shape, lambda i: (0, 0), pipeline_mode=pl.Buffered(1)),
        ],
        out_specs=(
            pl.BlockSpec((tile, 2 * count), lambda i: (i, 0)),
            pl.BlockSpec((tile, count), lambda i: (i, 0)),
        ),
        compiler_params=pltpu.CompilerParams(vmem_limit_bytes=40 * 1024 * 1024),
        cost_estimate=pl.CostEstimate(
            flops=4 * tokens * width * count,
            bytes_accessed=2 * (tokens * width + 2 * width * count + 5 * tokens * count),
            transcendentals=tokens * count,
        ),
        name="feed",
    )(x, both)


def feed_back(cotangent, down, values):
    tokens, width = cotangent.shape
    count = down.shape[0]
    tile = min(tokens, 256)
    return pl.pallas_call(
        feed_back_body,
        grid=(tokens // tile,),
        out_shape=jax.ShapeDtypeStruct((tokens, 2 * count), bf16),
        in_specs=[
            pl.BlockSpec((tile, width), lambda i: (i, 0)),
            pl.BlockSpec(down.shape, lambda i: (0, 0), pipeline_mode=pl.Buffered(1)),
            pl.BlockSpec((tile, 2 * count), lambda i: (i, 0)),
        ],
        out_specs=pl.BlockSpec((tile, 2 * count), lambda i: (i, 0)),
        compiler_params=pltpu.CompilerParams(vmem_limit_bytes=32 * 1024 * 1024),
        cost_estimate=pl.CostEstimate(
            flops=2 * tokens * width * count,
            bytes_accessed=2 * (tokens * width + width * count + 6 * tokens * count),
            transcendentals=tokens * count,
        ),
        name="feed_back",
    )(cotangent, down, values)


def on_device(
    tokens,
    positions,
    cotangent,
    query_weight,
    key_weight,
    value_weight,
    output_weight,
    gate_weight,
    up_weight,
    down_weight,
    first_gain,
    second_gain,
):
    token_count, width = tokens.shape
    group = lax.axis_size(GROUP)
    owners = lax.axis_size(PLANE)
    owner = lax.axis_index(PLANE)
    lane = owner % 2
    chip = owner // 2
    chips = owners // 2
    rows = token_count // group
    own_rows = query_weight.shape[0]
    hidden_part = gate_weight.shape[1] // chips
    down_rows = down_weight.shape[0]
    kv_width = key_weight.shape[1]
    line = lax.axis_size("seq")
    line_place = lax.axis_index("seq")
    direct = [r for r in range(1, chips) if r & (r - 1) == 0]
    indirect = [r for r in range(1, chips) if r & (r - 1)]

    digits = jnp.stack([positions // 256, positions % 256], axis=1).astype(bf16)
    moved = spread(jnp.concatenate([tokens, jnp.pad(digits, ((0, 0), (0, 126)))], axis=1))
    by_head = (own_rows, KV_HEADS, 1, HEAD_DIM)
    gains = jnp.pad(jnp.stack([first_gain, second_gain], axis=1), ((0, 0), (0, 126)))
    pair_own = jnp.concatenate([key_weight.reshape(by_head), value_weight.reshape(by_head)], 2)
    pair_own = jnp.concatenate([pair_own.reshape(own_rows, 2 * kv_width), gains], axis=1)
    pair_weight = gather_plane(pair_own)
    query_full = lax.all_gather(query_weight, PLANE, axis=0, tiled=True)
    output_full = lax.all_gather(output_weight, PLANE, axis=0, tiled=True)
    scales = pair_weight[:, 2 * kv_width : 2 * kv_width + 2].astype(f32).T
    first_scale, second_scale = scales[0:1], scales[1:2]

    def columns(r, first, count):
        start = (chip ^ r) * hidden_part
        parts = []
        for weight in (gate_weight, up_weight):
            some = lax.dynamic_slice_in_dim(weight, first, count, 0)
            parts.append(lax.dynamic_slice_in_dim(some, start, hidden_part, 1))
        return jnp.concatenate(parts, axis=1)

    blocks = [columns(r, 0, own_rows) for r in range(chips)]

    places = moved[:, width].astype(f32) * 256.0 + moved[:, width + 1].astype(f32)
    cosine, sine = angles_of(places)
    is_key = jnp.arange(2 * HEAD_DIM) < HEAD_DIM
    pair_cosine, pair_sine = jnp.where(is_key, cosine, 1.0), jnp.where(is_key, sine, 0.0)
    inputs = moved[:, :width].astype(f32)
    first_normed, first_inverse = normalize(inputs)
    first_input = (first_normed * first_scale).astype(bf16)
    paired = project(first_input, pair_weight, pair_cosine, pair_sine, 1.0, 2 * kv_width)

    line_pairs = [paired] + [swap(paired, m, "seq") for m in (1, 2, 3)]
    both_full = jnp.broadcast_to(moved[0, 0] * 0.0, (own_rows * owners, 2 * hidden_part))
    line_pairs[0], both_full = tie(line_pairs[0], both_full)
    pairs = [(piece, swap(piece, 2, "ctx")) for piece in line_pairs]
    all_pairs = gather_lanes(pairs).reshape(group, group, rows, -1)
    query_scale = HEAD_DIM**-0.5 * log2_e
    queries = project(first_input, query_full, cosine, sine, query_scale, width)

    queries, all_pairs, blocks, cotangent, down_weight = tie(
        queries, all_pairs, blocks, cotangent, down_weight
    )
    blocks = to_chips(blocks)
    slopes = spread(cotangent)
    down_other = swap(down_weight, 1)
    own_other = swap(blocks[0], 1)
    attended, raw_outputs, log_sums = attend_forward(queries, all_pairs, 0, KV_HEADS)
    attended, down_other, own_other = tie(attended, down_other, own_other)

    middle = inputs + dot(attended, output_full)
    second_normed, second_inverse = normalize(middle)
    second_input = (second_normed * second_scale).astype(bf16)
    second_input, slopes = tie(second_input, slopes)
    feed_input = ChipGather(second_input)
    feed_input.first()
    both_full = lax.dynamic_update_slice_in_dim(both_full, blocks[0], owner * own_rows, 0)
    both_full = lax.dynamic_update_slice_in_dim(both_full, own_other, (owner ^ 1) * own_rows, 0)
    down_full = jnp.where(
        lane == 0,
        jnp.concatenate([down_weight, down_other], axis=0),
        jnp.concatenate([down_other, down_weight], axis=0),
    )
    feed_input.ends, blocks, both_full, down_full, slopes = tie(
        feed_input.ends, blocks, both_full, down_full, slopes
    )
    feed_input.second()
    feed_slope = ChipGather(slopes)
    feed_slope.first()
    for r in range(1, chips):
        other = swap(blocks[r], 1)
        both_full = lax.dynamic_update_slice_in_dim(
            both_full, blocks[r], (owner ^ (2 * r)) * own_rows, 0
        )
        both_full = lax.dynamic_update_slice_in_dim(
            both_full, other, (owner ^ (2 * r + 1)) * own_rows, 0
        )
    feed_slope.ends, feed_input.rest, both_full = tie(
        feed_slope.ends, feed_input.rest, both_full
    )
    feed_slope.second()
    feed_input = feed_input.result()

    if hidden_part % 128:
        gate_values = dot(feed_input, both_full[:, :hidden_part])
        up_values = dot(feed_input, both_full[:, hidden_part:])
        gate_sigmoid = jax.nn.sigmoid(gate_values)
        hidden = (gate_values * gate_sigmoid * up_values).astype(bf16)
    else:
        feed_values, hidden = feed(feed_input, both_full, hidden_part)
    hidden, feed_slope.rest = tie(hidden, feed_slope.rest)
    feed_slope = feed_slope.result()
    if hidden_part % 128:
        hidden_slope = dot(feed_slope, down_full, NT)
        gate_slope = (
            hidden_slope * up_values * gate_sigmoid * (1.0 + gate_values * (1.0 - gate_sigmoid))
        ).astype(bf16)
        up_slope = (hidden_slope * gate_values * gate_sigmoid).astype(bf16)
        both_slope = jnp.concatenate([gate_slope, up_slope], axis=1)
    else:
        both_slope = feed_back(feed_slope, down_full, feed_values)

    def by_chip(share):
        return [share[r * token_count : (r + 1) * token_count] for r in range(chips)]

    def for_chips(features):
        count = 2 * own_rows
        return [
            lax.dynamic_slice_in_dim(features, (chip ^ r) * count, count, 1) for r in range(chips)
        ]

    def swap_rows(share):
        count = share.shape[0] // 2
        kept = lax.dynamic_slice_in_dim(share, lane * count, count, 0)
        return kept, swap(lax.dynamic_slice_in_dim(share, (1 - lane) * count, count, 0), 1)

    feed_share = dot(both_slope, both_full, NT).astype(bf16)
    feed_share, both_slope, hidden = tie(feed_share, both_slope, hidden)
    second_slope = ChipSum(by_chip(feed_share))
    second_slope.first()
    down_share = dot(hidden, feed_slope, TN).astype(bf16)
    second_slope.came, down_share, both_slope = tie(second_slope.came, down_share, both_slope)
    second_slope.second()
    down_two = swap_rows(down_share)
    down_two, both_slope = tie(down_two, both_slope)
    down_part = lax.psum_scatter(add(*down_two), "seq", scatter_dimension=0, tiled=True)
    both_lanes = LaneSum(dot(feed_input, both_slope, TN).astype(bf16))
    both_stack = jnp.stack(both_lanes.blocks())
    second_slope.ends, both_stack = tie(second_slope.ends, both_stack)
    both_part = lax.psum_scatter(both_stack, "seq", scatter_dimension=1, tiled=True)
    second_slope = second_slope.result()
    second_gain_share = jnp.sum(second_slope * second_normed, axis=0)
    middle_slope = slopes.astype(f32) + norm_backward(
        second_slope * second_scale, second_normed, second_inverse
    )
    attention_slope = middle_slope.astype(bf16)
    attended_slope = dot(attention_slope, output_full, NT).astype(bf16)
    payload = [
        jnp.concatenate([attention_slope, *both], axis=1)
        for both in zip(for_chips(attended), for_chips(first_input))
    ]

    attended_slope, payload = tie(attended_slope, payload)
    payload = to_chips(payload)
    query_turned, pair_terms = attend_backward(
        queries, attended_slope, all_pairs, raw_outputs, log_sums, 0, group // 2
    )
    query_turned, pair_terms, payload, down_part = tie(
        query_turned, pair_terms, payload, down_part
    )

    pair_slope = GroupSum(pair_terms.reshape(token_count * group, -1))
    down_sum = lax.all_gather(down_part, "seq", axis=0, tiled=True)
    query_slope = turn_back(query_turned, cosine, sine)
    pair_slope.came, query_slope, payload = tie(pair_slope.came, query_slope, payload)
    pair_slope.along_x()
    payload = jnp.concatenate(payload)
    output_share = dot(payload[:, width : width + 2 * own_rows], payload[:, :width], TN)
    first_columns = payload[:, width + 2 * own_rows :]
    query_side = dot(query_slope, query_full, NT)
    pair_slope.came, output_share, query_side, query_slope, both_part, hidden = tie(
        pair_slope.came, output_share.astype(bf16), query_side, query_slope, both_part, hidden
    )
    pair_slope.along_seq()
    both_part = to_chips([both_part[r] for r in range(chips)])
    query_chunks = to_chips([query_slope] * chips)
    output_own = add(*swap_rows(output_share))
    out_share = dot(hidden, down_full).astype(bf16)
    pair_slope.came, both_part, output_own, out_share = tie(
        pair_slope.came, both_part, output_own, out_share
    )
    both_sums = lax.all_gather(jnp.stack(both_part), "seq", axis=1, tiled=True)
    kv_slope = turn_back(pair_slope.result().astype(bf16), pair_cosine, pair_sine)
    first_slope = query_side + dot(kv_slope, pair_weight[:, : 2 * kv_width], NT)
    input_gradient = middle_slope + norm_backward(
        first_slope * first_scale, first_normed, first_inverse
    )
    gain_shares = jnp.stack([jnp.sum(first_slope * first_normed, axis=0), second_gain_share])
    input_gradient, kv_slope, gain_shares, query_chunks = tie(
        input_gradient.astype(bf16), kv_slope, gain_shares.astype(bf16), query_chunks
    )
    kv_chunks = to_chips([kv_slope] * chips)
    gain_parts = to_chips(for_chips(gain_shares))
    query_share = dot(first_columns, jnp.concatenate(query_chunks), TN).astype(bf16)
    query_own = add(*swap_rows(query_share))
    query_own, kv_chunks, gain_parts, out_share, down_sum = tie(
        query_own, kv_chunks, gain_parts, out_share, down_sum
    )
    out_parts = to_chips(by_chip(out_share))
    kv_share = dot(first_columns, jnp.concatenate(kv_chunks), TN).astype(bf16)
    gain_two = swap_rows(add_all(gain_parts).T.astype(bf16))
    last = jnp.concatenate(
        [
            output_own,
            add(*swap_rows(kv_share)),
            jnp.pad(add(*gain_two), ((0, 0), (0, 126))),
        ],
        axis=1,
    )
    last, query_own, input_gradient, both_sums, down_sum = tie(
        last, query_own, input_gradient, both_sums, down_sum
    )
    lasts = [LineTree(last)]
    input_gradient = spread(input_gradient)
    gate_gradient, up_gradient = place_columns(both_sums, chip)
    lasts[0].moving, gate_gradient, query_own = tie(
        lasts[0].moving, gate_gradient, query_own
    )
    lasts[0].across()
    lasts.append(LineTree(query_own))
    layer_output = (middle + add_all(out_parts)).astype(bf16)
    lasts[0].moving, lasts[1].moving, layer_output = tie(
        lasts[0].moving, lasts[1].moving, layer_output
    )
    lasts[0].outwards()
    lasts[1].across()
    layer_output = spread(layer_output)
    lasts[1].moving, input_gradient = tie(lasts[1].moving, input_gradient)
    lasts[1].outwards()
    down_gradient = down_sum.astype(f32)
    input_gradient = input_gradient.astype(f32)
    lasts[0].moving, lasts[1].moving, layer_output, down_gradient, input_gradient = tie(
        lasts[0].moving, lasts[1].moving, layer_output, down_gradient, input_gradient
    )

    last, query_gradient = lasts[0].result(), lasts[1].result()
    output_gradient, pairs = last[:, :width], last[:, width:]
    gain_gradients = pairs[:, 2 * kv_width : 2 * kv_width + 2].T
    pairs = pairs[:, : 2 * kv_width].reshape(own_rows, KV_HEADS, 2, HEAD_DIM)
    return (
        layer_output,
        input_gradient,
        query_gradient,
        pairs[:, :, 0].reshape(own_rows, kv_width),
        pairs[:, :, 1].reshape(own_rows, kv_width),
        output_gradient,
        gate_gradient,
        up_gradient,
        down_gradient,
        gain_gradients[0],
        gain_gradients[1],
    )


def solution(mesh):
    tokens = P(("dp", "seq", "ctx"), None)
    rows = P(PLANE, None)
    return jax.shard_map(
        on_device,
        mesh=mesh,
        in_specs=(tokens, P(("dp", "seq", "ctx")), tokens) + (rows,) * 7 + (P(PLANE),) * 2,
        out_specs=(tokens,) * 2 + (rows,) * 7 + (P(PLANE),) * 2,
        check_vma=False,
    )
```

```python
from functools import partial

import jax
import jax.numpy as jnp
from jax import lax
from jax.experimental import pallas as pl
from jax.experimental.pallas import tpu as pltpu
from jax.sharding import PartitionSpec as P

HEADS = 32
KV_HEADS = 4
HEAD_DIM = 64
BLOCK = 256

epsilon = 1e-05
rotary_base = 10000.0
log2_e = 1.4426950408889634
ln_2 = 0.6931471805599453
bf16, f32 = jnp.bfloat16, jnp.float32
PLANE = ("dp", "ctx")
GROUP = ("seq", "ctx")
NT = (((1,), (1,)), ((), ()))
NN = (((1,), (0,)), ((), ()))
TN = (((0,), (0,)), ((), ()))


def dot(left, right, dims=NN):
    return lax.dot_general(left, right, dims, preferred_element_type=f32)


def normalize(features):
    inverse_rms = lax.rsqrt(jnp.mean(features * features, axis=-1, keepdims=True) + epsilon)
    return (features * inverse_rms, inverse_rms)


def norm_backward(slopes, normed, inverse_rms):
    return inverse_rms * (slopes - normed * jnp.mean(slopes * normed, axis=-1, keepdims=True))


def angles_of(places):
    lane = jnp.arange(2 * HEAD_DIM)
    exponent = (lane % (HEAD_DIM // 2)).astype(f32) * (2.0 / HEAD_DIM)
    frequency = rotary_base ** (-exponent)
    angles = places[:, None] * frequency[None, :]
    sign = jnp.where(lane % HEAD_DIM < HEAD_DIM // 2, -1.0, 1.0)
    return jnp.cos(angles), jnp.sin(angles) * sign


def tie(*values):
    return lax.optimization_barrier(values)


def swap(values, mask, axes=PLANE):
    count = lax.axis_size(axes)
    return lax.ppermute(values, axes, [(i, i ^ mask) for i in range(count)])


def halves(count):
    return (slice(0, count // 2), slice(count // 2, count))


class ChipGather:
    def __init__(self, own):
        self.own = own

    def first(self):
        self.ends = {}
        r = 1
        while r < lax.axis_size(PLANE) // 2:
            self.ends[r] = swap(self.own, r << 1)
            r *= 2

    def second(self):
        top, bottom = halves(self.own.shape[0])
        parts = {r: (values[top], values[bottom]) for r, values in self.ends.items()}
        for r in range(1, lax.axis_size(PLANE) // 2):
            low, high = r & -r, 1 << (r.bit_length() - 1)
            if low != high:
                first = swap(parts[r ^ low][0], low << 1)
                parts[r] = (first, swap(parts[r ^ high][1], high << 1))
        self.rest = {r: both for r, both in parts.items() if r not in self.ends}

    def chunks(self):
        half = self.own.shape[0] // 2
        chunks = [(0, 0, self.own)]
        for r in range(1, lax.axis_size(PLANE) // 2):
            if r in self.ends:
                chunks.append((r, 0, self.ends[r]))
            else:
                chunks += [(r, 0, self.rest[r][0]), (r, half, self.rest[r][1])]
        return chunks

    def result(self):
        return jnp.concatenate([values for _, _, values in self.chunks()], axis=0)


def add(left, right):
    return (left.astype(f32) + right.astype(f32)).astype(bf16)


class ChipSum:
    def __init__(self, blocks):
        self.parts = [[block[half] for half in halves(block.shape[0])] for block in blocks]

    def first(self):
        chips = len(self.parts)
        self.came = {}
        for r in sorted(range(1, chips), key=lambda r: -bin(r).count("1")):
            low, high = r & -r, 1 << (r.bit_length() - 1)
            if low == high:
                continue
            if bin(r).count("1") < bin(chips - 1).count("1"):
                self.settle(r)
            self.came[r ^ low, 0, r] = swap(self.parts[r][0], low << 1)
            self.came[r ^ high, 1, r] = swap(self.parts[r][1], high << 1)

    def settle(self, only=None):
        for key in sorted(self.came):
            if only is None or key[0] == only:
                self.parts[key[0]][key[1]] = add(self.parts[key[0]][key[1]], self.came.pop(key))

    def second(self):
        self.settle()
        self.ends = []
        r = 1
        while r < len(self.parts):
            self.ends.append(swap(jnp.concatenate(self.parts[r], axis=0), r << 1))
            r *= 2

    def result(self):
        return add_all([jnp.concatenate(self.parts[0], axis=0)] + self.ends)


def to_chips(blocks):
    return [block if r == 0 else swap(block, r << 1) for r, block in enumerate(blocks)]


def add_all(values):
    total = values[0].astype(f32)
    for other in values[1:]:
        total = total + other.astype(f32)
    return total


def gather_plane(own):
    rows = own.shape[0]
    owner = lax.axis_index(PLANE)
    full = jnp.zeros((rows * lax.axis_size(PLANE), own.shape[1]), own.dtype)
    gather = ChipGather(own)
    gather.first()
    gather.second()
    for r, first, chunk in gather.chunks():
        other = swap(chunk, 1)
        full = lax.dynamic_update_slice_in_dim(full, chunk, (owner ^ (2 * r)) * rows + first, 0)
        full = lax.dynamic_update_slice_in_dim(full, other, (owner ^ (2 * r + 1)) * rows + first, 0)
    return full


class LaneSum:
    def __init__(self, values):
        owners = lax.axis_size(PLANE)
        owner = lax.axis_index(PLANE)
        rows = values.shape[0] // owners
        self.kept, self.came = [], []
        for r in range(owners // 2):
            away = lax.dynamic_slice_in_dim(values, (owner ^ (2 * r + 1)) * rows, rows, 0)
            self.kept.append(lax.dynamic_slice_in_dim(values, (owner ^ (2 * r)) * rows, rows, 0))
            self.came.append(swap(away, 1))

    def blocks(self):
        return [add(kept, came) for kept, came in zip(self.kept, self.came)]


class LineTree:
    def __init__(self, share):
        self.share = share
        self.moving = lax.ppermute(share, "seq", [(0, 1), (3, 2)])

    def across(self):
        self.share = add(self.share, self.moving)
        self.moving = lax.ppermute(self.share, "seq", [(1, 2), (2, 1)])

    def outwards(self):
        self.share = add(self.share, self.moving)
        self.moving = lax.ppermute(self.share, "seq", [(1, 0), (2, 3)])

    def result(self):
        place = lax.axis_index("seq")
        inner = (place == 1) | (place == 2)
        return jnp.where(inner, self.share, self.moving).astype(f32)


class LineSum:
    def __init__(self, share):
        self.share = share

    def scatter(self):
        place = lax.axis_index("seq")
        count = lax.axis_size("seq")
        rows = self.share.shape[0] // count

        def part(m):
            return lax.dynamic_slice_in_dim(self.share, (place ^ m) * rows, rows, 0)

        self.parts = [part(0)] + [swap(part(m), m, "seq") for m in range(1, count)]

    def gather(self):
        total = add_all(self.parts).astype(bf16)
        self.parts = [total] + [swap(total, m, "seq") for m in range(1, len(self.parts))]

    def result(self):
        place = lax.axis_index("seq")
        rows = self.parts[0].shape[0]
        out = self.share
        for m, values in enumerate(self.parts):
            out = lax.dynamic_update_slice_in_dim(out, values, (place ^ m) * rows, 0)
        return out


def gather_lanes(pairs):
    pairs = [jnp.concatenate(pair, axis=0) for pair in pairs]
    others = [swap(pair, 1, "ctx") for pair in pairs]
    return jnp.concatenate([half for both in zip(pairs, others) for half in both], axis=0)


class GroupSum:
    def __init__(self, values):
        shaped = values.reshape(4, 2, 2, -1, values.shape[1])
        self.kept, self.came = shaped[:, 0], swap(shaped[:, 1], 1, "ctx")

    def along_x(self):
        pair = add(self.kept, self.came)
        self.kept, self.came = pair[:, 0], swap(pair[:, 1], 2, "ctx")

    def along_seq(self):
        line = add(self.kept, self.came)
        self.kept, self.came = line[0], [swap(line[m], m, "seq") for m in (1, 2, 3)]

    def result(self):
        total = self.kept.astype(f32)
        for values in self.came:
            total = total + values.astype(f32)
        return total


def spread(rows):
    count = lax.axis_size(GROUP)
    shaped = rows.reshape(count, -1, rows.shape[1])
    return lax.all_to_all(shaped, GROUP, 0, 0, tiled=True).reshape(rows.shape)


def place_body(at_ref, values_ref, gate_ref, up_ref):
    count = gate_ref.shape[1]
    gate_ref[...] = values_ref[0, :, :count].astype(f32)
    up_ref[...] = values_ref[0, :, count:].astype(f32)


def place_columns(values, at):
    chips, rows, both = values.shape
    count = both // 2
    if count % 128:
        gate = jnp.zeros((rows, chips * count), f32)
        up = jnp.zeros((rows, chips * count), f32)
        for r in range(chips):
            block, start = values[r].astype(f32), (at ^ r) * count
            gate = lax.dynamic_update_slice_in_dim(gate, block[:, :count], start, 1)
            up = lax.dynamic_update_slice_in_dim(up, block[:, count:], start, 1)
        return gate, up
    shape = jax.ShapeDtypeStruct((rows, chips * count), f32)
    return pl.pallas_call(
        place_body,
        grid_spec=pltpu.PrefetchScalarGridSpec(
            num_scalar_prefetch=1,
            grid=(chips,),
            in_specs=[pl.BlockSpec((1, rows, both), lambda t, at_ref: (at_ref[0] ^ t, 0, 0))],
            out_specs=[pl.BlockSpec((rows, count), lambda t, at_ref: (0, t))] * 2,
        ),
        out_shape=(shape, shape),
        cost_estimate=pl.CostEstimate(
            flops=0, bytes_accessed=10 * chips * rows * both // 2, transcendentals=0
        ),
        compiler_params=pltpu.CompilerParams(vmem_limit_bytes=24 * 1024 * 1024),
        name="place_columns",
    )(at.astype(jnp.int32)[None], values)


class LineGather:
    def __init__(self, own):
        self.own, self.right, self.left = own, [], []

    def step(self):
        at = len(self.right)
        count = lax.axis_size("seq")
        right = self.right[-1] if at else self.own
        left = self.left[-1] if at else self.own
        pairs = [(i, i + 1) for i in range(at, count - 1)]
        self.right.append(lax.ppermute(right, "seq", pairs))
        back = [(i, i - 1) for i in range(count - 1 - at, 0, -1)]
        self.left.append(lax.ppermute(left, "seq", back))

    def result(self):
        count = lax.axis_size("seq")
        rows = self.own.shape[0]
        around = jnp.concatenate([*self.right[::-1], self.own, *self.left], axis=0)
        start = (count - 1 - lax.axis_index("seq")) * rows
        return lax.dynamic_slice_in_dim(around, start, count * rows, 0)


def stack_heads(block, heads, rows, first):
    return jnp.concatenate(
        [
            block[b * rows : (b + 1) * rows, (first + h) * HEAD_DIM : (first + h + 1) * HEAD_DIM]
            for b in range(2)
            for h in range(heads)
        ],
        axis=0,
    )


def spread_heads(stacked, heads, rows, b):
    return jnp.concatenate(
        [stacked[(b * heads + h) * rows : (b * heads + h + 1) * rows] for h in range(heads)], axis=1
    )


def forward_body(
    q_ref, kv_ref, o_ref, ot_ref, lse_ref, kvt, qs, m_s, l_s, *, groups, heads, rows, blocks
):
    c = pl.program_id(0)
    keys = kv_ref.shape[0] * rows
    width = 2 * heads * rows
    half = heads * rows

    @pl.when(c == 0)
    def _():
        def one(kt, carry):
            for g in range(groups):
                tile = kv_ref[:, kt, :, g * 128 : (g + 1) * 128].reshape(keys, 128)
                kvt[g, kt] = tile.astype(f32).T.astype(bf16)[HEAD_DIM:]
            return carry

        lax.fori_loop(0, blocks, one, 0)

    for g in range(groups):
        q = stack_heads(q_ref[...], heads, rows, g * heads)
        qs[g] = jnp.concatenate([q, jnp.zeros((width, HEAD_DIM), bf16)], axis=1)

    def tiles(kts, lo, first):
        scores = []
        for g in range(groups):
            for kt in kts:
                kv = kv_ref[:, kt, :, g * 128 : (g + 1) * 128].reshape(keys, 128)
                scores.append(dot(kv, qs[g, lo:], NT))
        for g in range(groups):
            sts = scores[g * len(kts) : (g + 1) * len(kts)]
            peak = jnp.max(sts[0], axis=0, keepdims=True)
            for st in sts[1:]:
                peak = jnp.maximum(peak, jnp.max(st, axis=0, keepdims=True))
            if not first:
                m_old = m_s[g, :, lo:]
                peak = jnp.maximum(m_old, peak)
            total, pv = 0.0, 0.0
            for kt, st in zip(kts, sts):
                p = jnp.exp2(st - peak)
                total = total + jnp.sum(p, axis=0, keepdims=True)
                pv = pv + dot(kvt[g, kt], p.astype(bf16))
            if first:
                l_s[g, :, lo:] = total
                ot_ref[0, g, :, lo:] = pv
            else:
                shrink = jnp.exp2(m_old - peak)
                l_s[g, :, lo:] = l_s[g, :, lo:] * shrink + total
                ot_ref[0, g, :, lo:] = ot_ref[0, g, :, lo:] * shrink + pv
            m_s[g, :, lo:] = peak

    def step(i, carry):
        tiles((2 * i + 1, 2 * i + 2), 0, False)
        return carry

    tiles((0,), 0, True)
    lax.fori_loop(0, c, step, 0)
    tiles((2 * c + 1,), half, False)
    for g in range(groups):
        total = l_s[g]
        o = ot_ref[0, g] / total
        ot_ref[0, g] = o
        lse_ref[0, g : g + 1, :] = m_s[g] + jnp.log2(total)
        stacked = o.T.astype(bf16)
        for b in range(2):
            o_ref[b * rows : (b + 1) * rows, g * heads * HEAD_DIM : (g + 1) * heads * HEAD_DIM] = (
                spread_heads(stacked, heads, rows, b)
            )


def attend_forward(q, kv, first, groups):
    devices, blocks, rows, kv_width = kv.shape
    heads = q.shape[1] * 128 // HEAD_DIM // kv_width
    wide = heads * HEAD_DIM * groups
    width = 2 * heads * rows
    pairs = blocks // 2
    keys = devices * rows
    tiles = groups * blocks * (blocks + 1) // 2
    at = first // groups
    return pl.pallas_call(
        partial(forward_body, groups=groups, heads=heads, rows=rows, blocks=blocks),
        grid=(pairs,),
        out_shape=(
            jax.ShapeDtypeStruct((q.shape[0], wide), bf16),
            jax.ShapeDtypeStruct((pairs, groups, HEAD_DIM, width), f32),
            jax.ShapeDtypeStruct((pairs, groups, width), f32),
        ),
        in_specs=[
            pl.BlockSpec((2 * rows, wide), lambda c: (c, at)),
            pl.BlockSpec((devices, blocks, rows, groups * 128), lambda c: (0, 0, 0, at)),
        ],
        out_specs=(
            pl.BlockSpec((2 * rows, wide), lambda c: (c, 0)),
            pl.BlockSpec((1, groups, HEAD_DIM, width), lambda c: (c, 0, 0, 0)),
            pl.BlockSpec((1, groups, width), lambda c: (c, 0, 0)),
        ),
        scratch_shapes=[
            pltpu.VMEM((groups, blocks, HEAD_DIM, keys), bf16),
            pltpu.VMEM((groups, width, 128), bf16),
            pltpu.VMEM((groups, 1, width), f32),
            pltpu.VMEM((groups, 1, width), f32),
        ],
        compiler_params=pltpu.CompilerParams(vmem_limit_bytes=40 * 1024 * 1024),
        cost_estimate=pl.CostEstimate(
            flops=tiles * keys * width * 8,
            bytes_accessed=6 * 1024 * 1024,
            transcendentals=0,
        ),
        name="attend_forward",
    )(q, kv)


def backward_body(
    q_ref,
    do_ref,
    kv_ref,
    ot_ref,
    lse_ref,
    dq_ref,
    dkv_ref,
    kt_s,
    qs,
    dos,
    d_s,
    dqt,
    acc,
    *,
    groups,
    heads,
    rows,
    blocks,
    start,
):
    c = pl.program_id(0) + start
    devices = kv_ref.shape[0]
    keys = devices * rows
    width = 2 * heads * rows
    half = heads * rows

    @pl.when(c == start)
    def _():
        def one(kt, carry):
            for g in range(groups):
                tile = kv_ref[:, kt, :, g * 128 : (g + 1) * 128].reshape(keys, 128)
                kt_s[g, kt] = tile.astype(f32).T.astype(bf16)[:HEAD_DIM]
                acc[g, kt] = jnp.zeros((keys, 128), f32)
            return carry

        lax.fori_loop(0, blocks, one, 0)

    zero = jnp.zeros((width, HEAD_DIM), bf16)
    for g in range(groups):
        q = stack_heads(q_ref[...], heads, rows, g * heads)
        do = stack_heads(do_ref[...], heads, rows, g * heads)
        qs[g] = jnp.concatenate([q, zero], axis=1)
        dos[g] = jnp.concatenate([zero, do], axis=1)
        d_s[g] = jnp.sum(do.astype(f32).T * ot_ref[0, g], axis=0, keepdims=True)
        dqt[g] = jnp.zeros((HEAD_DIM, width), f32)

    def tiles(kt, lo):
        kvs = [
            kv_ref[:, kt, :, g * 128 : (g + 1) * 128].reshape(keys, 128) for g in range(groups)
        ]
        sts = [dot(kvs[g], qs[g, lo:], NT) for g in range(groups)]
        dpts = [dot(kvs[g], dos[g, lo:], NT) for g in range(groups)]
        ps = [jnp.exp2(sts[g] - lse_ref[0, g : g + 1, lo:]) for g in range(groups)]
        dss = [(ps[g] * (dpts[g] - d_s[g, :, lo:])).astype(bf16) for g in range(groups)]
        for g in range(groups):
            dqt[g, :, lo:] += dot(kt_s[g, kt], dss[g])
        for g in range(groups):
            acc[g, kt] += dot(dss[g], qs[g, lo:]) + dot(ps[g].astype(bf16), dos[g, lo:])

    def step(kt, carry):
        tiles(kt, 0)
        return carry

    lax.fori_loop(0, 2 * c + 1, step, 0)
    tiles(2 * c + 1, half)
    for g in range(groups):
        dq = (dqt[g] * (HEAD_DIM**-0.5)).T.astype(bf16)
        for b in range(2):
            dq_ref[b * rows : (b + 1) * rows, g * heads * HEAD_DIM : (g + 1) * heads * HEAD_DIM] = (
                spread_heads(dq, heads, rows, b)
            )

    @pl.when(c == start + pl.num_programs(0) - 1)
    def _():
        column = lax.broadcasted_iota(jnp.int32, (1, 128), 1)
        factor = jnp.where(column < HEAD_DIM, ln_2, 1.0)

        def one(kt, carry):
            for g in range(groups):
                dkv_ref[:, kt, :, g * 128 : (g + 1) * 128] = (
                    (acc[g, kt] * factor).astype(bf16).reshape(devices, rows, 128)
                )
            return carry

        lax.fori_loop(0, blocks, one, 0)


def attend_backward(q, do, kv, ot, lse, start, count):
    groups = KV_HEADS
    devices, blocks, rows, kv_width = kv.shape
    heads = q.shape[1] * 128 // HEAD_DIM // kv_width
    wide = heads * HEAD_DIM * groups
    width = 2 * heads * rows
    keys = devices * rows
    tiles = groups * sum(4 * c + 3 for c in range(start, start + count))
    kv_shape = (devices, blocks, rows, groups * 128)
    return pl.pallas_call(
        partial(backward_body, groups=groups, heads=heads, rows=rows, blocks=blocks, start=start),
        grid=(count,),
        out_shape=(
            jax.ShapeDtypeStruct((2 * rows * count, wide), bf16),
            jax.ShapeDtypeStruct(kv_shape, bf16),
        ),
        in_specs=[
            pl.BlockSpec((2 * rows, wide), lambda c: (c + start, 0)),
            pl.BlockSpec((2 * rows, wide), lambda c: (c + start, 0)),
            pl.BlockSpec(kv_shape, lambda c: (0, 0, 0, 0)),
            pl.BlockSpec((1, groups, HEAD_DIM, width), lambda c: (c + start, 0, 0, 0)),
            pl.BlockSpec((1, groups, width), lambda c: (c + start, 0, 0)),
        ],
        out_specs=(
            pl.BlockSpec((2 * rows, wide), lambda c: (c, 0)),
            pl.BlockSpec(kv_shape, lambda c: (0, 0, 0, 0)),
        ),
        scratch_shapes=[
            pltpu.VMEM((groups, blocks, HEAD_DIM, keys), bf16),
            pltpu.VMEM((groups, width, 128), bf16),
            pltpu.VMEM((groups, width, 128), bf16),
            pltpu.VMEM((groups, 1, width), f32),
            pltpu.VMEM((groups, HEAD_DIM, width), f32),
            pltpu.VMEM((groups, blocks, keys, 128), f32),
        ],
        compiler_params=pltpu.CompilerParams(vmem_limit_bytes=40 * 1024 * 1024),
        cost_estimate=pl.CostEstimate(
            flops=tiles * keys * width * 8,
            bytes_accessed=8 * 1024 * 1024,
            transcendentals=0,
        ),
        name="attend_backward",
    )(q, do, kv, ot, lse)


def turn_lanes(values, cosine, sine):
    count, width = values.shape
    lane = lax.broadcasted_iota(jnp.int32, (count, width), 1) % HEAD_DIM
    half_width = HEAD_DIM // 2
    other = jnp.where(
        lane < half_width,
        pltpu.roll(values, width - half_width, 1),
        pltpu.roll(values, half_width, 1),
    )
    times = width // cosine.shape[1]
    return values * jnp.tile(cosine, (1, times)) + other * jnp.tile(sine, (1, times))


def project_body(x_ref, w_ref, cosine_ref, sine_ref, out_ref, *, scale):
    values = dot(x_ref[...], w_ref[...])
    out_ref[...] = (turn_lanes(values, cosine_ref[...], sine_ref[...]) * scale).astype(bf16)


def project(x, weight, cosine, sine, scale, width):
    count, depth = x.shape
    tile = min(width, 512)
    return pl.pallas_call(
        partial(project_body, scale=scale),
        grid=(width // tile,),
        out_shape=jax.ShapeDtypeStruct((count, width), bf16),
        in_specs=[
            pl.BlockSpec((count, depth), lambda i: (0, 0)),
            pl.BlockSpec((depth, tile), lambda i: (0, i)),
            pl.BlockSpec(cosine.shape, lambda i: (0, 0)),
            pl.BlockSpec(sine.shape, lambda i: (0, 0)),
        ],
        out_specs=pl.BlockSpec((count, tile), lambda i: (0, i)),
        compiler_params=pltpu.CompilerParams(vmem_limit_bytes=24 * 1024 * 1024),
        cost_estimate=pl.CostEstimate(
            flops=2 * count * depth * width,
            bytes_accessed=2 * (count * depth + depth * width + count * width),
            transcendentals=0,
        ),
        name="project",
    )(x, weight, cosine, sine)


def turn_body(x_ref, cosine_ref, sine_ref, out_ref):
    values = x_ref[...].astype(f32)
    out_ref[...] = turn_lanes(values, cosine_ref[...], sine_ref[...]).astype(bf16)


def turn_back(x, cosine, sine):
    count, width = x.shape
    tile = min(width, 512)
    return pl.pallas_call(
        turn_body,
        grid=(width // tile,),
        out_shape=jax.ShapeDtypeStruct(x.shape, bf16),
        in_specs=[
            pl.BlockSpec((count, tile), lambda i: (0, i)),
            pl.BlockSpec(cosine.shape, lambda i: (0, 0)),
            pl.BlockSpec(sine.shape, lambda i: (0, 0)),
        ],
        out_specs=pl.BlockSpec((count, tile), lambda i: (0, i)),
        cost_estimate=pl.CostEstimate(
            flops=6 * count * width, bytes_accessed=4 * count * width, transcendentals=0
        ),
        name="turn_back",
    )(x, cosine, -sine)


def tiles_of(count):
    return [(at, min(256, count - at)) for at in range(0, count, 256)]


def feed_body(x_ref, w_ref, values_ref, hidden_ref):
    count = hidden_ref.shape[1]
    for at, size in tiles_of(count):
        here, there = slice(at, at + size), slice(count + at, count + at + size)
        gate = dot(x_ref[...], w_ref[:, here])
        up = dot(x_ref[...], w_ref[:, there])
        values_ref[:, here] = gate
        values_ref[:, there] = up
        hidden_ref[:, here] = (gate * jax.nn.sigmoid(gate) * up).astype(bf16)


def feed_back_body(c_ref, d_ref, values_ref, slope_ref):
    count = d_ref.shape[0]
    for at, size in tiles_of(count):
        here, there = slice(at, at + size), slice(count + at, count + at + size)
        slope = dot(c_ref[...], d_ref[here, :], NT)
        gate, up = values_ref[:, here], values_ref[:, there]
        sigmoid = jax.nn.sigmoid(gate)
        silu = gate * sigmoid
        slope_ref[:, here] = (slope * up * sigmoid * (1.0 + gate * (1.0 - sigmoid))).astype(bf16)
        slope_ref[:, there] = (slope * silu).astype(bf16)


def feed(x, both, count):
    tokens, width = x.shape
    tile = min(tokens, 256)
    return pl.pallas_call(
        feed_body,
        grid=(tokens // tile,),
        out_shape=(
            jax.ShapeDtypeStruct((tokens, 2 * count), f32),
            jax.ShapeDtypeStruct((tokens, count), bf16),
        ),
        in_specs=[
            pl.BlockSpec((tile, width), lambda i: (i, 0)),
            pl.BlockSpec(both.shape, lambda i: (0, 0), pipeline_mode=pl.Buffered(1)),
        ],
        out_specs=(
            pl.BlockSpec((tile, 2 * count), lambda i: (i, 0)),
            pl.BlockSpec((tile, count), lambda i: (i, 0)),
        ),
        compiler_params=pltpu.CompilerParams(vmem_limit_bytes=40 * 1024 * 1024),
        cost_estimate=pl.CostEstimate(
            flops=4 * tokens * width * count,
            bytes_accessed=2 * (tokens * width + 2 * width * count + 5 * tokens * count),
            transcendentals=tokens * count,
        ),
        name="feed",
    )(x, both)


def feed_back(cotangent, down, values):
    tokens, width = cotangent.shape
    count = down.shape[0]
    tile = min(tokens, 256)
    return pl.pallas_call(
        feed_back_body,
        grid=(tokens // tile,),
        out_shape=jax.ShapeDtypeStruct((tokens, 2 * count), bf16),
        in_specs=[
            pl.BlockSpec((tile, width), lambda i: (i, 0)),
            pl.BlockSpec(down.shape, lambda i: (0, 0), pipeline_mode=pl.Buffered(1)),
            pl.BlockSpec((tile, 2 * count), lambda i: (i, 0)),
        ],
        out_specs=pl.BlockSpec((tile, 2 * count), lambda i: (i, 0)),
        compiler_params=pltpu.CompilerParams(vmem_limit_bytes=32 * 1024 * 1024),
        cost_estimate=pl.CostEstimate(
            flops=2 * tokens * width * count,
            bytes_accessed=2 * (tokens * width + width * count + 6 * tokens * count),
            transcendentals=tokens * count,
        ),
        name="feed_back",
    )(cotangent, down, values)


def on_device(
    tokens,
    positions,
    cotangent,
    query_weight,
    key_weight,
    value_weight,
    output_weight,
    gate_weight,
    up_weight,
    down_weight,
    first_gain,
    second_gain,
):
    token_count, width = tokens.shape
    group = lax.axis_size(GROUP)
    owners = lax.axis_size(PLANE)
    owner = lax.axis_index(PLANE)
    lane = owner % 2
    chip = owner // 2
    chips = owners // 2
    rows = token_count // group
    own_rows = query_weight.shape[0]
    hidden_part = gate_weight.shape[1] // chips
    down_rows = down_weight.shape[0]
    kv_width = key_weight.shape[1]
    line = lax.axis_size("seq")
    line_place = lax.axis_index("seq")
    direct = [r for r in range(1, chips) if r & (r - 1) == 0]
    indirect = [r for r in range(1, chips) if r & (r - 1)]

    digits = jnp.stack([positions // 256, positions % 256], axis=1).astype(bf16)
    moved = spread(jnp.concatenate([tokens, jnp.pad(digits, ((0, 0), (0, 126)))], axis=1))
    by_head = (own_rows, KV_HEADS, 1, HEAD_DIM)
    gains = jnp.pad(jnp.stack([first_gain, second_gain], axis=1), ((0, 0), (0, 126)))
    pair_own = jnp.concatenate([key_weight.reshape(by_head), value_weight.reshape(by_head)], 2)
    pair_own = jnp.concatenate([pair_own.reshape(own_rows, 2 * kv_width), gains], axis=1)
    pair_weight = gather_plane(pair_own)
    query_full = lax.all_gather(query_weight, PLANE, axis=0, tiled=True)
    output_full = lax.all_gather(output_weight, PLANE, axis=0, tiled=True)
    scales = pair_weight[:, 2 * kv_width : 2 * kv_width + 2].astype(f32).T
    first_scale, second_scale = scales[0:1], scales[1:2]

    def columns(r, first, count):
        start = (chip ^ r) * hidden_part
        parts = []
        for weight in (gate_weight, up_weight):
            some = lax.dynamic_slice_in_dim(weight, first, count, 0)
            parts.append(lax.dynamic_slice_in_dim(some, start, hidden_part, 1))
        return jnp.concatenate(parts, axis=1)

    blocks = [columns(r, 0, own_rows) for r in range(chips)]

    places = moved[:, width].astype(f32) * 256.0 + moved[:, width + 1].astype(f32)
    cosine, sine = angles_of(places)
    is_key = jnp.arange(2 * HEAD_DIM) < HEAD_DIM
    pair_cosine, pair_sine = jnp.where(is_key, cosine, 1.0), jnp.where(is_key, sine, 0.0)
    inputs = moved[:, :width].astype(f32)
    first_normed, first_inverse = normalize(inputs)
    first_input = (first_normed * first_scale).astype(bf16)
    paired = project(first_input, pair_weight, pair_cosine, pair_sine, 1.0, 2 * kv_width)

    line_pairs = [paired] + [swap(paired, m, "seq") for m in (1, 2, 3)]
    both_full = jnp.broadcast_to(moved[0, 0] * 0.0, (own_rows * owners, 2 * hidden_part))
    line_pairs[0], both_full = tie(line_pairs[0], both_full)
    pairs = [(piece, swap(piece, 2, "ctx")) for piece in line_pairs]
    all_pairs = gather_lanes(pairs).reshape(group, group, rows, -1)
    query_scale = HEAD_DIM**-0.5 * log2_e
    queries = project(first_input, query_full, cosine, sine, query_scale, width)

    queries, all_pairs, blocks, cotangent, down_weight = tie(
        queries, all_pairs, blocks, cotangent, down_weight
    )
    blocks = to_chips(blocks)
    slopes = spread(cotangent)
    down_other = swap(down_weight, 1)
    own_other = swap(blocks[0], 1)
    attended, raw_outputs, log_sums = attend_forward(queries, all_pairs, 0, KV_HEADS)
    attended, down_other, own_other = tie(attended, down_other, own_other)

    middle = inputs + dot(attended, output_full)
    second_normed, second_inverse = normalize(middle)
    second_input = (second_normed * second_scale).astype(bf16)
    second_input, slopes = tie(second_input, slopes)
    feed_input = ChipGather(second_input)
    feed_input.first()
    both_full = lax.dynamic_update_slice_in_dim(both_full, blocks[0], owner * own_rows, 0)
    both_full = lax.dynamic_update_slice_in_dim(both_full, own_other, (owner ^ 1) * own_rows, 0)
    down_full = jnp.where(
        lane == 0,
        jnp.concatenate([down_weight, down_other], axis=0),
        jnp.concatenate([down_other, down_weight], axis=0),
    )
    feed_input.ends, blocks, both_full, down_full, slopes = tie(
        feed_input.ends, blocks, both_full, down_full, slopes
    )
    feed_input.second()
    feed_slope = ChipGather(slopes)
    feed_slope.first()
    for r in range(1, chips):
        other = swap(blocks[r], 1)
        both_full = lax.dynamic_update_slice_in_dim(
            both_full, blocks[r], (owner ^ (2 * r)) * own_rows, 0
        )
        both_full = lax.dynamic_update_slice_in_dim(
            both_full, other, (owner ^ (2 * r + 1)) * own_rows, 0
        )
    feed_slope.ends, feed_input.rest, both_full = tie(
        feed_slope.ends, feed_input.rest, both_full
    )
    feed_slope.second()
    feed_input = feed_input.result()

    if hidden_part % 128:
        gate_values = dot(feed_input, both_full[:, :hidden_part])
        up_values = dot(feed_input, both_full[:, hidden_part:])
        gate_sigmoid = jax.nn.sigmoid(gate_values)
        hidden = (gate_values * gate_sigmoid * up_values).astype(bf16)
    else:
        feed_values, hidden = feed(feed_input, both_full, hidden_part)
    hidden, feed_slope.rest = tie(hidden, feed_slope.rest)
    feed_slope = feed_slope.result()
    if hidden_part % 128:
        hidden_slope = dot(feed_slope, down_full, NT)
        gate_slope = (
            hidden_slope * up_values * gate_sigmoid * (1.0 + gate_values * (1.0 - gate_sigmoid))
        ).astype(bf16)
        up_slope = (hidden_slope * gate_values * gate_sigmoid).astype(bf16)
        both_slope = jnp.concatenate([gate_slope, up_slope], axis=1)
    else:
        both_slope = feed_back(feed_slope, down_full, feed_values)

    def by_chip(share):
        return [share[r * token_count : (r + 1) * token_count] for r in range(chips)]

    def for_chips(features):
        count = 2 * own_rows
        return [
            lax.dynamic_slice_in_dim(features, (chip ^ r) * count, count, 1) for r in range(chips)
        ]

    def swap_rows(share):
        count = share.shape[0] // 2
        kept = lax.dynamic_slice_in_dim(share, lane * count, count, 0)
        return kept, swap(lax.dynamic_slice_in_dim(share, (1 - lane) * count, count, 0), 1)

    feed_share = dot(both_slope, both_full, NT).astype(bf16)
    feed_share, both_slope, hidden = tie(feed_share, both_slope, hidden)
    second_slope = ChipSum(by_chip(feed_share))
    second_slope.first()
    down_share = dot(hidden, feed_slope, TN).astype(bf16)
    second_slope.came, down_share, both_slope = tie(second_slope.came, down_share, both_slope)
    second_slope.second()
    down_two = swap_rows(down_share)
    down_two, both_slope = tie(down_two, both_slope)
    down_part = lax.psum_scatter(add(*down_two), "seq", scatter_dimension=0, tiled=True)
    both_lanes = LaneSum(dot(feed_input, both_slope, TN).astype(bf16))
    both_stack = jnp.stack(both_lanes.blocks())
    second_slope.ends, both_stack = tie(second_slope.ends, both_stack)
    both_part = lax.psum_scatter(both_stack, "seq", scatter_dimension=1, tiled=True)
    second_slope = second_slope.result()
    second_gain_share = jnp.sum(second_slope * second_normed, axis=0)
    middle_slope = slopes.astype(f32) + norm_backward(
        second_slope * second_scale, second_normed, second_inverse
    )
    attention_slope = middle_slope.astype(bf16)
    attended_slope = dot(attention_slope, output_full, NT).astype(bf16)
    payload = [
        jnp.concatenate([attention_slope, *both], axis=1)
        for both in zip(for_chips(attended), for_chips(first_input))
    ]

    attended_slope, payload = tie(attended_slope, payload)
    payload = to_chips(payload)
    query_turned, pair_terms = attend_backward(
        queries, attended_slope, all_pairs, raw_outputs, log_sums, 0, group // 2
    )
    query_turned, pair_terms, payload, down_part = tie(
        query_turned, pair_terms, payload, down_part
    )

    pair_slope = GroupSum(pair_terms.reshape(token_count * group, -1))
    down_sum = lax.all_gather(down_part, "seq", axis=0, tiled=True)
    query_slope = turn_back(query_turned, cosine, sine)
    pair_slope.came, query_slope, payload = tie(pair_slope.came, query_slope, payload)
    pair_slope.along_x()
    payload = jnp.concatenate(payload)
    output_share = dot(payload[:, width : width + 2 * own_rows], payload[:, :width], TN)
    first_columns = payload[:, width + 2 * own_rows :]
    query_side = dot(query_slope, query_full, NT)
    pair_slope.came, output_share, query_side, query_slope, both_part, hidden = tie(
        pair_slope.came, output_share.astype(bf16), query_side, query_slope, both_part, hidden
    )
    pair_slope.along_seq()
    both_part = to_chips([both_part[r] for r in range(chips)])
    query_chunks = to_chips([query_slope] * chips)
    output_own = add(*swap_rows(output_share))
    out_share = dot(hidden, down_full).astype(bf16)
    pair_slope.came, both_part, output_own, out_share = tie(
        pair_slope.came, both_part, output_own, out_share
    )
    both_sums = lax.all_gather(jnp.stack(both_part), "seq", axis=1, tiled=True)
    kv_slope = turn_back(pair_slope.result().astype(bf16), pair_cosine, pair_sine)
    first_slope = query_side + dot(kv_slope, pair_weight[:, : 2 * kv_width], NT)
    input_gradient = middle_slope + norm_backward(
        first_slope * first_scale, first_normed, first_inverse
    )
    gain_shares = jnp.stack([jnp.sum(first_slope * first_normed, axis=0), second_gain_share])
    input_gradient, kv_slope, gain_shares, query_chunks = tie(
        input_gradient.astype(bf16), kv_slope, gain_shares.astype(bf16), query_chunks
    )
    kv_chunks = to_chips([kv_slope] * chips)
    gain_parts = to_chips(for_chips(gain_shares))
    query_share = dot(first_columns, jnp.concatenate(query_chunks), TN).astype(bf16)
    query_own = add(*swap_rows(query_share))
    query_own, kv_chunks, gain_parts, out_share, down_sum = tie(
        query_own, kv_chunks, gain_parts, out_share, down_sum
    )
    out_parts = to_chips(by_chip(out_share))
    kv_share = dot(first_columns, jnp.concatenate(kv_chunks), TN).astype(bf16)
    gain_two = swap_rows(add_all(gain_parts).T.astype(bf16))
    last = jnp.concatenate(
        [
            query_own,
            output_own,
            add(*swap_rows(kv_share)),
            jnp.pad(add(*gain_two), ((0, 0), (0, 126))),
        ],
        axis=1,
    )
    last, input_gradient, both_sums, down_sum = tie(last, input_gradient, both_sums, down_sum)
    lasts = [LineTree(last[half]) for half in halves(own_rows)[:1]]
    input_gradient = spread(input_gradient)
    gate_gradient, up_gradient = place_columns(both_sums, chip)
    lasts[0].moving, gate_gradient, last = tie(lasts[0].moving, gate_gradient, last)
    lasts[0].across()
    lasts.append(LineTree(last[halves(own_rows)[1]]))
    layer_output = (middle + add_all(out_parts)).astype(bf16)
    lasts[0].moving, lasts[1].moving, layer_output = tie(
        lasts[0].moving, lasts[1].moving, layer_output
    )
    lasts[0].outwards()
    lasts[1].across()
    layer_output = spread(layer_output)
    lasts[1].moving, input_gradient = tie(lasts[1].moving, input_gradient)
    lasts[1].outwards()
    down_gradient = down_sum.astype(f32)
    input_gradient = input_gradient.astype(f32)
    lasts[0].moving, lasts[1].moving, layer_output, down_gradient, input_gradient = tie(
        lasts[0].moving, lasts[1].moving, layer_output, down_gradient, input_gradient
    )

    last = jnp.concatenate([part.result() for part in lasts])
    query_gradient = last[:, :width]
    output_gradient = last[:, width : 2 * width]
    pairs = last[:, 2 * width :]
    gain_gradients = pairs[:, 2 * kv_width : 2 * kv_width + 2].T
    pairs = pairs[:, : 2 * kv_width].reshape(own_rows, KV_HEADS, 2, HEAD_DIM)
    return (
        layer_output,
        input_gradient,
        query_gradient,
        pairs[:, :, 0].reshape(own_rows, kv_width),
        pairs[:, :, 1].reshape(own_rows, kv_width),
        output_gradient,
        gate_gradient,
        up_gradient,
        down_gradient,
        gain_gradients[0],
        gain_gradients[1],
    )


def solution(mesh):
    tokens = P(("dp", "seq", "ctx"), None)
    rows = P(PLANE, None)
    return jax.shard_map(
        on_device,
        mesh=mesh,
        in_specs=(tokens, P(("dp", "seq", "ctx")), tokens) + (rows,) * 7 + (P(PLANE),) * 2,
        out_specs=(tokens,) * 2 + (rows,) * 7 + (P(PLANE),) * 2,
        check_vma=False,
    )
```
